512 devices in a mesh: gx: 8 (over x, core), gy: 8 (over z), gz: 8 (over y).
Axes of the slice: x: 4, y: 8, z: 8, core: 2. Of those that a mesh axis runs over, the one named last changes fastest.
Arguments:
- right_side: float32 [3, 64, 128, 1024], P(None, 'gx', 'gy', 'gz'), may hold values from -8 to 10
- iterate: float32 [3, 64, 128, 1024], P(None, 'gx', 'gy', 'gz'), may hold values from -4 to 4
- state: float32 [3, 64, 128, 1024], P(None, 'gx', 'gy', 'gz'), may hold values from -6 to 6
- classes: int32 [64, 128, 1024], P('gx', 'gy', 'gz'), may hold values from 0 to 15
- load_mask: int32 [64, 128, 1024], P('gx', 'gy', 'gz'), may hold values 0 or 1
- fixed_mask: int32 [64, 128, 1024], P('gx', 'gy', 'gz'), may hold values 0 or 1
Outputs:
- solution: float32 [3, 64, 128, 1024], P(None, 'gx', 'gy', 'gz')
- residual: float32 [3, 64, 128, 1024], P(None, 'gx', 'gy', 'gz')
- filtered: float32 [64, 128, 1024], P('gx', 'gy', 'gz')
The draws below stay inside these ranges and needn't reach their ends.
All inputs are finite; a program needn't handle non-finite values. No bound on the sum of `load_mask` or of `fixed_mask` on one device may be relied on, other than what follows from the above.
Results may differ from the reference program's by a relative error of at most 0.0003.
Values sent between devices are 32-bit elements; how exact they have to be, the bound alone decides.
No kernel may reach another device: no remote copies, remote signals or barrier semaphores. Data moves between devices by JAX's collectives and lax.ppermute only.
A program may use at most 128 MiB of HBM per device.

```python
import math
import jax
import jax.numpy as jnp
from jax import lax

LEVELS = 4
COARSE_SWEEPS = 4
CLASSES = 16
RADIUS = 3
NX = 64
NY = 128
NZ = 1024


def draw_right_side(key, part):
    key = jax.random.fold_in(key, 11)
    shape = (3, NX, NY, NZ)
    coord_x = (jnp.arange(NX, dtype=jnp.float32) + 0.5)[:, None, None] / NX
    coord_y = (jnp.arange(NY, dtype=jnp.float32) + 0.5)[None, :, None] / NY
    coord_z = (jnp.arange(NZ, dtype=jnp.float32) + 0.5)[None, None, :] / NZ
    signs = jnp.array([1.0, -0.7, 0.5], jnp.float32)[:, None, None, None]
    rough = jnp.clip(jax.random.normal(key, shape, jnp.float32), -4.0, 4.0)
    base = 1.0 + 0.3 * jnp.sin(math.pi * coord_x) * jnp.cos(2.0 * math.pi * coord_z) + 0.2 * coord_y
    return (signs * base[None] + rough).astype(jnp.float32)


def draw_classes(key, part):
    key = jax.random.fold_in(key, 23)
    block_key, cell_key = jax.random.split(key)
    blocks = jax.random.randint(block_key, (NX // 8, NY // 8, NZ // 8), 0, CLASSES, jnp.int32)
    blocks = jnp.repeat(jnp.repeat(jnp.repeat(blocks, 8, axis=0), 8, axis=1), 8, axis=2)
    offsets = jax.random.randint(cell_key, (NX, NY, NZ), -3, 4, jnp.int32)
    result = jnp.clip(blocks + offsets, 0, CLASSES - 1)
    result = result.at[0, 0, 0].set(0)
    result = result.at[0, 0, 1].set(CLASSES - 1)
    return result.astype(jnp.int32)


def set_ends(entries, rng, low, high):
    spot = [jax.random.randint(jax.random.fold_in(rng, axis), (), 0, length) for axis, length in enumerate(entries.shape)]
    longest = entries.shape.index(max(entries.shape))
    beside = spot[:longest] + [(spot[longest] + 1) % entries.shape[longest]] + spot[longest + 1:]
    return entries.at[tuple(spot)].set(low).at[tuple(beside)].set(high)


def steps_of(rng, shape, cuts, least, largest):
    factor_of, own = 1.0, jax.random.fold_in(rng, 6)
    for axis_at, blocks in cuts:
        steps = jnp.exp(jax.random.uniform(jax.random.fold_in(own, axis_at), (blocks,), jnp.float32, least / len(cuts), largest / len(cuts)))
        factor_of = factor_of * jnp.repeat(steps, shape[axis_at] // blocks).reshape([-1 if axis == axis_at else 1 for axis in range(len(shape))])
    return factor_of


def bell_draw(rng, extent, scale, limit, pieces=(), kind=jnp.bfloat16):
    gain = steps_of(rng, extent, pieces, -0.22, 0.18) if pieces else 1.0
    values = jax.random.normal(rng, extent, jnp.float32) * scale * gain
    return jnp.minimum(jnp.maximum(values, -limit), limit).astype(kind)


def setup_inputs(seed: int = 0) -> dict:
    arg_keys = jax.random.split(jax.random.key(seed), 7)
    return {
        "right_side": draw_right_side(jax.random.fold_in(arg_keys[6], 71), 0),
        "iterate": bell_draw(arg_keys[1], (3, NX, NY, NZ), 0.5, 4.0, ((1, 8), (2, 8), (3, 8)), jnp.float32),
        "state": bell_draw(arg_keys[2], (3, NX, NY, NZ), 1.0, 6.0, ((1, 8), (2, 8), (3, 8)), jnp.float32),
        "classes": draw_classes(jax.random.fold_in(arg_keys[6], 71), 0),
        "load_mask": set_ends((jax.random.randint(arg_keys[4], (NX, NY, NZ), 0, 2) < 1).astype(jnp.int32), jax.random.fold_in(arg_keys[4], 1), 0, 1),
        "fixed_mask": set_ends((jax.random.randint(arg_keys[5], (NX, NY, NZ), 0, 32) < 1).astype(jnp.int32), jax.random.fold_in(arg_keys[5], 1), 0, 1),
    }


rho_floor = 0.25
penalty = 4.0
sweep_first = 0.55
sweep_second = 1.05
coarse_weight = 0.6
couple = ((2.0, 1.0, 1.0), (1.0, 2.0, 1.0), (1.0, 1.0, 2.0))

def pad_cells(field, width):
    lead = field.ndim - 3
    return jnp.pad(field, [(0, 0)] * lead + [(width, width)] * 3)

def neighbour(padded, direction, step, width):
    lead = padded.ndim - 3
    starts = [0] * padded.ndim
    limits = list(padded.shape)
    for spatial in range(3):
        starts[lead + spatial] = width
        limits[lead + spatial] = padded.shape[lead + spatial] - width
    starts[lead + direction] = starts[lead + direction] + step
    limits[lead + direction] = limits[lead + direction] + step
    return lax.slice(padded, starts, limits)

def level_ops(energy, padded, pen, scale):
    faces = []
    for direction in range(3):
        pair = []
        for step in (-1, 1):
            near = neighbour(padded, direction, step, 1)
            harmonic = 2.0 * energy * near / (energy + near)
            pair.append(jnp.where(near > 0.0, harmonic, energy))
        faces.append(pair)
    rows = []
    for component in range(3):
        total = jnp.zeros_like(energy)
        for direction in range(3):
            total = total + couple[component][direction] * (faces[direction][0] + faces[direction][1])
        rows.append(scale * total + pen)
    return (faces, jnp.stack(rows), pen, scale)

def apply_padded(padded, field, ops):
    faces, diagonal, pen, scale = ops
    rows = []
    for component in range(3):
        total = jnp.zeros_like(pen)
        for direction in range(3):
            part = jnp.zeros_like(pen)
            for side, step in enumerate((-1, 1)):
                near = neighbour(padded[component], direction, step, 1)
                part = part + faces[direction][side] * (field[component] - near)
            total = total + couple[component][direction] * part
        rows.append(scale * total + pen * field[component])
    return jnp.stack(rows)

def restrict(field):
    shape = field.shape
    lead = tuple(shape[:-3])
    count = len(lead)
    grouped = field.reshape(lead + (shape[-3] // 2, 2, shape[-2] // 2, 2, shape[-1] // 2, 2))
    return grouped.sum(axis=(count + 1, count + 3, count + 5))

def prolong(field):
    shape = field.shape
    lead = tuple(shape[:-3])
    grouped = field[..., :, None, :, None, :, None]
    grouped = jnp.broadcast_to(grouped, lead + (shape[-3], 2, shape[-2], 2, shape[-1], 2))
    return grouped.reshape(lead + (shape[-3] * 2, shape[-2] * 2, shape[-1] * 2))

def apply_level(field, ops):
    return apply_padded(pad_cells(field, 1), field, ops)

def vcycle(levels, level, rhs):
    ops = levels[level]
    diagonal = ops[1]
    if level == LEVELS - 1:
        field = coarse_weight * rhs / diagonal
        for sweep in range(COARSE_SWEEPS - 1):
            field = field + coarse_weight * (rhs - apply_level(field, ops)) / diagonal
        return field
    field = sweep_first * rhs / diagonal
    field = field + sweep_second * (rhs - apply_level(field, ops)) / diagonal
    coarse = vcycle(levels, level + 1, restrict(rhs - apply_level(field, ops)))
    field = field + prolong(coarse)
    field = field + sweep_second * (rhs - apply_level(field, ops)) / diagonal
    field = field + sweep_first * (rhs - apply_level(field, ops)) / diagonal
    return field

def sensitivity(state_pad, iter_pad):
    state_mid = neighbour(state_pad, 0, 0, 1)
    iter_mid = neighbour(iter_pad, 0, 0, 1)
    energy = jnp.zeros_like(state_mid[0])
    for component in range(3):
        for direction in range(3):
            for step in (-1, 1):
                diff_state = state_mid[component] - neighbour(state_pad[component], direction, step, 1)
                diff_iter = iter_mid[component] - neighbour(iter_pad[component], direction, step, 1)
                energy = energy + 0.5 * couple[component][direction] * diff_state * diff_iter
    return energy

def filter_offsets():
    listing = []
    for a in range(-RADIUS, RADIUS + 1):
        for b in range(-RADIUS, RADIUS + 1):
            for c in range(-RADIUS, RADIUS + 1):
                weight = RADIUS - math.sqrt(a * a + b * b + c * c)
                if weight > 0.0:
                    listing.append((a, b, c, weight))
    return listing

def density_filter(term_pad, rho_pad, rho_own):
    shape = rho_own.shape
    weighted = jnp.zeros_like(rho_own)
    coverage = jnp.zeros_like(rho_own)
    for a, b, c, weight in filter_offsets():
        anchor = (RADIUS + a, RADIUS + b, RADIUS + c)
        ending = (anchor[0] + shape[0], anchor[1] + shape[1], anchor[2] + shape[2])
        weighted = weighted + weight * lax.slice(term_pad, anchor, ending)
        inside = jnp.where(lax.slice(rho_pad, anchor, ending) > 0.0, 1.0, 0.0).astype(rho_own.dtype)
        coverage = coverage + weight * inside
    return weighted / (rho_own * coverage)

def reference(right_side, iterate, state, classes, load_mask, fixed_mask):
    rho = rho_floor + (1.0 - rho_floor) * classes.astype(jnp.float32) / (CLASSES - 1)
    energy = rho * rho * rho
    pen = penalty * fixed_mask.astype(jnp.float32)
    levels = []
    for level in range(LEVELS):
        levels.append(level_ops(energy, pad_cells(energy, 1), pen, float(2 ** level)))
        if level + 1 < LEVELS:
            energy = restrict(energy) / 8.0
            pen = restrict(pen)
    load = right_side * load_mask.astype(jnp.float32)[None]
    start = load - apply_level(iterate, levels[0])
    precond = vcycle(levels, 0, start)
    image = apply_level(precond, levels[0])
    alpha = jnp.sum(start * precond) / jnp.sum(precond * image)
    solution = iterate + alpha * precond
    residual = start - alpha * image
    stored = sensitivity(pad_cells(state, 1), pad_cells(solution, 1))
    term = rho * (-3.0 * rho * rho * stored)
    filtered = density_filter(pad_cells(term, RADIUS), pad_cells(rho, RADIUS), rho)
    return (solution, residual, filtered)
```

```python
import functools
import math

import jax
import jax.numpy as jnp
from jax import lax
from jax.experimental import pallas as pl
from jax.experimental.pallas import tpu as pltpu
from jax.sharding import PartitionSpec as P

F32 = jnp.float32
FLOOR = 0.25
CLASSES = 16
PENALTY = 4.0
FIRST = 0.55
SECOND = 1.05
COARSE = 0.6
RADIUS = 3

BX, BY, BZ = 8, 16, 128
HALO = 7
SLABS = BX + 2 * HALO
ROWS = 2 * BY
LANES = 2 * BZ

PACKED = 8
ITERATE = ((0, 0, 7), (1, 7, 7), (2, 14, 7))
RHO = (3, 21, 7)
LOAD = ((4, 28, 6), (5, 34, 6), (6, 40, 6))
PEN = (7, 46, 6)
STATE = ((9, 52, 3), (10, 55, 3), (11, 58, 3))
HALF = BZ // 2

VMEM_LIMIT = 56 * 1024 * 1024


def iota(shape, dim):
    return lax.broadcasted_iota(jnp.int32, shape, dim)


def roll(x, shift, axis):
    return pltpu.roll(x, shift % x.shape[axis], axis)


def loop(lower, upper, step):
    def run(i, carry):
        step(i)
        return carry

    lax.fori_loop(lower, upper, run, 0)


def times(x, m):
    return jnp.dot(x, m, precision=lax.Precision.HIGHEST, preferred_element_type=F32)


def matrix(shape, rule):
    return jnp.where(rule(iota(shape, 0), iota(shape, 1)), 1.0, 0.0).astype(F32)


def face(a, b):
    total = a + b
    both = (a > 0.0) & (b > 0.0)
    return jnp.where(both, 2.0 * a * b / jnp.where(both, total, 1.0), total)


def launch(kernel, outs, scratch, *operands):
    specs = [pl.BlockSpec(memory_space=pltpu.SMEM)] + [pl.BlockSpec(memory_space=pltpu.VMEM)] * (len(operands) - 1)
    return pl.pallas_call(
        kernel,
        out_shape=[jax.ShapeDtypeStruct(shape, F32) for shape in outs],
        in_specs=specs,
        out_specs=[pl.BlockSpec(memory_space=pltpu.VMEM)] * len(outs),
        scratch_shapes=[pltpu.VMEM(shape, F32) for shape in scratch],
        compiler_params=pltpu.CompilerParams(vmem_limit_bytes=VMEM_LIMIT),
    )(*operands)


def shift_along(x, axis, step):
    devices = lax.axis_size(axis)
    return lax.ppermute(x, axis, [(i, (i + step) % devices) for i in range(devices)])


def prepare(pos, right, iterate, state, classes, load_mask, fixed_mask, main, to_upper, to_lower):
    lane = iota((BY, BZ), 1)

    def slab(x):
        rho = FLOOR + (1.0 - FLOOR) * classes[x].astype(F32) / (CLASSES - 1)
        mask = load_mask[x].astype(F32)
        values = {
            RHO: rho,
            PEN: PENALTY * fixed_mask[x].astype(F32),
        }
        for c in range(3):
            values[ITERATE[c]] = iterate[c, x]
            values[LOAD[c]] = right[c, x] * mask
            values[STATE[c]] = state[c, x]
        last = jnp.zeros((BY, BZ), F32)
        first = jnp.zeros((BY, BZ), F32)
        for (tile, offset, width), value in values.items():
            if tile < PACKED:
                main[tile, x] = value
            last = jnp.where((lane >= offset) & (lane < offset + width), roll(value, offset + width, 1), last)
            low = HALF + offset
            first = jnp.where((lane >= low) & (lane < low + width), roll(value, low, 1), first)
        to_upper[x] = last
        to_lower[x] = first

    loop(0, BX, slab)


def pack_rows(pos, main, state, from_lower, from_upper, packed, to_upper, to_lower):
    below = jnp.where(pos[2] > 0, 1.0, 0.0)
    above = jnp.where(pos[2] < pos[5] - 1, 1.0, 0.0)
    lane = iota((BY, BZ), 1)
    half = BY // 2

    def slab(x):
        joined = jnp.where(lane < HALF, from_lower[x] * below, from_upper[x] * above)
        packed[x] = joined
        for tile in range(12):
            value = joined if tile == PACKED else (main[tile, x] if tile < PACKED else state[tile - 9, x])
            to_upper[tile, x] = value[half:]
            to_lower[tile, x] = value[:half]

    loop(0, BX, slab)


def pack_slabs(pos, main, packed, state, from_lower, from_upper, own, to_upper, to_lower):
    below = jnp.where(pos[1] > 0, 1.0, 0.0)
    above = jnp.where(pos[1] < pos[4] - 1, 1.0, 0.0)

    def slab(x):
        for tile in range(12):
            value = packed[x] if tile == PACKED else (main[tile, x] if tile < PACKED else state[tile - 9, x])
            own[tile, x] = jnp.concatenate([value, from_upper[tile, x] * above, from_lower[tile, x] * below], 0)

    loop(0, BX, slab)
    for tile in range(9):
        for j in range(HALO):
            to_upper[tile * HALO + j] = own[tile, j + 1]
            to_lower[tile * HALO + j] = own[tile, j]
    for c in range(3):
        for j in range(3):
            to_upper[9 * HALO + 3 * c + j] = own[9 + c, BX - 3 + j]
            to_lower[9 * HALO + 3 * c + j] = own[9 + c, j]


def neighbours(field, c, s, kx, ky, kyp, kz, kzp):
    v = field[c, s]
    x = kx[s] * field[c, s - 1] + kx[s + 1] * field[c, s + 1]
    y = ky[s] * roll(v, 1, 0) + kyp[s] * roll(v, -1, 0)
    z = kz[s] * roll(v, 1, 1) + kzp[s] * roll(v, -1, 1)
    return x + y + z + (x, y, z)[c]


def coefficients(stiff, pen, s, scale, kx, ky, kyp, kz, kzp, inverse, diagonal):
    e = stiff[s]
    upper = scale * face(e, stiff[s + 1])
    kx[s + 1] = upper
    y = scale * face(e, roll(e, 1, 0))
    ky[s] = y
    yp = roll(y, -1, 0)
    kyp[s] = yp
    z = scale * face(e, roll(e, 1, 1))
    kz[s] = z
    zp = roll(z, -1, 1)
    kzp[s] = zp
    pairs = (kx[s] + upper, y + yp, z + zp)
    total = pairs[0] + pairs[1] + pairs[2] + pen[s]
    for c in range(3):
        value = total + pairs[c]
        diagonal[c, s] = value
        inverse[c, s] = jnp.where(e > 0.0, 1.0 / jnp.where(e > 0.0, value, 1.0), 0.0)


def descend(pos, own, lower, upper, coarse, v1, start, kx, ky, kyp, kz, kzp, inverse, shifted, weights, forward,
            stiff, load, pen, u, diagonal, v0, half_rows, rows):
    below = jnp.where(pos[0] > 0, 1.0, 0.0)
    above = jnp.where(pos[0] < pos[3] - 1, 1.0, 0.0)
    lane = iota((ROWS, BZ), 1)

    def spread(raw, packed, field, store):
        tile, offset, width = field
        store[0][store[1] + (slice(None), slice(0, BZ))] = raw(tile)
        tail = jnp.where(lane >= BZ - width, roll(packed, BZ - width - offset, 1), 0.0)
        tail = jnp.where(lane < width, roll(packed, -(HALF + offset), 1), tail)
        store[0][store[1] + (slice(None), slice(BZ, LANES))] = tail

    def expand(raw, s):
        packed = raw(PACKED)
        spread(raw, packed, RHO, (stiff, (s,)))
        spread(raw, packed, PEN, (pen, (s,)))
        for c in range(3):
            spread(raw, packed, ITERATE[c], (u, (c, s)))
            spread(raw, packed, LOAD[c], (load, (c, s)))

    def expand_state(raw, packed, s):
        for c in range(3):
            spread(raw, packed, STATE[c], (forward, (c, s)))

    loop(0, HALO, lambda s: expand(lambda t: lower[t * HALO + s] * below, s))
    loop(0, BX, lambda s: expand(lambda t: own[t, s], s + HALO))
    loop(0, HALO, lambda s: expand(lambda t: upper[t * HALO + s] * above, s + HALO + BX))
    shape = (ROWS, BZ)
    loop(0, 3, lambda s: expand_state(lambda t: lower[9 * HALO + 3 * (t - 9) + s] * below, lower[PACKED * HALO + s + HALO - 3] * below, s))
    loop(0, BX, lambda s: expand_state(lambda t: own[t, s], own[PACKED, s], s + 3))
    loop(0, 3, lambda s: expand_state(lambda t: upper[9 * HALO + 3 * (t - 9) + s] * above, upper[PACKED * HALO + s] * above, s + 3 + BX))

    def keep(s):
        weights[s] = stiff[s + HALO - 3]
        for c in range(3):
            shifted[c, s] = u[c, s + HALO - 3]

    loop(0, BX + 6, keep)

    def cube(s):
        rho = stiff[s]
        stiff[s] = rho * rho * rho

    loop(0, SLABS, cube)
    kx[1] = face(stiff[0], stiff[1])
    loop(1, SLABS - 1, lambda s: coefficients(stiff, pen, s, 1.0, kx, ky, kyp, kz, kzp, inverse, diagonal))
    faces = (kx, ky, kyp, kz, kzp)

    def begin(s):
        for c in range(3):
            f = load[c, s] - (diagonal[c, s] * u[c, s] - neighbours(u, c, s, *faces))
            start[c, s] = f
            v0[c, s] = FIRST * f * inverse[c, s]

    loop(1, SLABS - 1, begin)

    def sweep(s):
        for c in range(3):
            v1[c, s] = (1.0 - SECOND) * v0[c, s] + SECOND * inverse[c, s] * (start[c, s] + neighbours(v0, c, s, *faces))

    loop(2, SLABS - 2, sweep)

    def remainder(c, s):
        r = start[c, s] - diagonal[c, s] * v1[c, s] + neighbours(v1, c, s, *faces)
        return r[:BY, :BZ]

    def gather_rows(at, value):
        half_rows[...] = value
        n = BY // 2
        rows[pl.ds(pl.multiple_of(at * n, n), n), :] = half_rows[pl.ds(0, n, stride=2), :] + half_rows[pl.ds(1, n, stride=2), :]

    def pair(i):
        for c in range(3):
            gather_rows(c * 8 + i, remainder(c, 3 + 2 * i) + remainder(c, 4 + 2 * i))

    loop(0, 8, pair)

    def pair_up(i):
        s = 1 + 2 * i
        gather_rows(24 + i, (stiff[s] + stiff[s + 1])[:BY, :BZ] * 0.125)
        gather_rows(34 + i, (pen[s] + pen[s + 1])[:BY, :BZ])

    loop(0, 10, pair_up)
    halve = matrix((BZ, BZ), lambda l, k: (l >> 1) == (k & (HALF - 1)))
    coarse[...] = times(rows[...], halve).reshape(44, 8, BZ)


def level_one(pos, own, lower, upper, chunk, v1, f, kx, ky, kyp, kz, kzp, inverse,
              stiff, pen, diagonal, v0, half_rows, rows, wide):
    below = jnp.where(pos[0] > 0, 1.0, 0.0)
    above = jnp.where(pos[0] < pos[3] - 1, 1.0, 0.0)
    slabs, ys = 18, 24
    for field, at in ((stiff, 0), (pen, 1)):
        for j in range(7):
            field[j] = lower[18 + 7 * at + j] * below
            field[11 + j] = upper[18 + 7 * at + j] * above
        for j in range(4):
            field[7 + j] = own[24 + 10 * at + 3 + j]
    for c in range(3):
        f[c, 0] = jnp.zeros((ys, BZ), F32)
        f[c, 17] = jnp.zeros((ys, BZ), F32)
        for j in range(6):
            f[c, 1 + j] = lower[6 * c + j] * below
            f[c, 11 + j] = upper[6 * c + j] * above
        for j in range(4):
            f[c, 7 + j] = own[8 * c + 2 + j]
    kx[1] = 2.0 * face(stiff[0], stiff[1])
    loop(1, slabs - 1, lambda s: coefficients(stiff, pen, s, 2.0, kx, ky, kyp, kz, kzp, inverse, diagonal))
    faces = (kx, ky, kyp, kz, kzp)

    def begin(s):
        for c in range(3):
            v0[c, s] = FIRST * f[c, s] * inverse[c, s]

    loop(1, slabs - 1, begin)

    def sweep(s):
        for c in range(3):
            v1[c, s] = (1.0 - SECOND) * v0[c, s] + SECOND * inverse[c, s] * (f[c, s] + neighbours(v0, c, s, *faces))

    loop(2, slabs - 2, sweep)

    def gather_rows(at, value):
        half_rows[...] = value
        rows[pl.ds(at * 4, 4), :] = half_rows[pl.ds(0, 4, stride=2), :] + half_rows[pl.ds(1, 4, stride=2), :]

    for i in range(2):
        s = 7 + 2 * i
        for c in range(3):
            total = 0.0
            for at in (s, s + 1):
                total = total + (f[c, at] - diagonal[c, at] * v1[c, at] + neighbours(v1, c, at, *faces))[:8]
            gather_rows(2 * c + i, total)
        gather_rows(6 + i, (stiff[s] + stiff[s + 1])[:8] * 0.125)
        gather_rows(8 + i, (pen[s] + pen[s + 1])[:8])

    def rule(j, k):
        z = jnp.where(j < 96, j, j - BZ)
        return (z >> 1) == (k & 63) - 16

    wide[...] = times(rows[...], matrix((BZ, BZ), rule))
    lane = iota((4, BZ), 1)
    chunk[...] = jnp.zeros((24, BZ), F32)
    for field in range(5):
        chunk[4 * field:4 * field + 4] = jnp.where(lane < 64, wide[8 * field:8 * field + 4], wide[8 * field + 4:8 * field + 8])


def coarse_levels(pos, gathered, out, nx, ny, work):
    (e2, p2, f2, kxm, kxp, kym, kyp, kzm, kzp, iv, dg, va, vb, tall, rows3, e3, p3, f3, jx, jym, jyp, jz, jzp, iv3, wa, wb, rows2) = work
    ys = 4 * ny
    pairs = nx
    lane = iota((ys, BZ), 1)
    row = iota((ys, BZ), 0)
    even = lane < 64
    zero = jnp.zeros((ys, BZ), F32)
    for field in (e2, p2):
        field[0] = zero
        field[pairs + 1] = zero
    for c in range(3):
        for field in (va, vb):
            field[c, 0] = zero
            field[c, pairs + 1] = zero

    def collect(g):
        for field in range(5):
            for yy in range(ny):
                value = gathered[g * ny + yy, pl.ds(4 * field, 4), :]
                if field < 3:
                    f2[field, g + 1, pl.ds(4 * yy, 4), :] = value
                else:
                    (e2, p2)[field - 3][g + 1, pl.ds(4 * yy, 4), :] = value

    loop(0, pairs, collect)

    def x_neighbours(below, mid, above):
        swapped = roll(mid, 64, 1)
        return jnp.where(even, roll(below, 64, 1), swapped), jnp.where(even, swapped, roll(above, 64, 1))

    def coefs(s):
        e = e2[s]
        xm, xp = x_neighbours(e2[s - 1], e, e2[s + 1])
        ym = jnp.where(row == 0, 0.0, roll(e, 1, 0))
        yp = jnp.where(row == ys - 1, 0.0, roll(e, -1, 0))
        a, b = 4.0 * face(e, xm), 4.0 * face(e, xp)
        c0, d = 4.0 * face(e, ym), 4.0 * face(e, yp)
        z = 4.0 * face(e, roll(e, 1, 1))
        zp = roll(z, -1, 1)
        kxm[s] = a
        kxp[s] = b
        kym[s] = jnp.where(row == 0, 0.0, c0)
        kyp[s] = jnp.where(row == ys - 1, 0.0, d)
        kzm[s] = z
        kzp[s] = zp
        sums = (a + b, c0 + d, z + zp)
        total = sums[0] + sums[1] + sums[2] + p2[s]
        for c in range(3):
            value = total + sums[c]
            dg[c, s] = value
            iv[c, s] = jnp.where(e > 0.0, 1.0 / jnp.where(e > 0.0, value, 1.0), 0.0)
            va[c, s] = FIRST * f2[c, s] * iv[c, s]

    loop(1, pairs + 1, coefs)

    def around(v, c, s):
        mid = v[c, s]
        below, above = x_neighbours(v[c, s - 1], mid, v[c, s + 1])
        x = kxm[s] * below + kxp[s] * above
        y = kym[s] * roll(mid, 1, 0) + kyp[s] * roll(mid, -1, 0)
        z = kzm[s] * roll(mid, 1, 1) + kzp[s] * roll(mid, -1, 1)
        return x + y + z + (x, y, z)[c]

    def sweep(source, target, weight):
        def step(s):
            for c in range(3):
                target[c, s] = (1.0 - weight) * source[c, s] + weight * iv[c, s] * (f2[c, s] + around(source, c, s))

        loop(1, pairs + 1, step)

    sweep(va, vb, SECOND)
    n3 = ys // 2

    def gather_rows(at, value):
        tall[...] = value
        rows3[pl.ds(pl.multiple_of(at * n3, 8), n3), :] = tall[pl.ds(0, n3, stride=2), :] + tall[pl.ds(1, n3, stride=2), :]

    def reduce(s):
        for c in range(3):
            gather_rows(c * pairs + s - 1, f2[c, s] - dg[c, s] * vb[c, s] + around(vb, c, s))
        gather_rows(3 * pairs + s - 1, e2[s] * 0.125)
        gather_rows(4 * pairs + s - 1, p2[s])

    loop(1, pairs + 1, reduce)
    down = matrix((BZ, BZ), lambda l, k: ((l & 63) >> 1) == (k & 31))
    rows3[...] = times(rows3[...], down)
    row3 = iota((n3, BZ), 0)
    zero3 = jnp.zeros((n3, BZ), F32)

    def third(at):
        return rows3[pl.ds(pl.multiple_of(at * n3, 8), n3), :]

    e3[0] = zero3
    e3[pairs + 1] = zero3
    for c in range(3):
        for field in (wa, wb):
            field[c, 0] = zero3
            field[c, pairs + 1] = zero3

    def place(s):
        e3[s] = third(3 * pairs + s - 1)

    loop(1, pairs + 1, place)

    def coefs3(s):
        e = e3[s]
        a, b = 8.0 * face(e, e3[s - 1]), 8.0 * face(e, e3[s + 1])
        c0 = 8.0 * face(e, jnp.where(row3 == 0, 0.0, roll(e, 1, 0)))
        d = 8.0 * face(e, jnp.where(row3 == n3 - 1, 0.0, roll(e, -1, 0)))
        z = 8.0 * face(e, roll(e, 1, 1))
        zp = roll(z, -1, 1)
        jx[s] = a
        jx[s + 1] = b
        jym[s] = jnp.where(row3 == 0, 0.0, c0)
        jyp[s] = jnp.where(row3 == n3 - 1, 0.0, d)
        jz[s] = z
        jzp[s] = zp
        sums = (a + b, c0 + d, z + zp)
        total = sums[0] + sums[1] + sums[2] + third(4 * pairs + s - 1)
        for c in range(3):
            value = total + sums[c]
            iv3[c, s] = jnp.where(e > 0.0, 1.0 / jnp.where(e > 0.0, value, 1.0), 0.0)
            wa[c, s] = COARSE * third(c * pairs + s - 1) * iv3[c, s]

    loop(1, pairs + 1, coefs3)
    source, target = wa, wb
    for sweep_at in range(3):
        def step(s, source=source, target=target):
            for c in range(3):
                near = neighbours(source, c, s, jx, jym, jyp, jz, jzp)
                target[c, s] = (1.0 - COARSE) * source[c, s] + COARSE * iv3[c, s] * (third(c * pairs + s - 1) + near)

        loop(1, pairs + 1, step)
        source, target = target, source
    up = matrix((BZ, BZ), lambda k, l: k == ((l & 63) >> 1))
    for c in range(3):
        rows2[...] = times(source[c, 1:pairs + 1].reshape(pairs * n3, BZ), up)

        def add(s, c=c):
            value = rows2[pl.ds(pl.multiple_of((s - 1) * n3, 8), n3), :]
            tall[pl.ds(0, n3, stride=2), :] = value
            tall[pl.ds(1, n3, stride=2), :] = value
            vb[c, s] = vb[c, s] + jnp.where(iv[c, s] > 0.0, tall[...], 0.0)

        loop(1, pairs + 1, add)
    sweep(vb, va, SECOND)

    for c in range(3):
        for at in (0, 1, pairs + 2, pairs + 3):
            out[c, at] = zero

    def last(s):
        for c in range(3):
            out[c, s + 1] = (1.0 - FIRST) * va[c, s] + FIRST * iv[c, s] * (f2[c, s] + around(va, c, s))

    loop(1, pairs + 1, last)


def ascend(pos, gathered, v1, f1, kx1, ky1, kyp1, kz1, kzp1, inverse1, v, start, kx, ky, kyp, kz, kzp, inverse,
           precond, image, sums, e2out, window, rows24, va1, vb1, rows32, spread, va, vb, *work, nx, ny):
    coarse_levels(pos, gathered, e2out, nx, ny, work)
    gx, gy = pos[0], pos[1]
    ys = 4 * ny
    turn = lax.rem(ys - 4 * gy, ys)

    def rule(k, j):
        z = jnp.where((j & 127) < 96, j & 127, (j & 127) - BZ)
        return k == 64 * (j >> 7) + (z >> 1) + 16

    grow = matrix((BZ, LANES), rule)
    for c in range(3):
        for j in range(5):
            window[pl.ds((5 * c + j) * ys, ys), :] = times(pltpu.roll(e2out[c, gx + j], turn, 0), grow)
    for c in range(3):
        for s in range(2, 16):
            x2 = (s - 7) // 2
            j, part = (x2 + 4) // 2, (x2 + 4) % 2
            base = (5 * c + j) * ys
            cols = slice(128 * part, 128 * part + 128)
            if s % 2 == 1 or s == 2:
                low = window[base:base + 8, cols]
                high = window[base + ys - 4:base + ys, cols]
                for at in (0, 1):
                    rows24[pl.ds(at, 8, stride=2), :] = low
                    rows24[pl.ds(16 + at, 4, stride=2), :] = high
            va1[c, s] = v1[c, s] + jnp.where(inverse1[c, s] > 0.0, rows24[...], 0.0)
    faces1 = (kx1, ky1, kyp1, kz1, kzp1)

    def sweep1(source, target, weight, lower, upper):
        def step(s):
            for c in range(3):
                target[c, s] = (1.0 - weight) * source[c, s] + weight * inverse1[c, s] * (
                    f1[c, s] + neighbours(source, c, s, *faces1))

        loop(lower, upper, step)

    sweep1(va1, vb1, SECOND, 3, 15)
    sweep1(vb1, va1, FIRST, 4, 14)
    grow0 = matrix((BZ, LANES), lambda j, l: j == (l >> 1))
    for c in range(3):
        spread[...] = times(va1[c, 4:14].reshape(240, BZ), grow0)

        def widen(i, c=c):
            base = pl.multiple_of(24 * i, 8)
            for half in (0, 1):
                cols = slice(BZ * half, BZ * half + BZ)
                value = spread[pl.ds(base, 24), cols]
                for at in (0, 1):
                    rows32[pl.ds(at, 12, stride=2), :] = value[:12]
                    rows32[pl.ds(24 + at, 4, stride=2), :] = value[20:]
                for at in (0, 1):
                    s = 1 + 2 * i + at
                    va[c, s, :, cols] = v[c, s, :, cols] + rows32[...]

        loop(0, 10, widen)
    faces = (kx, ky, kyp, kz, kzp)

    def sweep_one(s):
        for c in range(3):
            vb[c, s] = (1.0 - SECOND) * va[c, s] + SECOND * inverse[c, s] * (start[c, s] + neighbours(va, c, s, *faces))

    loop(3, SLABS - 3, sweep_one)

    def sweep_two(s):
        for c in range(3):
            precond[c, s - 4] = (1.0 - FIRST) * vb[c, s] + FIRST * inverse[c, s] * (start[c, s] + neighbours(vb, c, s, *faces))

    loop(4, SLABS - 4, sweep_two)

    def inner(x, carry):
        one, two = carry
        s = x + HALO
        for c in range(3):
            p = precond[c, x + 3]
            near = kx[s] * precond[c, x + 2] + kx[s + 1] * precond[c, x + 4]
            y = ky[s] * roll(p, 1, 0) + kyp[s] * roll(p, -1, 0)
            z = kz[s] * roll(p, 1, 1) + kzp[s] * roll(p, -1, 1)
            total = (near + y + z + (near, y, z)[c])[:BY, :BZ]
            mid = p[:BY, :BZ]
            value = mid / inverse[c, s][:BY, :BZ] - total
            image[c, x] = value
            one = one + start[c, s][:BY, :BZ] * mid
            two = two + mid * value
        return one, two

    zero = jnp.zeros((BY, BZ), F32)
    one, two = lax.fori_loop(0, BX, inner, (zero, zero))
    lane = iota((8, BZ), 1)
    sums[...] = jnp.where(lane == 0, jnp.sum(one), jnp.where(lane == 1, jnp.sum(two), 0.0))


def distance_weight(square):
    return max(RADIUS - math.sqrt(square), 0.0)


def finish(pos, totals, precond, image, start, iterate, weights, state, solution, residual, filtered, whole, term, inside):
    total = jnp.sum(totals[...], axis=0, keepdims=True)
    lane = iota((1, BZ), 1)
    one = jnp.sum(jnp.where(lane == 0, total, 0.0), axis=1, keepdims=True)
    two = jnp.sum(jnp.where(lane == 1, total, 0.0), axis=1, keepdims=True)
    alpha = one / two

    def update(s):
        for c in range(3):
            whole[c, s] = iterate[c, s] + alpha * precond[c, s]

    loop(0, BX + 6, update)

    def emit(x):
        for c in range(3):
            solution[c, x] = whole[c, x + 3][:BY, :BZ]
            residual[c, x] = start[c, x + HALO][:BY, :BZ] - alpha * image[c, x]

    loop(0, BX, emit)

    def energy(i):
        s = i + 1
        total = jnp.zeros((ROWS, LANES), F32)
        for c in range(3):
            a, b = state[c, s], whole[c, s]
            along = [
                (a - state[c, s - 1]) * (b - whole[c, s - 1]) + (a - state[c, s + 1]) * (b - whole[c, s + 1])
            ]
            for axis in (0, 1):
                along.append(
                    (a - roll(a, 1, axis)) * (b - roll(b, 1, axis)) + (a - roll(a, -1, axis)) * (b - roll(b, -1, axis))
                )
            total = total + (along[0] + along[1] + along[2] + along[c])
        rho = weights[s]
        term[i] = rho * (-3.0 * rho * rho * (0.5 * total))
        inside[i] = jnp.where(rho > 0.0, 1.0, 0.0)

    loop(0, BX + 4, energy)

    def column(field, x):
        classes = {}
        for a in range(-2, 3):
            t = field[x + 2 + a]
            for b, value in ((0, t), (1, roll(t, 1, 0) + roll(t, -1, 0)), (2, roll(t, 2, 0) + roll(t, -2, 0))):
                q = a * a + b * b
                classes[q] = value if q not in classes else classes[q] + value
        parts = []
        for z in (0, 1, 2):
            part = None
            for q, value in classes.items():
                w = distance_weight(q + z * z)
                if w > 0.0:
                    part = w * value if part is None else part + w * value
            parts.append(part)
        result = parts[0] + roll(parts[1], 1, 1) + roll(parts[1], -1, 1) + roll(parts[2], 2, 1) + roll(parts[2], -2, 1)
        return result[:BY, :BZ]

    def smooth(x):
        rho = weights[x + 3][:BY, :BZ]
        filtered[x] = column(term, x) / (rho * column(inside, x))

    loop(0, BX, smooth)


def body(right_side, iterate, state, classes, load_mask, fixed_mask):
    nx, ny, nz = (lax.axis_size(axis) for axis in ("gx", "gy", "gz"))
    pos = jnp.stack([lax.axis_index("gx"), lax.axis_index("gy"), lax.axis_index("gz")]).astype(jnp.int32)
    pos = jnp.concatenate([pos, jnp.array([nx, ny, nz], jnp.int32)])
    inner = (BX, BY, BZ)
    main, last, first = launch(prepare, [(8,) + inner, inner, inner], [], pos, right_side, iterate, state, classes, load_mask, fixed_mask)
    from_lower, from_upper = shift_along(last, "gz", 1), shift_along(first, "gz", -1)
    edge = (12, BX, BY // 2, BZ)
    packed, to_upper, to_lower = launch(pack_rows, [inner, edge, edge], [], pos, main, state, from_lower, from_upper)
    from_lower, from_upper = shift_along(to_upper, "gy", 1), shift_along(to_lower, "gy", -1)
    sides = (9 * HALO + 9, ROWS, BZ)
    own, to_upper, to_lower = launch(
        pack_slabs, [(12, BX, ROWS, BZ), sides, sides], [], pos, main, packed, state, from_lower, from_upper)
    from_lower, from_upper = shift_along(to_upper, "gx", 1), shift_along(to_lower, "gx", -1)

    wide = (ROWS, LANES)
    one, three = (SLABS,) + wide, (3, SLABS) + wide
    near = (3, BX + 6) + wide
    coarse, v1, start, kx, ky, kyp, kz, kzp, inverse, shifted, weights, forward = launch(
        descend,
        [(44, 8, BZ), three, three, one, one, one, one, one, three, near, (BX + 6,) + wide, near],
        [one, three, one, three, three, three, (BY, BZ), (44 * 8, BZ)],
        pos, own, from_lower, from_upper)

    at_z = pos[2]
    at_y = pos[1]
    lower, upper = shift_along(coarse, "gz", 1), shift_along(coarse, "gz", -1)
    lane = iota(coarse.shape, 2)
    coarse = jnp.where(
        lane < 64, coarse, jnp.where(lane < 96, jnp.where(at_z < nz - 1, upper, 0.0), jnp.where(at_z > 0, lower, 0.0)))
    lower, upper = shift_along(coarse, "gy", 1), shift_along(coarse, "gy", -1)
    coarse = jnp.concatenate([coarse, jnp.where(at_y < ny - 1, upper, 0.0), jnp.where(at_y > 0, lower, 0.0)], 1)
    to_lower = jnp.concatenate([coarse[2:8], coarse[10:16], coarse[18:24], coarse[27:34], coarse[37:44]], 0)
    to_upper = jnp.concatenate([coarse[0:6], coarse[8:14], coarse[16:22], coarse[24:31], coarse[34:41]], 0)
    lower, upper = shift_along(to_upper, "gx", 1), shift_along(to_lower, "gx", -1)

    wide1 = (24, BZ)
    one1, three1 = (18,) + wide1, (3, 18) + wide1
    chunk, v1_1, f1, kx1, ky1, kyp1, kz1, kzp1, inverse1 = launch(
        level_one,
        [(24, BZ), three1, three1, one1, one1, one1, one1, one1, three1],
        [one1, one1, three1, three1, (8, BZ), (40, BZ), (40, BZ)],
        pos, coarse, lower, upper)
    gathered = lax.all_to_all(jnp.broadcast_to(chunk[None], (nx * ny, 24, BZ)), ("gx", "gy"), 0, 0, tiled=True)

    wide2, wide3 = (4 * ny, BZ), (2 * ny, BZ)
    one2, three2 = (nx + 2,) + wide2, (3, nx + 2) + wide2
    one3, three3 = (nx + 2,) + wide3, (3, nx + 2) + wide3
    work = [one2, one2, three2] + [one2] * 6 + [three2] * 4 + [wide2, (5 * nx * 2 * ny, BZ)]
    work += [one3, one3, three3] + [one3] * 5 + [three3] * 3 + [(nx * 2 * ny, BZ)]
    precond, image, sums = launch(
        functools.partial(ascend, nx=nx, ny=ny),
        [near, (3,) + inner, (8, BZ)],
        [(3, nx + 4) + wide2, (15 * 4 * ny, LANES), wide1, three1, three1, (ROWS, BZ), (240, LANES), three, three] + work,
        pos, gathered, v1_1, f1, kx1, ky1, kyp1, kz1, kzp1, inverse1, v1, start, kx, ky, kyp, kz, kzp, inverse)

    total = lax.all_to_all(jnp.broadcast_to(sums[:1], (nx * ny, BZ)), ("gx", "gy"), 0, 0, tiled=True)
    total = jnp.sum(total, axis=0, keepdims=True)
    total = lax.all_to_all(jnp.broadcast_to(total, (nz, BZ)), "gz", 0, 0, tiled=True)
    return tuple(launch(
        finish,
        [(3,) + inner, (3,) + inner, inner],
        [near, (BX + 4,) + wide, (BX + 4,) + wide],
        pos, total, precond, image, start, shifted, weights, forward))


def solution(mesh):
    field, cells = P(None, "gx", "gy", "gz"), P("gx", "gy", "gz")
    return jax.shard_map(
        body,
        mesh=mesh,
        in_specs=(field, field, field, cells, cells, cells),
        out_specs=(field, field, cells),
        check_vma=False,
    )
```

```python
import functools
import math

import jax
import jax.numpy as jnp
from jax import lax
from jax.experimental import pallas as pl
from jax.experimental.pallas import tpu as pltpu
from jax.sharding import PartitionSpec as P

F32 = jnp.float32
FLOOR = 0.25
CLASSES = 16
PENALTY = 4.0
FIRST = 0.55
SECOND = 1.05
COARSE = 0.6
RADIUS = 3

BX, BY, BZ = 8, 16, 128
HALO = 7
SLABS = BX + 2 * HALO
ROWS = 2 * BY
LANES = 2 * BZ

PACKED = 8
ITERATE = ((0, 0, 7), (1, 7, 7), (2, 14, 7))
RHO = (3, 21, 7)
LOAD = ((4, 28, 6), (5, 34, 6), (6, 40, 6))
PEN = (7, 46, 6)
STATE = ((9, 52, 3), (10, 55, 3), (11, 58, 3))
HALF = BZ // 2

VMEM_LIMIT = 34 * 1024 * 1024


def iota(shape, dim):
    return lax.broadcasted_iota(jnp.int32, shape, dim)


def roll(x, shift, axis):
    return pltpu.roll(x, shift % x.shape[axis], axis)


def loop(lower, upper, step, unroll=4):
    def run(i, carry):
        step(i)
        return carry

    lax.fori_loop(lower, upper, run, 0, unroll=unroll)


def times(x, m):
    m = m.astype(jnp.bfloat16)
    high = x.astype(jnp.bfloat16)
    low = (x - high.astype(F32)).astype(jnp.bfloat16)
    return jnp.dot(high, m, preferred_element_type=F32) + jnp.dot(low, m, preferred_element_type=F32)


def matrix(shape, rule):
    return jnp.where(rule(iota(shape, 0), iota(shape, 1)), 1.0, 0.0).astype(F32)


def face(a, b):
    total = a + b
    both = (a > 0.0) & (b > 0.0)
    return jnp.where(both, 2.0 * a * b / jnp.where(both, total, 1.0), total)


def launch(kernel, outs, scratch, *operands):
    specs = [pl.BlockSpec(memory_space=pltpu.SMEM)] + [pl.BlockSpec(memory_space=pltpu.VMEM)] * (len(operands) - 1)
    return pl.pallas_call(
        kernel,
        out_shape=[jax.ShapeDtypeStruct(shape, F32) for shape in outs],
        in_specs=specs,
        out_specs=[pl.BlockSpec(memory_space=pltpu.VMEM)] * len(outs),
        scratch_shapes=[pltpu.VMEM(shape, F32) for shape in scratch],
        compiler_params=pltpu.CompilerParams(vmem_limit_bytes=VMEM_LIMIT),
    )(*operands)


def shift_along(x, axis, step):
    devices = lax.axis_size(axis)
    return lax.ppermute(x, axis, [(i, (i + step) % devices) for i in range(devices)])


def prepare(pos, right, iterate, state, classes, load_mask, fixed_mask, main, to_upper, to_lower):
    lane = iota((BY, BZ), 1)

    def slab(x):
        rho = FLOOR + (1.0 - FLOOR) * classes[x].astype(F32) / (CLASSES - 1)
        mask = load_mask[x].astype(F32)
        values = {
            RHO: rho,
            PEN: PENALTY * fixed_mask[x].astype(F32),
        }
        for c in range(3):
            values[ITERATE[c]] = iterate[c, x]
            values[LOAD[c]] = right[c, x] * mask
            values[STATE[c]] = state[c, x]
        last = jnp.zeros((BY, BZ), F32)
        first = jnp.zeros((BY, BZ), F32)
        for (tile, offset, width), value in values.items():
            if tile < PACKED:
                main[tile, x] = value
            last = jnp.where((lane >= offset) & (lane < offset + width), roll(value, offset + width, 1), last)
            low = HALF + offset
            first = jnp.where((lane >= low) & (lane < low + width), roll(value, low, 1), first)
        to_upper[x] = last
        to_lower[x] = first

    loop(0, BX, slab)


def pack_rows(pos, main, state, from_lower, from_upper, packed, to_upper, to_lower):
    below = jnp.where(pos[2] > 0, 1.0, 0.0)
    above = jnp.where(pos[2] < pos[5] - 1, 1.0, 0.0)
    lane = iota((BY, BZ), 1)
    half = BY // 2

    def slab(x):
        joined = jnp.where(lane < HALF, from_lower[x] * below, from_upper[x] * above)
        packed[x] = joined
        for tile in range(12):
            value = joined if tile == PACKED else (main[tile, x] if tile < PACKED else state[tile - 9, x])
            to_upper[tile, x] = value[half:]
            to_lower[tile, x] = value[:half]

    loop(0, BX, slab)


def pack_slabs(pos, main, packed, state, from_lower, from_upper, own, to_upper, to_lower):
    below = jnp.where(pos[1] > 0, 1.0, 0.0)
    above = jnp.where(pos[1] < pos[4] - 1, 1.0, 0.0)

    def slab(x):
        for tile in range(12):
            value = packed[x] if tile == PACKED else (main[tile, x] if tile < PACKED else state[tile - 9, x])
            own[tile, x] = jnp.concatenate([value, from_upper[tile, x] * above, from_lower[tile, x] * below], 0)

    loop(0, BX, slab)
    for tile in range(9):
        for j in range(HALO):
            to_upper[tile * HALO + j] = own[tile, j + 1]
            to_lower[tile * HALO + j] = own[tile, j]
    for c in range(3):
        for j in range(3):
            to_upper[9 * HALO + 3 * c + j] = own[9 + c, BX - 3 + j]
            to_lower[9 * HALO + 3 * c + j] = own[9 + c, j]


def neighbours(field, c, s, kx, ky, kyp, kz, kzp):
    v = field[c, s]
    x = kx[s] * field[c, s - 1] + kx[s + 1] * field[c, s + 1]
    y = ky[s] * roll(v, 1, 0) + kyp[s] * roll(v, -1, 0)
    z = kz[s] * roll(v, 1, 1) + kzp[s] * roll(v, -1, 1)
    return x + y + z + (x, y, z)[c]


def coefficients(stiff, pen, s, scale, kx, ky, kyp, kz, kzp, inverse, diagonal):
    e = stiff[s]
    upper = scale * face(e, stiff[s + 1])
    kx[s + 1] = upper
    y = scale * face(e, roll(e, 1, 0))
    ky[s] = y
    yp = roll(y, -1, 0)
    kyp[s] = yp
    z = scale * face(e, roll(e, 1, 1))
    kz[s] = z
    zp = roll(z, -1, 1)
    kzp[s] = zp
    pairs = (kx[s] + upper, y + yp, z + zp)
    total = pairs[0] + pairs[1] + pairs[2] + pen[s]
    for c in range(3):
        value = total + pairs[c]
        diagonal[c, s] = value
        inverse[c, s] = jnp.where(e > 0.0, 1.0 / jnp.where(e > 0.0, value, 1.0), 0.0)


def descend(pos, own, lower, upper, coarse, v1, start, kx, ky, kyp, kz, kzp, inverse, shifted, weights, forward,
            stiff, load, pen, u, diagonal, v0, half_rows, rows):
    below = jnp.where(pos[0] > 0, 1.0, 0.0)
    above = jnp.where(pos[0] < pos[3] - 1, 1.0, 0.0)
    lane = iota((ROWS, BZ), 1)

    def spread(raw, packed, field, store):
        tile, offset, width = field
        store[0][store[1] + (slice(None), slice(0, BZ))] = raw(tile)
        tail = jnp.where(lane >= BZ - width, roll(packed, BZ - width - offset, 1), 0.0)
        tail = jnp.where(lane < width, roll(packed, -(HALF + offset), 1), tail)
        store[0][store[1] + (slice(None), slice(BZ, LANES))] = tail

    def expand(raw, s):
        packed = raw(PACKED)
        spread(raw, packed, RHO, (stiff, (s,)))
        spread(raw, packed, PEN, (pen, (s,)))
        for c in range(3):
            spread(raw, packed, ITERATE[c], (u, (c, s)))
            spread(raw, packed, LOAD[c], (load, (c, s)))

    def expand_state(raw, packed, s):
        for c in range(3):
            spread(raw, packed, STATE[c], (forward, (c, s)))

    loop(0, HALO, lambda s: expand(lambda t: lower[t * HALO + s] * below, s))
    loop(0, BX, lambda s: expand(lambda t: own[t, s], s + HALO))
    loop(0, HALO, lambda s: expand(lambda t: upper[t * HALO + s] * above, s + HALO + BX))
    shape = (ROWS, BZ)
    loop(0, 3, lambda s: expand_state(lambda t: lower[9 * HALO + 3 * (t - 9) + s] * below, lower[PACKED * HALO + s + HALO - 3] * below, s))
    loop(0, BX, lambda s: expand_state(lambda t: own[t, s], own[PACKED, s], s + 3))
    loop(0, 3, lambda s: expand_state(lambda t: upper[9 * HALO + 3 * (t - 9) + s] * above, upper[PACKED * HALO + s] * above, s + 3 + BX))

    def keep(s):
        weights[s] = stiff[s + HALO - 3]
        for c in range(3):
            shifted[c, s] = u[c, s + HALO - 3]

    loop(0, BX + 6, keep)

    def cube(s):
        rho = stiff[s]
        stiff[s] = rho * rho * rho

    loop(0, SLABS, cube)
    kx[1] = face(stiff[0], stiff[1])
    loop(1, SLABS - 1, lambda s: coefficients(stiff, pen, s, 1.0, kx, ky, kyp, kz, kzp, inverse, diagonal))
    faces = (kx, ky, kyp, kz, kzp)

    def begin(s):
        for c in range(3):
            f = load[c, s] - (diagonal[c, s] * u[c, s] - neighbours(u, c, s, *faces))
            start[c, s] = f
            v0[c, s] = FIRST * f * inverse[c, s]

    loop(1, SLABS - 1, begin)

    def sweep(s):
        for c in range(3):
            v1[c, s] = (1.0 - SECOND) * v0[c, s] + SECOND * inverse[c, s] * (start[c, s] + neighbours(v0, c, s, *faces))

    loop(2, SLABS - 2, sweep)

    def remainder(c, s):
        r = start[c, s] - diagonal[c, s] * v1[c, s] + neighbours(v1, c, s, *faces)
        return r[:BY, :BZ]

    def gather_rows(at, value):
        half_rows[...] = value
        n = BY // 2
        rows[pl.ds(pl.multiple_of(at * n, n), n), :] = half_rows[pl.ds(0, n, stride=2), :] + half_rows[pl.ds(1, n, stride=2), :]

    def pair(i):
        for c in range(3):
            gather_rows(c * 8 + i, remainder(c, 3 + 2 * i) + remainder(c, 4 + 2 * i))

    loop(0, 8, pair)

    def pair_up(i):
        s = 1 + 2 * i
        gather_rows(24 + i, (stiff[s] + stiff[s + 1])[:BY, :BZ] * 0.125)
        gather_rows(34 + i, (pen[s] + pen[s + 1])[:BY, :BZ])

    loop(0, 10, pair_up)
    halve = matrix((BZ, BZ), lambda l, k: (l >> 1) == (k & (HALF - 1)))
    coarse[...] = times(rows[...], halve).reshape(44, 8, BZ)


def level_one(pos, own, lower, upper, chunk, v1, f, kx, ky, kyp, kz, kzp, inverse,
              stiff, pen, diagonal, v0, half_rows, rows, wide):
    below = jnp.where(pos[0] > 0, 1.0, 0.0)
    above = jnp.where(pos[0] < pos[3] - 1, 1.0, 0.0)
    slabs, ys = 18, 24
    for field, at in ((stiff, 0), (pen, 1)):
        for j in range(7):
            field[j] = lower[18 + 7 * at + j] * below
            field[11 + j] = upper[18 + 7 * at + j] * above
        for j in range(4):
            field[7 + j] = own[24 + 10 * at + 3 + j]
    for c in range(3):
        f[c, 0] = jnp.zeros((ys, BZ), F32)
        f[c, 17] = jnp.zeros((ys, BZ), F32)
        for j in range(6):
            f[c, 1 + j] = lower[6 * c + j] * below
            f[c, 11 + j] = upper[6 * c + j] * above
        for j in range(4):
            f[c, 7 + j] = own[8 * c + 2 + j]
    kx[1] = 2.0 * face(stiff[0], stiff[1])
    loop(1, slabs - 1, lambda s: coefficients(stiff, pen, s, 2.0, kx, ky, kyp, kz, kzp, inverse, diagonal))
    faces = (kx, ky, kyp, kz, kzp)

    def begin(s):
        for c in range(3):
            v0[c, s] = FIRST * f[c, s] * inverse[c, s]

    loop(1, slabs - 1, begin)

    def sweep(s):
        for c in range(3):
            v1[c, s] = (1.0 - SECOND) * v0[c, s] + SECOND * inverse[c, s] * (f[c, s] + neighbours(v0, c, s, *faces))

    loop(2, slabs - 2, sweep)

    def gather_rows(at, value):
        half_rows[...] = value
        rows[pl.ds(at * 4, 4), :] = half_rows[pl.ds(0, 4, stride=2), :] + half_rows[pl.ds(1, 4, stride=2), :]

    for i in range(2):
        s = 7 + 2 * i
        for c in range(3):
            total = 0.0
            for at in (s, s + 1):
                total = total + (f[c, at] - diagonal[c, at] * v1[c, at] + neighbours(v1, c, at, *faces))[:8]
            gather_rows(2 * c + i, total)
        gather_rows(6 + i, (stiff[s] + stiff[s + 1])[:8] * 0.125)
        gather_rows(8 + i, (pen[s] + pen[s + 1])[:8])

    def rule(j, k):
        z = jnp.where(j < 96, j, j - BZ)
        return (z >> 1) == (k & 63) - 16

    wide[...] = times(rows[...], matrix((BZ, BZ), rule))
    lane = iota((4, BZ), 1)
    chunk[...] = jnp.zeros((24, BZ), F32)
    for field in range(5):
        chunk[4 * field:4 * field + 4] = jnp.where(lane < 64, wide[8 * field:8 * field + 4], wide[8 * field + 4:8 * field + 8])


def coarse_levels(pos, gathered, out, nx, ny, work):
    (e2, p2, f2, kxm, kxp, kym, kyp, kzm, kzp, iv, dg, va, vb, tall, rows3, e3, p3, f3, jx, jym, jyp, jz, jzp, iv3, wa, wb, rows2) = work
    ys = 4 * ny
    pairs = nx
    lane = iota((ys, BZ), 1)
    row = iota((ys, BZ), 0)
    even = lane < 64
    zero = jnp.zeros((ys, BZ), F32)
    for field in (e2, p2):
        field[0] = zero
        field[pairs + 1] = zero
    for c in range(3):
        for field in (va, vb):
            field[c, 0] = zero
            field[c, pairs + 1] = zero

    def collect(g):
        for field in range(5):
            for yy in range(ny):
                value = gathered[g * ny + yy, pl.ds(4 * field, 4), :]
                if field < 3:
                    f2[field, g + 1, pl.ds(4 * yy, 4), :] = value
                else:
                    (e2, p2)[field - 3][g + 1, pl.ds(4 * yy, 4), :] = value

    loop(0, pairs, collect)

    def x_neighbours(below, mid, above):
        swapped = roll(mid, 64, 1)
        return jnp.where(even, roll(below, 64, 1), swapped), jnp.where(even, swapped, roll(above, 64, 1))

    def coefs(s):
        e = e2[s]
        xm, xp = x_neighbours(e2[s - 1], e, e2[s + 1])
        ym = jnp.where(row == 0, 0.0, roll(e, 1, 0))
        yp = jnp.where(row == ys - 1, 0.0, roll(e, -1, 0))
        a, b = 4.0 * face(e, xm), 4.0 * face(e, xp)
        c0, d = 4.0 * face(e, ym), 4.0 * face(e, yp)
        z = 4.0 * face(e, roll(e, 1, 1))
        zp = roll(z, -1, 1)
        kxm[s] = a
        kxp[s] = b
        kym[s] = jnp.where(row == 0, 0.0, c0)
        kyp[s] = jnp.where(row == ys - 1, 0.0, d)
        kzm[s] = z
        kzp[s] = zp
        sums = (a + b, c0 + d, z + zp)
        total = sums[0] + sums[1] + sums[2] + p2[s]
        for c in range(3):
            value = total + sums[c]
            dg[c, s] = value
            iv[c, s] = jnp.where(e > 0.0, 1.0 / jnp.where(e > 0.0, value, 1.0), 0.0)
            va[c, s] = FIRST * f2[c, s] * iv[c, s]

    loop(1, pairs + 1, coefs)

    def around(v, c, s):
        mid = v[c, s]
        below, above = x_neighbours(v[c, s - 1], mid, v[c, s + 1])
        x = kxm[s] * below + kxp[s] * above
        y = kym[s] * roll(mid, 1, 0) + kyp[s] * roll(mid, -1, 0)
        z = kzm[s] * roll(mid, 1, 1) + kzp[s] * roll(mid, -1, 1)
        return x + y + z + (x, y, z)[c]

    def sweep(source, target, weight):
        def step(s):
            for c in range(3):
                target[c, s] = (1.0 - weight) * source[c, s] + weight * iv[c, s] * (f2[c, s] + around(source, c, s))

        loop(1, pairs + 1, step)

    sweep(va, vb, SECOND)
    n3 = ys // 2

    def gather_rows(at, value):
        tall[...] = value
        rows3[pl.ds(pl.multiple_of(at * n3, 8), n3), :] = tall[pl.ds(0, n3, stride=2), :] + tall[pl.ds(1, n3, stride=2), :]

    def reduce(s):
        for c in range(3):
            gather_rows(c * pairs + s - 1, f2[c, s] - dg[c, s] * vb[c, s] + around(vb, c, s))
        gather_rows(3 * pairs + s - 1, e2[s] * 0.125)
        gather_rows(4 * pairs + s - 1, p2[s])

    loop(1, pairs + 1, reduce)
    down = matrix((BZ, BZ), lambda l, k: ((l & 63) >> 1) == (k & 31))
    rows3[...] = times(rows3[...], down)
    row3 = iota((n3, BZ), 0)
    zero3 = jnp.zeros((n3, BZ), F32)

    def third(at):
        return rows3[pl.ds(pl.multiple_of(at * n3, 8), n3), :]

    e3[0] = zero3
    e3[pairs + 1] = zero3
    for c in range(3):
        for field in (wa, wb):
            field[c, 0] = zero3
            field[c, pairs + 1] = zero3

    def place(s):
        e3[s] = third(3 * pairs + s - 1)

    loop(1, pairs + 1, place)

    def coefs3(s):
        e = e3[s]
        a, b = 8.0 * face(e, e3[s - 1]), 8.0 * face(e, e3[s + 1])
        c0 = 8.0 * face(e, jnp.where(row3 == 0, 0.0, roll(e, 1, 0)))
        d = 8.0 * face(e, jnp.where(row3 == n3 - 1, 0.0, roll(e, -1, 0)))
        z = 8.0 * face(e, roll(e, 1, 1))
        zp = roll(z, -1, 1)
        jx[s] = a
        jx[s + 1] = b
        jym[s] = jnp.where(row3 == 0, 0.0, c0)
        jyp[s] = jnp.where(row3 == n3 - 1, 0.0, d)
        jz[s] = z
        jzp[s] = zp
        sums = (a + b, c0 + d, z + zp)
        total = sums[0] + sums[1] + sums[2] + third(4 * pairs + s - 1)
        for c in range(3):
            value = total + sums[c]
            iv3[c, s] = jnp.where(e > 0.0, 1.0 / jnp.where(e > 0.0, value, 1.0), 0.0)
            wa[c, s] = COARSE * third(c * pairs + s - 1) * iv3[c, s]

    loop(1, pairs + 1, coefs3)
    source, target = wa, wb
    for sweep_at in range(3):
        def step(s, source=source, target=target):
            for c in range(3):
                near = neighbours(source, c, s, jx, jym, jyp, jz, jzp)
                target[c, s] = (1.0 - COARSE) * source[c, s] + COARSE * iv3[c, s] * (third(c * pairs + s - 1) + near)

        loop(1, pairs + 1, step)
        source, target = target, source
    up = matrix((BZ, BZ), lambda k, l: k == ((l & 63) >> 1))
    for c in range(3):
        rows2[...] = times(source[c, 1:pairs + 1].reshape(pairs * n3, BZ), up)

        def add(s, c=c):
            value = rows2[pl.ds(pl.multiple_of((s - 1) * n3, 8), n3), :]
            tall[pl.ds(0, n3, stride=2), :] = value
            tall[pl.ds(1, n3, stride=2), :] = value
            vb[c, s] = vb[c, s] + jnp.where(iv[c, s] > 0.0, tall[...], 0.0)

        loop(1, pairs + 1, add)
    sweep(vb, va, SECOND)

    for c in range(3):
        for at in (0, 1, pairs + 2, pairs + 3):
            out[c, at] = zero

    def last(s):
        for c in range(3):
            out[c, s + 1] = (1.0 - FIRST) * va[c, s] + FIRST * iv[c, s] * (f2[c, s] + around(va, c, s))

    loop(1, pairs + 1, last)


def ascend(pos, gathered, v1, f1, kx1, ky1, kyp1, kz1, kzp1, inverse1, v, start, kx, ky, kyp, kz, kzp, inverse,
           precond, image, sums, e2out, window, rows24, va1, vb1, rows32, spread, va, vb, *work, nx, ny):
    coarse_levels(pos, gathered, e2out, nx, ny, work)
    gx, gy = pos[0], pos[1]
    ys = 4 * ny
    turn = lax.rem(ys - 4 * gy, ys)

    def rule(k, j):
        z = jnp.where((j & 127) < 96, j & 127, (j & 127) - BZ)
        return k == 64 * (j >> 7) + (z >> 1) + 16

    grow = matrix((BZ, LANES), rule)
    for c in range(3):
        for j in range(5):
            window[pl.ds((5 * c + j) * ys, ys), :] = times(pltpu.roll(e2out[c, gx + j], turn, 0), grow)
    for c in range(3):
        for s in range(2, 16):
            x2 = (s - 7) // 2
            j, part = (x2 + 4) // 2, (x2 + 4) % 2
            base = (5 * c + j) * ys
            cols = slice(128 * part, 128 * part + 128)
            if s % 2 == 1 or s == 2:
                low = window[base:base + 8, cols]
                high = window[base + ys - 4:base + ys, cols]
                for at in (0, 1):
                    rows24[pl.ds(at, 8, stride=2), :] = low
                    rows24[pl.ds(16 + at, 4, stride=2), :] = high
            va1[c, s] = v1[c, s] + jnp.where(inverse1[c, s] > 0.0, rows24[...], 0.0)
    faces1 = (kx1, ky1, kyp1, kz1, kzp1)

    def sweep1(source, target, weight, lower, upper):
        def step(s):
            for c in range(3):
                target[c, s] = (1.0 - weight) * source[c, s] + weight * inverse1[c, s] * (
                    f1[c, s] + neighbours(source, c, s, *faces1))

        loop(lower, upper, step)

    sweep1(va1, vb1, SECOND, 3, 15)
    sweep1(vb1, va1, FIRST, 4, 14)
    grow0 = matrix((BZ, LANES), lambda j, l: j == (l >> 1))
    for c in range(3):
        spread[...] = times(va1[c, 4:14].reshape(240, BZ), grow0)

        def widen(i, c=c):
            base = pl.multiple_of(24 * i, 8)
            for half in (0, 1):
                cols = slice(BZ * half, BZ * half + BZ)
                value = spread[pl.ds(base, 24), cols]
                for at in (0, 1):
                    rows32[pl.ds(at, 12, stride=2), :] = value[:12]
                    rows32[pl.ds(24 + at, 4, stride=2), :] = value[20:]
                for at in (0, 1):
                    s = 1 + 2 * i + at
                    va[c, s, :, cols] = v[c, s, :, cols] + rows32[...]

        loop(0, 10, widen)
    faces = (kx, ky, kyp, kz, kzp)

    def sweep_one(s):
        for c in range(3):
            vb[c, s] = (1.0 - SECOND) * va[c, s] + SECOND * inverse[c, s] * (start[c, s] + neighbours(va, c, s, *faces))

    loop(3, SLABS - 3, sweep_one)

    def sweep_two(s):
        for c in range(3):
            precond[c, s - 4] = (1.0 - FIRST) * vb[c, s] + FIRST * inverse[c, s] * (start[c, s] + neighbours(vb, c, s, *faces))

    loop(4, SLABS - 4, sweep_two)

    def inner(x, carry):
        one, two = carry
        s = x + HALO
        for c in range(3):
            p = precond[c, x + 3]
            near = kx[s] * precond[c, x + 2] + kx[s + 1] * precond[c, x + 4]
            y = ky[s] * roll(p, 1, 0) + kyp[s] * roll(p, -1, 0)
            z = kz[s] * roll(p, 1, 1) + kzp[s] * roll(p, -1, 1)
            total = (near + y + z + (near, y, z)[c])[:BY, :BZ]
            mid = p[:BY, :BZ]
            value = mid / inverse[c, s][:BY, :BZ] - total
            image[c, x] = value
            one = one + start[c, s][:BY, :BZ] * mid
            two = two + mid * value
        return one, two

    zero = jnp.zeros((BY, BZ), F32)
    one, two = lax.fori_loop(0, BX, inner, (zero, zero))
    lane = iota((8, BZ), 1)
    sums[...] = jnp.where(lane == 0, jnp.sum(one), jnp.where(lane == 1, jnp.sum(two), 0.0))


def distance_weight(square):
    return max(RADIUS - math.sqrt(square), 0.0)


def finish(pos, totals, precond, image, start, iterate, weights, state, solution, residual, filtered, whole, term, inside):
    total = jnp.sum(totals[...], axis=0, keepdims=True)
    lane = iota((1, BZ), 1)
    one = jnp.sum(jnp.where(lane == 0, total, 0.0), axis=1, keepdims=True)
    two = jnp.sum(jnp.where(lane == 1, total, 0.0), axis=1, keepdims=True)
    alpha = one / two

    def update(s):
        for c in range(3):
            whole[c, s] = iterate[c, s] + alpha * precond[c, s]

    loop(0, BX + 6, update)

    def emit(x):
        for c in range(3):
            solution[c, x] = whole[c, x + 3][:BY, :BZ]
            residual[c, x] = start[c, x + HALO][:BY, :BZ] - alpha * image[c, x]

    loop(0, BX, emit)

    def energy(i):
        s = i + 1
        total = jnp.zeros((ROWS, LANES), F32)
        for c in range(3):
            a, b = state[c, s], whole[c, s]
            along = [
                (a - state[c, s - 1]) * (b - whole[c, s - 1]) + (a - state[c, s + 1]) * (b - whole[c, s + 1])
            ]
            for axis in (0, 1):
                along.append(
                    (a - roll(a, 1, axis)) * (b - roll(b, 1, axis)) + (a - roll(a, -1, axis)) * (b - roll(b, -1, axis))
                )
            total = total + (along[0] + along[1] + along[2] + along[c])
        rho = weights[s]
        term[i] = rho * (-3.0 * rho * rho * (0.5 * total))
        inside[i] = jnp.where(rho > 0.0, 1.0, 0.0)

    loop(0, BX + 4, energy)

    def column(field, x):
        classes = {}
        for a in range(-2, 3):
            t = field[x + 2 + a]
            for b, value in ((0, t), (1, roll(t, 1, 0) + roll(t, -1, 0)), (2, roll(t, 2, 0) + roll(t, -2, 0))):
                q = a * a + b * b
                classes[q] = value if q not in classes else classes[q] + value
        parts = []
        for z in (0, 1, 2):
            part = None
            for q, value in classes.items():
                w = distance_weight(q + z * z)
                if w > 0.0:
                    part = w * value if part is None else part + w * value
            parts.append(part)
        result = parts[0] + roll(parts[1], 1, 1) + roll(parts[1], -1, 1) + roll(parts[2], 2, 1) + roll(parts[2], -2, 1)
        return result[:BY, :BZ]

    def smooth(x):
        rho = weights[x + 3][:BY, :BZ]
        filtered[x] = column(term, x) / (rho * column(inside, x))

    loop(0, BX, smooth)


def body(right_side, iterate, state, classes, load_mask, fixed_mask):
    nx, ny, nz = (lax.axis_size(axis) for axis in ("gx", "gy", "gz"))
    pos = jnp.stack([lax.axis_index("gx"), lax.axis_index("gy"), lax.axis_index("gz")]).astype(jnp.int32)
    pos = jnp.concatenate([pos, jnp.array([nx, ny, nz], jnp.int32)])
    inner = (BX, BY, BZ)
    main, last, first = launch(prepare, [(8,) + inner, inner, inner], [], pos, right_side, iterate, state, classes, load_mask, fixed_mask)
    from_lower, from_upper = shift_along(last, "gz", 1), shift_along(first, "gz", -1)
    edge = (12, BX, BY // 2, BZ)
    packed, to_upper, to_lower = launch(pack_rows, [inner, edge, edge], [], pos, main, state, from_lower, from_upper)
    from_lower, from_upper = shift_along(to_upper, "gy", 1), shift_along(to_lower, "gy", -1)
    sides = (9 * HALO + 9, ROWS, BZ)
    own, to_upper, to_lower = launch(
        pack_slabs, [(12, BX, ROWS, BZ), sides, sides], [], pos, main, packed, state, from_lower, from_upper)
    from_lower, from_upper = shift_along(to_upper, "gx", 1), shift_along(to_lower, "gx", -1)

    wide = (ROWS, LANES)
    one, three = (SLABS,) + wide, (3, SLABS) + wide
    near = (3, BX + 6) + wide
    coarse, v1, start, kx, ky, kyp, kz, kzp, inverse, shifted, weights, forward = launch(
        descend,
        [(44, 8, BZ), three, three, one, one, one, one, one, three, near, (BX + 6,) + wide, near],
        [one, three, one, three, three, three, (BY, BZ), (44 * 8, BZ)],
        pos, own, from_lower, from_upper)

    at_z = pos[2]
    at_y = pos[1]
    lower, upper = shift_along(coarse, "gz", 1), shift_along(coarse, "gz", -1)
    lane = iota(coarse.shape, 2)
    coarse = jnp.where(
        lane < 64, coarse, jnp.where(lane < 96, jnp.where(at_z < nz - 1, upper, 0.0), jnp.where(at_z > 0, lower, 0.0)))
    lower, upper = shift_along(coarse, "gy", 1), shift_along(coarse, "gy", -1)
    coarse = jnp.concatenate([coarse, jnp.where(at_y < ny - 1, upper, 0.0), jnp.where(at_y > 0, lower, 0.0)], 1)
    to_lower = jnp.concatenate([coarse[2:8], coarse[10:16], coarse[18:24], coarse[27:34], coarse[37:44]], 0)
    to_upper = jnp.concatenate([coarse[0:6], coarse[8:14], coarse[16:22], coarse[24:31], coarse[34:41]], 0)
    lower, upper = shift_along(to_upper, "gx", 1), shift_along(to_lower, "gx", -1)

    wide1 = (24, BZ)
    one1, three1 = (18,) + wide1, (3, 18) + wide1
    chunk, v1_1, f1, kx1, ky1, kyp1, kz1, kzp1, inverse1 = launch(
        level_one,
        [(24, BZ), three1, three1, one1, one1, one1, one1, one1, three1],
        [one1, one1, three1, three1, (8, BZ), (40, BZ), (40, BZ)],
        pos, coarse, lower, upper)
    gathered = lax.all_to_all(jnp.broadcast_to(chunk[None], (nx * ny, 24, BZ)), ("gx", "gy"), 0, 0, tiled=True)

    wide2, wide3 = (4 * ny, BZ), (2 * ny, BZ)
    one2, three2 = (nx + 2,) + wide2, (3, nx + 2) + wide2
    one3, three3 = (nx + 2,) + wide3, (3, nx + 2) + wide3
    work = [one2, one2, three2] + [one2] * 6 + [three2] * 4 + [wide2, (5 * nx * 2 * ny, BZ)]
    work += [one3, one3, three3] + [one3] * 5 + [three3] * 3 + [(nx * 2 * ny, BZ)]
    precond, image, sums = launch(
        functools.partial(ascend, nx=nx, ny=ny),
        [near, (3,) + inner, (8, BZ)],
        [(3, nx + 4) + wide2, (15 * 4 * ny, LANES), wide1, three1, three1, (ROWS, BZ), (240, LANES), three, three] + work,
        pos, gathered, v1_1, f1, kx1, ky1, kyp1, kz1, kzp1, inverse1, v1, start, kx, ky, kyp, kz, kzp, inverse)

    total = lax.all_to_all(jnp.broadcast_to(sums[:1], (nx * ny, BZ)), ("gx", "gy"), 0, 0, tiled=True)
    total = jnp.sum(total, axis=0, keepdims=True)
    total = lax.all_to_all(jnp.broadcast_to(total, (nz, BZ)), "gz", 0, 0, tiled=True)
    return tuple(launch(
        finish,
        [(3,) + inner, (3,) + inner, inner],
        [near, (BX + 4,) + wide, (BX + 4,) + wide],
        pos, total, precond, image, start, shifted, weights, forward))


def solution(mesh):
    field, cells = P(None, "gx", "gy", "gz"), P("gx", "gy", "gz")
    return jax.shard_map(
        body,
        mesh=mesh,
        in_specs=(field, field, field, cells, cells, cells),
        out_specs=(field, field, cells),
        check_vma=False,
    )
```

```python
import functools
import math

import jax
import jax.numpy as jnp
from jax import lax
from jax.experimental import pallas as pl
from jax.experimental.pallas import tpu as pltpu
from jax.sharding import PartitionSpec as P

F32 = jnp.float32
FLOOR = 0.25
CLASSES = 16
PENALTY = 4.0
FIRST = 0.55
SECOND = 1.05
COARSE = 0.6
RADIUS = 3

BX, BY, BZ = 8, 16, 128
HALO = 7
SLABS = BX + 2 * HALO
ROWS = 2 * BY
LANES = 2 * BZ

PACKED = 8
ITERATE = ((0, 0, 7), (1, 7, 7), (2, 14, 7))
RHO = (3, 21, 7)
LOAD = ((4, 28, 6), (5, 34, 6), (6, 40, 6))
PEN = (7, 46, 6)
STATE = ((9, 52, 3), (10, 55, 3), (11, 58, 3))
FIELDS = ITERATE + (RHO,) + LOAD + (PEN,) + STATE
HALF = BZ // 2

MIB = 1024 * 1024


def iota(shape, dim):
    return lax.broadcasted_iota(jnp.int32, shape, dim)


def roll(x, shift, axis):
    return pltpu.roll(x, shift % x.shape[axis], axis)


def loop(lower, upper, step, unroll=4):
    def run(i, carry):
        step(i)
        return carry

    lax.fori_loop(lower, upper, run, 0, unroll=unroll)


def times(x, m):
    m = m.astype(jnp.bfloat16)
    high = x.astype(jnp.bfloat16)
    low = (x - high.astype(F32)).astype(jnp.bfloat16)
    return jnp.dot(high, m, preferred_element_type=F32) + jnp.dot(low, m, preferred_element_type=F32)


def matrix(shape, rule):
    return jnp.where(rule(iota(shape, 0), iota(shape, 1)), 1.0, 0.0).astype(F32)


def face(a, b):
    total = a + b
    both = (a > 0.0) & (b > 0.0)
    return jnp.where(both, 2.0 * a * b / jnp.where(both, total, 1.0), total)


def launch(limit, kernel, outs, scratch, operands, far_outs=(), far=(), copies=0, cost=None):
    near_spec, far_spec = pl.BlockSpec(memory_space=pltpu.VMEM), pl.BlockSpec(memory_space=pltpu.HBM)
    specs = [pl.BlockSpec(memory_space=pltpu.SMEM)] + [near_spec] * (len(operands) - 1) + [far_spec] * len(far)
    return pl.pallas_call(
        kernel,
        out_shape=[jax.ShapeDtypeStruct(shape, F32) for shape in outs] + [pltpu.HBM(shape, F32) for shape in far_outs],
        in_specs=specs,
        out_specs=[near_spec] * len(outs) + [far_spec] * len(far_outs),
        scratch_shapes=[pltpu.VMEM(shape, F32) for shape in scratch] + ([pltpu.SemaphoreType.DMA((copies,))] if copies else []),
        compiler_params=pltpu.CompilerParams(vmem_limit_bytes=limit * MIB),
        cost_estimate=cost,
    )(*operands, *[pltpu.with_memory_space_constraint(x, pltpu.HBM) for x in far])


def shift_along(x, axis, step):
    devices = lax.axis_size(axis)
    return lax.ppermute(x, axis, [(i, (i + step) % devices) for i in range(devices)])


def prepare(pos, right_far, iterate_far, state_far, classes_far, load_far, fixed_far, main, to_upper, to_lower, right, copied):
    def rest(classes, load_mask, fixed_mask):
        moves = [
            pltpu.make_async_copy(source, target, copied.at[i])
            for i, (source, target) in enumerate((
                (classes_far, classes), (load_far, load_mask), (fixed_far, fixed_mask), (right_far, right),
                (iterate_far, main.at[0:3]), (state_far, main.at[8:11])))
        ]
        for move in moves:
            move.start()
        for move in moves:
            move.wait()
        lane = iota((BY, BZ), 1)

        def slab(x):
            mask = load_mask[x].astype(F32)
            main[3, x] = FLOOR + (1.0 - FLOOR) * classes[x].astype(F32) / (CLASSES - 1)
            main[7, x] = PENALTY * fixed_mask[x].astype(F32)
            for c in range(3):
                main[4 + c, x] = right[c, x] * mask
            last = jnp.zeros((BY, BZ), F32)
            first = jnp.zeros((BY, BZ), F32)
            for tile, offset, width in FIELDS:
                value = main[tile if tile < PACKED else tile - 1, x]
                last = jnp.where((lane >= offset) & (lane < offset + width), roll(value, offset + width, 1), last)
                low = HALF + offset
                first = jnp.where((lane >= low) & (lane < low + width), roll(value, low, 1), first)
            to_upper[x] = last
            to_lower[x] = first

        loop(0, BX, slab)

    cells = pltpu.VMEM((BX, BY, BZ), jnp.int32)
    pl.run_scoped(rest, cells, cells, cells)


def pack_rows(pos, main, from_lower, from_upper, packed, to_upper, to_lower):
    below = jnp.where(pos[2] > 0, 1.0, 0.0)
    above = jnp.where(pos[2] < pos[5] - 1, 1.0, 0.0)
    lane = iota((BY, BZ), 1)
    half = BY // 2

    def slab(x):
        joined = jnp.where(lane < HALF, from_lower[x] * below, from_upper[x] * above)
        packed[x] = joined
        for tile in range(12):
            value = joined if tile == PACKED else main[tile if tile < PACKED else tile - 1, x]
            to_upper[tile, x] = value[half:]
            to_lower[tile, x] = value[:half]

    loop(0, BX, slab)


def pack_slabs(pos, main, packed, from_lower, from_upper, own, to_upper, to_lower):
    below = jnp.where(pos[1] > 0, 1.0, 0.0)
    above = jnp.where(pos[1] < pos[4] - 1, 1.0, 0.0)

    def slab(x):
        for tile in range(12):
            value = packed[x] if tile == PACKED else main[tile if tile < PACKED else tile - 1, x]
            own[tile, x] = jnp.concatenate([value, from_upper[tile, x] * above, from_lower[tile, x] * below], 0)

    loop(0, BX, slab)
    for tile in range(9):
        for j in range(HALO):
            to_upper[tile * HALO + j] = own[tile, j + 1]
            to_lower[tile * HALO + j] = own[tile, j]
    for c in range(3):
        for j in range(3):
            to_upper[9 * HALO + 3 * c + j] = own[9 + c, BX - 3 + j]
            to_lower[9 * HALO + 3 * c + j] = own[9 + c, j]


def neighbours(field, c, s, kx, ky, kyp, kz, kzp, at=None):
    at = s if at is None else at
    v = field[c, s]
    x = kx[at] * field[c, s - 1] + kx[at + 1] * field[c, s + 1]
    y = ky[at] * roll(v, 1, 0) + kyp[at] * roll(v, -1, 0)
    z = kz[at] * roll(v, 1, 1) + kzp[at] * roll(v, -1, 1)
    return x + y + z + (x, y, z)[c]


def coefficients(stiff, pen, s, scale, kx, ky, kyp, kz, kzp, inverse, diagonal):
    e = stiff[s]
    upper = scale * face(e, stiff[s + 1])
    kx[s + 1] = upper
    y = scale * face(e, roll(e, 1, 0))
    ky[s] = y
    yp = roll(y, -1, 0)
    kyp[s] = yp
    z = scale * face(e, roll(e, 1, 1))
    kz[s] = z
    zp = roll(z, -1, 1)
    kzp[s] = zp
    pairs = (kx[s] + upper, y + yp, z + zp)
    total = pairs[0] + pairs[1] + pairs[2] + pen[s]
    for c in range(3):
        value = total + pairs[c]
        diagonal[c, s] = value
        inverse[c, s] = jnp.where(e > 0.0, 1.0 / jnp.where(e > 0.0, value, 1.0), 0.0)


def descend(pos, own, lower, upper, coarse, low_lanes, high_lanes, *rest):
    far, rest = rest[:11], rest[11:]
    (v1, start, kx, ky, kyp, kz, kzp, inverse, u, weights, forward, stiff, load, pen, diagonal, v0, half_rows, rows, copied) = rest
    moves = []

    def send(*pairs):
        for source, target in pairs:
            move = pltpu.make_async_copy(source, far[target], copied.at[target])
            move.start()
            moves.append(move)

    below = jnp.where(pos[0] > 0, 1.0, 0.0)
    above = jnp.where(pos[0] < pos[3] - 1, 1.0, 0.0)
    lane = iota((ROWS, BZ), 1)

    def spread(raw, packed, field, store):
        tile, offset, width = field
        store[0][store[1] + (slice(None), slice(0, BZ))] = raw(tile)
        tail = jnp.where(lane >= BZ - width, roll(packed, BZ - width - offset, 1), 0.0)
        tail = jnp.where(lane < width, roll(packed, -(HALF + offset), 1), tail)
        store[0][store[1] + (slice(None), slice(BZ, LANES))] = tail

    def expand(raw, s):
        packed = raw(PACKED)
        spread(raw, packed, RHO, (weights, (s,)))
        spread(raw, packed, PEN, (pen, (s,)))
        for c in range(3):
            spread(raw, packed, ITERATE[c], (u, (c, s)))
            spread(raw, packed, LOAD[c], (load, (c, s)))

    def expand_state(raw, packed, s):
        for c in range(3):
            spread(raw, packed, STATE[c], (forward, (c, s)))

    loop(0, HALO, lambda s: expand(lambda t: lower[t * HALO + s] * below, s))
    loop(0, BX, lambda s: expand(lambda t: own[t, s], s + HALO))
    loop(0, HALO, lambda s: expand(lambda t: upper[t * HALO + s] * above, s + HALO + BX))
    loop(0, 3, lambda s: expand_state(lambda t: lower[9 * HALO + 3 * (t - 9) + s] * below, lower[PACKED * HALO + s + HALO - 3] * below, s))
    loop(0, BX, lambda s: expand_state(lambda t: own[t, s], own[PACKED, s], s + 3))
    loop(0, 3, lambda s: expand_state(lambda t: upper[9 * HALO + 3 * (t - 9) + s] * above, upper[PACKED * HALO + s] * above, s + 3 + BX))

    send((u.at[:, 4:18], 8), (weights.at[4:18], 9), (forward, 10))

    def cube(s):
        rho = weights[s]
        stiff[s] = rho * rho * rho

    loop(0, SLABS, cube)
    kx[1] = face(stiff[0], stiff[1])
    loop(1, SLABS - 1, lambda s: coefficients(stiff, pen, s, 1.0, kx, ky, kyp, kz, kzp, inverse, diagonal))
    faces = (kx, ky, kyp, kz, kzp)
    send((kx.at[3:20], 2), (ky.at[3:19], 3), (kyp.at[3:19], 4), (kz.at[3:19], 5), (kzp.at[3:19], 6), (inverse.at[:, 3:19], 7))

    def begin(s):
        for c in range(3):
            f = load[c, s] - (diagonal[c, s] * u[c, s] - neighbours(u, c, s, *faces))
            start[c, s] = f
            v0[c, s] = FIRST * f * inverse[c, s]

    loop(1, SLABS - 1, begin)
    send((start.at[:, 3:19], 1))

    def sweep(s):
        for c in range(3):
            v1[c, s] = (1.0 - SECOND) * v0[c, s] + SECOND * inverse[c, s] * (start[c, s] + neighbours(v0, c, s, *faces))

    loop(2, SLABS - 2, sweep)
    send((v1.at[:, 2:20], 0))

    def remainder(c, s):
        r = start[c, s] - diagonal[c, s] * v1[c, s] + neighbours(v1, c, s, *faces)
        return r[:, :BZ]

    def gather_rows(at, value):
        half_rows[...] = value
        n = ROWS // 2
        rows[pl.ds(pl.multiple_of(at * n, n), n), :] = half_rows[pl.ds(0, n, stride=2), :] + half_rows[pl.ds(1, n, stride=2), :]

    def pair(i):
        for c in range(3):
            gather_rows(c * 8 + i, remainder(c, 3 + 2 * i) + remainder(c, 4 + 2 * i))

    loop(0, 8, pair)

    def pair_up(i):
        s = 1 + 2 * i
        gather_rows(24 + i, (stiff[s] + stiff[s + 1])[:, :BZ] * 0.125)
        gather_rows(34 + i, (pen[s] + pen[s + 1])[:, :BZ])

    loop(0, 10, pair_up)
    halve = matrix((BZ, BZ), lambda l, k: (l >> 1) == (k & (HALF - 1)))
    coarse[...] = times(rows[...], halve).reshape(44, 16, BZ)
    quarter = iota((8, BZ), 1) >> 5

    def pack(g):
        for h in range(2):
            low = jnp.zeros((8, BZ), F32)
            high = jnp.zeros((8, BZ), F32)
            for q in range(4):
                value = coarse[4 * g + q, 8 * h:8 * h + 8]
                turned = roll(value, 32, 1)
                one, two = (value, turned) if q % 2 == 0 else (turned, value)
                low = jnp.where(quarter == q, one, low)
                high = jnp.where(quarter == q, two, high)
            low_lanes[2 * g + h] = low
            high_lanes[2 * g + h] = high

    loop(0, 11, pack)
    for move in moves:
        move.wait()


def join_lanes(pos, coarse, from_lower, from_upper, out, center):
    below = jnp.where(pos[2] > 0, 1.0, 0.0)
    above = jnp.where(pos[2] < pos[5] - 1, 1.0, 0.0)
    lane = iota((8, BZ), 1)

    def unpack(g):
        for h in range(2):
            low, high = from_lower[2 * g + h] * below, from_upper[2 * g + h] * above
            for q in range(4):
                halo = jnp.where(lane < 96, roll(high, 64 - 32 * q, 1), roll(low, 96 - 32 * q, 1))
                value = jnp.where(lane < 64, coarse[4 * g + q, 8 * h:8 * h + 8], halo)
                out[4 * g + q, 8 * h:8 * h + 8] = value
                if h == 0:
                    center[4 * g + q] = value

    loop(0, 11, unpack)


def join_rows(pos, coarse, from_lower, from_upper, out, to_upper, to_lower):
    below = jnp.where(pos[1] > 0, 1.0, 0.0)
    above = jnp.where(pos[1] < pos[4] - 1, 1.0, 0.0)

    def join(i):
        out[i] = jnp.concatenate([coarse[i], from_upper[i] * above, from_lower[i] * below], 0)

    loop(0, 44, join)
    at = 0
    for base, count in ((0, 6), (8, 6), (16, 6), (24, 7), (34, 7)):
        shift = 2 if count == 6 else 3
        for j in range(count):
            to_upper[at] = out[base + j]
            to_lower[at] = out[base + shift + j]
            at += 1


def smooth_down(slabs, f, v0, v1, inverse, faces):
    def begin(s):
        for c in range(3):
            v0[c, s] = FIRST * f[c, s] * inverse[c, s]

    loop(1, slabs - 1, begin)

    def sweep(s):
        for c in range(3):
            v1[c, s] = (1.0 - SECOND) * v0[c, s] + SECOND * inverse[c, s] * (f[c, s] + neighbours(v0, c, s, *faces))

    loop(2, slabs - 2, sweep)


def level_one(pos, own, chunk, kx, ky, kyp, kz, kzp, inverse, diagonal, f, v0, v1, half_rows, rows, wide):
    stiff, pen = own.at[24:34], own.at[34:44]
    slabs = 10
    for c in range(3):
        for i in range(8):
            f[c, 1 + i] = own[8 * c + i]
    kx[1] = 2.0 * face(stiff[0], stiff[1])
    loop(1, slabs - 1, lambda s: coefficients(stiff, pen, s, 2.0, kx, ky, kyp, kz, kzp, inverse, diagonal))
    faces = (kx, ky, kyp, kz, kzp)
    smooth_down(slabs, f, v0, v1, inverse, faces)

    def gather_rows(at, value):
        half_rows[...] = value
        rows[pl.ds(at * 4, 4), :] = half_rows[pl.ds(0, 4, stride=2), :] + half_rows[pl.ds(1, 4, stride=2), :]

    for i in range(2):
        s = 3 + 2 * i
        for c in range(3):
            total = 0.0
            for at in (s, s + 1):
                total = total + (f[c, at] - diagonal[c, at] * v1[c, at] + neighbours(v1, c, at, *faces))[:8]
            gather_rows(2 * c + i, total)
        gather_rows(6 + i, (stiff[s] + stiff[s + 1])[:8] * 0.125)
        gather_rows(8 + i, (pen[s] + pen[s + 1])[:8])

    def rule(j, k):
        z = jnp.where(j < 96, j, j - BZ)
        return (z >> 1) == (k & 63) - 16

    wide[...] = times(rows[...], matrix((BZ, BZ), rule))
    lane = iota((4, BZ), 1)
    chunk[...] = jnp.zeros((24, BZ), F32)
    for field in range(5):
        chunk[4 * field:4 * field + 4] = jnp.where(lane < 64, wide[8 * field:8 * field + 4], wide[8 * field + 4:8 * field + 8])


def level_one_again(pos, own, lower, upper, v1, f, kx, ky, kyp, kz, kzp, inverse, stiff, pen, diagonal, v0):
    below = jnp.where(pos[0] > 0, 1.0, 0.0)
    above = jnp.where(pos[0] < pos[3] - 1, 1.0, 0.0)
    slabs = 18
    for field, at in ((stiff, 0), (pen, 1)):
        for j in range(7):
            field[j] = lower[18 + 7 * at + j] * below
            field[11 + j] = upper[18 + 7 * at + j] * above
        for j in range(4):
            field[7 + j] = own[24 + 10 * at + 3 + j]
    for c in range(3):
        for j in range(6):
            f[c, 1 + j] = lower[6 * c + j] * below
            f[c, 11 + j] = upper[6 * c + j] * above
        for j in range(4):
            f[c, 7 + j] = own[8 * c + 2 + j]
    kx[1] = 2.0 * face(stiff[0], stiff[1])
    loop(1, slabs - 1, lambda s: coefficients(stiff, pen, s, 2.0, kx, ky, kyp, kz, kzp, inverse, diagonal))
    smooth_down(slabs, f, v0, v1, inverse, (kx, ky, kyp, kz, kzp))


def coarse_levels(pos, gathered, out, nx, ny, work):
    (e2, p2, f2, kxm, kxp, kym, kyp, kzm, kzp, iv, dg, va, vb, tall, rows3, e3, p3, f3, jx, jym, jyp, jz, jzp, iv3, wa, wb, rows2) = work
    ys = 4 * ny
    pairs = nx
    lane = iota((ys, BZ), 1)
    row = iota((ys, BZ), 0)
    even = lane < 64
    zero = jnp.zeros((ys, BZ), F32)
    for field in (e2, p2):
        field[0] = zero
        field[pairs + 1] = zero
    for c in range(3):
        for field in (va, vb):
            field[c, 0] = zero
            field[c, pairs + 1] = zero

    def collect(g):
        for field in range(5):
            for yy in range(ny):
                value = gathered[g * ny + yy, pl.ds(4 * field, 4), :]
                if field < 3:
                    f2[field, g + 1, pl.ds(4 * yy, 4), :] = value
                else:
                    (e2, p2)[field - 3][g + 1, pl.ds(4 * yy, 4), :] = value

    loop(0, pairs, collect)

    def x_neighbours(below, mid, above):
        swapped = roll(mid, 64, 1)
        return jnp.where(even, roll(below, 64, 1), swapped), jnp.where(even, swapped, roll(above, 64, 1))

    def coefs(s):
        e = e2[s]
        xm, xp = x_neighbours(e2[s - 1], e, e2[s + 1])
        ym = jnp.where(row == 0, 0.0, roll(e, 1, 0))
        yp = jnp.where(row == ys - 1, 0.0, roll(e, -1, 0))
        a, b = 4.0 * face(e, xm), 4.0 * face(e, xp)
        c0, d = 4.0 * face(e, ym), 4.0 * face(e, yp)
        z = 4.0 * face(e, roll(e, 1, 1))
        zp = roll(z, -1, 1)
        kxm[s] = a
        kxp[s] = b
        kym[s] = jnp.where(row == 0, 0.0, c0)
        kyp[s] = jnp.where(row == ys - 1, 0.0, d)
        kzm[s] = z
        kzp[s] = zp
        sums = (a + b, c0 + d, z + zp)
        total = sums[0] + sums[1] + sums[2] + p2[s]
        for c in range(3):
            value = total + sums[c]
            dg[c, s] = value
            iv[c, s] = jnp.where(e > 0.0, 1.0 / jnp.where(e > 0.0, value, 1.0), 0.0)
            va[c, s] = FIRST * f2[c, s] * iv[c, s]

    loop(1, pairs + 1, coefs)

    def around(v, c, s):
        mid = v[c, s]
        below, above = x_neighbours(v[c, s - 1], mid, v[c, s + 1])
        x = kxm[s] * below + kxp[s] * above
        y = kym[s] * roll(mid, 1, 0) + kyp[s] * roll(mid, -1, 0)
        z = kzm[s] * roll(mid, 1, 1) + kzp[s] * roll(mid, -1, 1)
        return x + y + z + (x, y, z)[c]

    def sweep(source, target, weight):
        def step(s):
            for c in range(3):
                target[c, s] = (1.0 - weight) * source[c, s] + weight * iv[c, s] * (f2[c, s] + around(source, c, s))

        loop(1, pairs + 1, step)

    sweep(va, vb, SECOND)
    n3 = ys // 2

    def gather_rows(at, value):
        tall[...] = value
        rows3[pl.ds(pl.multiple_of(at * n3, 8), n3), :] = tall[pl.ds(0, n3, stride=2), :] + tall[pl.ds(1, n3, stride=2), :]

    def reduce(s):
        for c in range(3):
            gather_rows(c * pairs + s - 1, f2[c, s] - dg[c, s] * vb[c, s] + around(vb, c, s))
        gather_rows(3 * pairs + s - 1, e2[s] * 0.125)
        gather_rows(4 * pairs + s - 1, p2[s])

    loop(1, pairs + 1, reduce)
    down = matrix((BZ, BZ), lambda l, k: ((l & 63) >> 1) == (k & 31))
    rows3[...] = times(rows3[...], down)
    row3 = iota((n3, BZ), 0)
    zero3 = jnp.zeros((n3, BZ), F32)

    def third(at):
        return rows3[pl.ds(pl.multiple_of(at * n3, 8), n3), :]

    e3[0] = zero3
    e3[pairs + 1] = zero3
    for c in range(3):
        for field in (wa, wb):
            field[c, 0] = zero3
            field[c, pairs + 1] = zero3

    def place(s):
        e3[s] = third(3 * pairs + s - 1)

    loop(1, pairs + 1, place)

    def coefs3(s):
        e = e3[s]
        a, b = 8.0 * face(e, e3[s - 1]), 8.0 * face(e, e3[s + 1])
        c0 = 8.0 * face(e, jnp.where(row3 == 0, 0.0, roll(e, 1, 0)))
        d = 8.0 * face(e, jnp.where(row3 == n3 - 1, 0.0, roll(e, -1, 0)))
        z = 8.0 * face(e, roll(e, 1, 1))
        zp = roll(z, -1, 1)
        jx[s] = a
        jx[s + 1] = b
        jym[s] = jnp.where(row3 == 0, 0.0, c0)
        jyp[s] = jnp.where(row3 == n3 - 1, 0.0, d)
        jz[s] = z
        jzp[s] = zp
        sums = (a + b, c0 + d, z + zp)
        total = sums[0] + sums[1] + sums[2] + third(4 * pairs + s - 1)
        for c in range(3):
            value = total + sums[c]
            iv3[c, s] = jnp.where(e > 0.0, 1.0 / jnp.where(e > 0.0, value, 1.0), 0.0)
            wa[c, s] = COARSE * third(c * pairs + s - 1) * iv3[c, s]

    loop(1, pairs + 1, coefs3)
    source, target = wa, wb
    for sweep_at in range(3):
        def step(s, source=source, target=target):
            for c in range(3):
                near = neighbours(source, c, s, jx, jym, jyp, jz, jzp)
                target[c, s] = (1.0 - COARSE) * source[c, s] + COARSE * iv3[c, s] * (third(c * pairs + s - 1) + near)

        loop(1, pairs + 1, step)
        source, target = target, source
    up = matrix((BZ, BZ), lambda k, l: k == ((l & 63) >> 1))
    for c in range(3):
        rows2[...] = times(source[c, 1:pairs + 1].reshape(pairs * n3, BZ), up)

        def add(s, c=c):
            value = rows2[pl.ds(pl.multiple_of((s - 1) * n3, 8), n3), :]
            tall[pl.ds(0, n3, stride=2), :] = value
            tall[pl.ds(1, n3, stride=2), :] = value
            vb[c, s] = vb[c, s] + jnp.where(iv[c, s] > 0.0, tall[...], 0.0)

        loop(1, pairs + 1, add)
    sweep(vb, va, SECOND)

    for c in range(3):
        for at in (0, 1, pairs + 2, pairs + 3):
            out[c, at] = zero

    def last(s):
        for c in range(3):
            out[c, s + 1] = (1.0 - FIRST) * va[c, s] + FIRST * iv[c, s] * (f2[c, s] + around(va, c, s))

    loop(1, pairs + 1, last)


def ascend(pos, gathered, coarse, lower, upper, *rest, nx, ny):
    far, (sums, parts), rest = rest[:10], rest[10:12], rest[12:]
    near, rest = rest[:10], rest[10:]
    e2out, window, rows24, va1, vb1, rows32, spread, vb, precond, term, held = rest[:11]
    v1, f1, kx1, ky1, kyp1, kz1, kzp1, inverse1, stiff1, pen1, diagonal1, v01 = rest[11:23]
    work, copied = rest[23:-1], rest[-1]
    va, start, kx, ky, kyp, kz, kzp, inverse, forward, weights = near
    arrivals = [pltpu.make_async_copy(source, target, copied.at[i]) for i, (source, target) in enumerate(zip(far, near))]
    for move in arrivals:
        move.start()
    departures = []

    def send(lower, upper):
        move = pltpu.make_async_copy(held.at[lower:upper], parts.at[lower:upper], copied.at[10 + len(departures)])
        move.start()
        departures.append(move)

    level_one_again(
        pos, coarse, lower, upper, v1, f1, kx1, ky1, kyp1, kz1, kzp1, inverse1, stiff1, pen1, diagonal1, v01)
    coarse_levels(pos, gathered, e2out, nx, ny, work)
    gx, gy = pos[0], pos[1]
    ys = 4 * ny
    turn = lax.rem(ys - 4 * gy, ys)

    def rule(k, j):
        z = jnp.where((j & 127) < 96, j & 127, (j & 127) - BZ)
        return k == 64 * (j >> 7) + (z >> 1) + 16

    grow = matrix((BZ, LANES), rule)
    for c in range(3):
        for j in range(5):
            window[pl.ds((5 * c + j) * ys, ys), :] = times(pltpu.roll(e2out[c, gx + j], turn, 0), grow)
    for c in range(3):
        for s in range(2, 16):
            x2 = (s - 7) // 2
            j, part = (x2 + 4) // 2, (x2 + 4) % 2
            base = (5 * c + j) * ys
            cols = slice(128 * part, 128 * part + 128)
            if s % 2 == 1 or s == 2:
                low = window[base:base + 8, cols]
                high = window[base + ys - 4:base + ys, cols]
                for at in (0, 1):
                    rows24[pl.ds(at, 8, stride=2), :] = low
                    rows24[pl.ds(16 + at, 4, stride=2), :] = high
            va1[c, s] = v1[c, s] + jnp.where(inverse1[c, s] > 0.0, rows24[...], 0.0)
    faces1 = (kx1, ky1, kyp1, kz1, kzp1)

    def sweep1(source, target, weight, lower, upper):
        def step(s):
            for c in range(3):
                target[c, s] = (1.0 - weight) * source[c, s] + weight * inverse1[c, s] * (
                    f1[c, s] + neighbours(source, c, s, *faces1))

        loop(lower, upper, step)

    sweep1(va1, vb1, SECOND, 3, 15)
    sweep1(vb1, va1, FIRST, 4, 14)
    grow0 = matrix((BZ, LANES), lambda j, l: j == (l >> 1))
    for move in arrivals:
        move.wait()
    for c in range(3):
        spread[...] = times(va1[c, 4:14].reshape(240, BZ), grow0)
        for i in range(10):
            for half in (0, 1):
                cols = slice(BZ * half, BZ * half + BZ)
                value = spread[24 * i:24 * i + 24, cols]
                for at in (0, 1):
                    rows32[pl.ds(at, 12, stride=2), :] = value[:12]
                    rows32[pl.ds(24 + at, 4, stride=2), :] = value[20:]
                for s in (2 * i - 1, 2 * i):
                    if 0 <= s < 18:
                        va[c, s, :, cols] = va[c, s, :, cols] + rows32[...]
    faces = (kx, ky, kyp, kz, kzp)

    def sweep_one(t):
        for c in range(3):
            vb[c, t] = (1.0 - SECOND) * va[c, t + 1] + SECOND * inverse[c, t] * (
                start[c, t] + neighbours(va, c, t + 1, *faces, at=t))

    loop(0, 16, sweep_one)

    def sweep_two(t):
        for c in range(3):
            precond[c, t - 1] = (1.0 - FIRST) * vb[c, t] + FIRST * inverse[c, t] * (start[c, t] + neighbours(vb, c, t, *faces))

    loop(1, 15, sweep_two)

    def keep(x):
        for c in range(3):
            held[c, x] = precond[c, x + 3][:BY, :BZ]
            held[3 + c, x] = start[c, x + 4][:BY, :BZ]

    loop(0, BX, keep)
    send(0, 6)

    def inner(x, carry):
        one, two = carry
        for c in range(3):
            mid = held[c, x]
            value = mid / inverse[c, x + 4][:BY, :BZ] - neighbours(precond, c, x + 3, *faces, at=x + 4)[:BY, :BZ]
            held[6 + c, x] = value
            one = one + held[3 + c, x] * mid
            two = two + mid * value
        return one, two

    zero = jnp.zeros((BY, BZ), F32)
    one, two = lax.fori_loop(0, BX, inner, (zero, zero), unroll=4)
    send(6, 9)
    lane = iota((8, BZ), 1)
    sums[...] = jnp.where(lane == 0, jnp.sum(one), jnp.where(lane == 1, jnp.sum(two), 0.0))
    sensitivity(forward, precond, weights, term)

    def smooth(x):
        held[9, x] = weigh(term, x)

    loop(0, BX, smooth)
    send(9, 10)
    for move in departures:
        move.wait()


def distance_weight(square):
    return max(RADIUS - math.sqrt(square), 0.0)


def sensitivity(state, field, weights, term):
    def energy(i):
        s = i + 1
        total = jnp.zeros((ROWS, LANES), F32)
        for c in range(3):
            a, b = state[c, s], field[c, s]
            along = [(a - state[c, s - 1]) * (b - field[c, s - 1]) + (a - state[c, s + 1]) * (b - field[c, s + 1])]
            for axis in (0, 1):
                along.append(
                    (a - roll(a, 1, axis)) * (b - roll(b, 1, axis)) + (a - roll(a, -1, axis)) * (b - roll(b, -1, axis))
                )
            total = total + (along[0] + along[1] + along[2] + along[c])
        rho = weights[s]
        term[i] = rho * (-3.0 * rho * rho * (0.5 * total))

    loop(0, BX + 4, energy)


def weigh(field, x):
    classes = {}
    for a in range(-2, 3):
        t = field[x + 2 + a]
        for b, value in ((0, t), (1, roll(t, 1, 0) + roll(t, -1, 0)), (2, roll(t, 2, 0) + roll(t, -2, 0))):
            q = a * a + b * b
            classes[q] = value if q not in classes else classes[q] + value
    parts = []
    for z in (0, 1, 2):
        part = None
        for q, value in classes.items():
            w = distance_weight(q + z * z)
            if w > 0.0:
                part = w * value if part is None else part + w * value
        parts.append(part)
    result = parts[0] + roll(parts[1], 1, 1) + roll(parts[1], -1, 1) + roll(parts[2], 2, 1) + roll(parts[2], -2, 1)
    return result[:BY, :BZ]


def filter_iterate(pos, iterate, state, weights, out, term, inside):
    sensitivity(state, iterate, weights, term)

    def mark(i):
        inside[i] = jnp.where(weights[i + 1] > 0.0, 1.0, 0.0)

    loop(0, BX + 4, mark)

    def smooth(x):
        factor = 1.0 / (weights[x + 3][:BY, :BZ] * weigh(inside, x))
        out[0, x] = factor * weigh(term, x)
        out[1, x] = factor

    loop(0, BX, smooth)


def finish(pos, totals, *rest):
    far, (solution, residual, filtered), near, copied = rest[:3], rest[3:6], rest[6:9], rest[9]
    moves = [pltpu.make_async_copy(source, target, copied.at[i]) for i, (source, target) in enumerate(zip(far, near))]
    for move in moves:
        move.start()
    iterate, parts, smooth = near
    total = jnp.sum(totals[...], axis=0, keepdims=True)
    lane = iota((1, BZ), 1)
    one = jnp.sum(jnp.where(lane == 0, total, 0.0), axis=1, keepdims=True)
    two = jnp.sum(jnp.where(lane == 1, total, 0.0), axis=1, keepdims=True)
    alpha = one / two
    for move in moves:
        move.wait()

    def update(x):
        for c in range(3):
            solution[c, x] = iterate[c, x] + alpha * parts[c, x]
            residual[c, x] = parts[3 + c, x] - alpha * parts[6 + c, x]
        filtered[x] = smooth[0, x] + alpha * (parts[9, x] * smooth[1, x])

    loop(0, BX, update)


def body(right_side, iterate, state, classes, load_mask, fixed_mask):
    nx, ny, nz = (lax.axis_size(axis) for axis in ("gx", "gy", "gz"))
    pos = jnp.stack([lax.axis_index("gx"), lax.axis_index("gy"), lax.axis_index("gz")]).astype(jnp.int32)
    pos = jnp.concatenate([pos, jnp.array([nx, ny, nz], jnp.int32)])
    cells = (BX, BY, BZ)
    field = (3,) + cells
    main, last, first = launch(
        4, prepare, [(11,) + cells, cells, cells], [field], [pos],
        far=[right_side, iterate, state, classes, load_mask, fixed_mask], copies=6)
    from_lower, from_upper = shift_along(last, "gz", 1), shift_along(first, "gz", -1)
    edge = (12, BX, BY // 2, BZ)
    packed, to_upper, to_lower = launch(4, pack_rows, [cells, edge, edge], [], [pos, main, from_lower, from_upper])
    from_lower, from_upper = shift_along(to_upper, "gy", 1), shift_along(to_lower, "gy", -1)
    sides = (9 * HALO + 9, ROWS, BZ)
    own, to_upper, to_lower = launch(
        8, pack_slabs, [(12, BX, ROWS, BZ), sides, sides], [], [pos, main, packed, from_lower, from_upper])
    from_lower, from_upper = shift_along(to_upper, "gx", 1), shift_along(to_lower, "gx", -1)

    wide = (ROWS, LANES)

    def slabs(n):
        return (n,) + wide

    def fields(n):
        return (3, n) + wide

    one, three = slabs(SLABS), fields(SLABS)
    quarters = (22, 8, BZ)
    coarse, low, high, v1, start, kx, ky, kyp, kz, kzp, inverse, u, weights, forward = launch(
        24, descend, [(44, 16, BZ), quarters, quarters],
        [three, three, one, one, one, one, one, three, three, one, fields(14), one, three, one, three, three, (ROWS, BZ), (44 * 16, BZ)],
        [pos, own, from_lower, from_upper],
        far_outs=[fields(18), fields(16), slabs(17)] + [slabs(16)] * 4 + [fields(16), fields(14), slabs(14), fields(14)],
        copies=11)
    smooth = launch(
        8, filter_iterate, [(2,) + cells], [slabs(12), slabs(12)], [pos, u, forward, weights],
        cost=pl.CostEstimate(flops=12_000_000, bytes_accessed=4_000_000, transcendentals=0))[0]

    from_lower, from_upper = shift_along(high, "gz", 1), shift_along(low, "gz", -1)
    coarse, center = launch(4, join_lanes, [(44, 16, BZ), (44, 8, BZ)], [], [pos, coarse, from_lower, from_upper])
    from_lower, from_upper = shift_along(center, "gy", 1), shift_along(center, "gy", -1)
    wide1 = (16, BZ)
    one1, three1 = (10,) + wide1, (3, 10) + wide1
    chunk = launch(
        4, level_one, [(24, BZ)], [one1] * 5 + [three1] * 5 + [(8, BZ), (40, BZ), (40, BZ)], [pos, coarse])[0]
    column = lax.all_to_all(jnp.broadcast_to(chunk[None], (ny, 24, BZ)), "gy", 0, 0, tiled=True)
    side = (32, 24, BZ)
    center, to_upper, to_lower = launch(4, join_rows, [(44, 24, BZ), side, side], [], [pos, center, from_lower, from_upper])
    from_lower, from_upper = shift_along(to_upper, "gx", 1), shift_along(to_lower, "gx", -1)
    column = jnp.broadcast_to(column[None], (nx, ny, 24, BZ)).reshape(nx * ny, 24, BZ)
    gathered = lax.all_to_all(column, "gx", 0, 0, tiled=True)

    wide1 = (24, BZ)
    one1, three1 = (18,) + wide1, (3, 18) + wide1
    wide2, wide3 = (4 * ny, BZ), (2 * ny, BZ)
    one2, three2 = (nx + 2,) + wide2, (3, nx + 2) + wide2
    one3, three3 = (nx + 2,) + wide3, (3, nx + 2) + wide3
    work = [one2, one2, three2] + [one2] * 6 + [three2] * 4 + [wide2, (5 * nx * 2 * ny, BZ)]
    work += [one3, one3, three3] + [one3] * 5 + [three3] * 3 + [(nx * 2 * ny, BZ)]
    far = [v1, start, kx, ky, kyp, kz, kzp, inverse, forward, weights]
    parts = (10,) + cells
    scratch = [x.shape for x in far] + [
        (3, nx + 4) + wide2, (15 * 4 * ny, LANES), wide1, three1, three1, (ROWS, BZ), (240, LANES), fields(16), fields(14), slabs(12), parts
    ] + [three1] * 2 + [one1] * 5 + [three1, one1, one1, three1, three1] + work
    sums, parts = launch(
        28, functools.partial(ascend, nx=nx, ny=ny), [(8, BZ)], scratch, [pos, gathered, center, from_lower, from_upper],
        far_outs=[parts], far=far, copies=13)

    total = lax.all_to_all(jnp.broadcast_to(sums[:1], (nx * ny, BZ)), ("gx", "gy"), 0, 0, tiled=True)
    total = jnp.sum(total, axis=0, keepdims=True)
    total = lax.all_to_all(jnp.broadcast_to(total, (nz, BZ)), "gz", 0, 0, tiled=True)
    return tuple(launch(
        4, finish, [field, field, cells], [field, parts.shape, smooth.shape], [pos, total], far=[iterate, parts, smooth], copies=3))


def solution(mesh):
    field, cells = P(None, "gx", "gy", "gz"), P("gx", "gy", "gz")
    return jax.shard_map(
        body,
        mesh=mesh,
        in_specs=(field, field, field, cells, cells, cells),
        out_specs=(field, field, cells),
        check_vma=False,
    )
```

```python
import functools
import math

import jax
import jax.numpy as jnp
from jax import lax
from jax.experimental import pallas as pl
from jax.experimental.pallas import tpu as pltpu
from jax.sharding import PartitionSpec as P

F32 = jnp.float32
FLOOR = 0.25
CLASSES = 16
PENALTY = 4.0
FIRST = 0.55
SECOND = 1.05
COARSE = 0.6
RADIUS = 3

BX, BY, BZ = 8, 16, 128
HALO = 7
SLABS = BX + 2 * HALO
ROWS = 2 * BY
LANES = 2 * BZ

PACKED = 8
ITERATE = ((0, 0, 7), (1, 7, 7), (2, 14, 7))
RHO = (3, 21, 7)
LOAD = ((4, 28, 6), (5, 34, 6), (6, 40, 6))
PEN = (7, 46, 6)
STATE = ((9, 52, 3), (10, 55, 3), (11, 58, 3))
FIELDS = ITERATE + (RHO,) + LOAD + (PEN,) + STATE
HALF = BZ // 2

MIB = 1024 * 1024


def iota(shape, dim):
    return lax.broadcasted_iota(jnp.int32, shape, dim)


def roll(x, shift, axis):
    return pltpu.roll(x, shift % x.shape[axis], axis)


def loop(lower, upper, step, unroll=4):
    def run(i, carry):
        step(i)
        return carry

    lax.fori_loop(lower, upper, run, 0, unroll=unroll)


def times(x, m):
    m = m.astype(jnp.bfloat16)
    high = x.astype(jnp.bfloat16)
    low = (x - high.astype(F32)).astype(jnp.bfloat16)
    return jnp.dot(high, m, preferred_element_type=F32) + jnp.dot(low, m, preferred_element_type=F32)


def matrix(shape, rule):
    return jnp.where(rule(iota(shape, 0), iota(shape, 1)), 1.0, 0.0).astype(F32)


def face(a, b):
    total = a + b
    both = (a > 0.0) & (b > 0.0)
    return jnp.where(both, 2.0 * a * b / jnp.where(both, total, 1.0), total)


def launch(limit, kernel, outs, scratch, operands, far_outs=(), far=(), copies=0, cost=None, pin=False):
    near_spec, far_spec = pl.BlockSpec(memory_space=pltpu.VMEM), pl.BlockSpec(memory_space=pltpu.HBM)
    specs = [pl.BlockSpec(memory_space=pltpu.SMEM)] + [near_spec] * (len(operands) - 1) + [far_spec] * len(far)
    return pl.pallas_call(
        kernel,
        out_shape=[pltpu.VMEM(shape, F32) if pin else jax.ShapeDtypeStruct(shape, F32) for shape in outs] + [pltpu.HBM(shape, F32) for shape in far_outs],
        in_specs=specs,
        out_specs=[near_spec] * len(outs) + [far_spec] * len(far_outs),
        scratch_shapes=[pltpu.VMEM(shape, F32) for shape in scratch] + ([pltpu.SemaphoreType.DMA((copies,))] if copies else []),
        compiler_params=pltpu.CompilerParams(vmem_limit_bytes=limit * MIB),
        cost_estimate=cost,
    )(*(operands[:1] + [pltpu.with_memory_space_constraint(x, pltpu.VMEM) for x in operands[1:]] if pin else operands), *[pltpu.with_memory_space_constraint(x, pltpu.HBM) for x in far])


def shift_along(x, axis, step):
    devices = lax.axis_size(axis)
    return lax.ppermute(x, axis, [(i, (i + step) % devices) for i in range(devices)])


def prepare(pos, right_far, iterate_far, state_far, classes_far, load_far, fixed_far, main, to_upper, to_lower, right, copied):
    def rest(classes, load_mask, fixed_mask):
        moves = [
            pltpu.make_async_copy(source, target, copied.at[i])
            for i, (source, target) in enumerate((
                (classes_far, classes), (load_far, load_mask), (fixed_far, fixed_mask), (right_far, right),
                (iterate_far, main.at[0:3]), (state_far, main.at[8:11])))
        ]
        for move in moves:
            move.start()
        for move in moves:
            move.wait()
        lane = iota((BY, BZ), 1)

        def slab(x):
            mask = load_mask[x].astype(F32)
            main[3, x] = FLOOR + (1.0 - FLOOR) * classes[x].astype(F32) / (CLASSES - 1)
            main[7, x] = PENALTY * fixed_mask[x].astype(F32)
            for c in range(3):
                main[4 + c, x] = right[c, x] * mask
            last = jnp.zeros((BY, BZ), F32)
            first = jnp.zeros((BY, BZ), F32)
            for tile, offset, width in FIELDS:
                value = main[tile if tile < PACKED else tile - 1, x]
                last = jnp.where((lane >= offset) & (lane < offset + width), roll(value, offset + width, 1), last)
                low = HALF + offset
                first = jnp.where((lane >= low) & (lane < low + width), roll(value, low, 1), first)
            to_upper[x] = last
            to_lower[x] = first

        loop(0, BX, slab)

    cells = pltpu.VMEM((BX, BY, BZ), jnp.int32)
    pl.run_scoped(rest, cells, cells, cells)


def pack_rows(pos, main, from_lower, from_upper, packed, to_upper, to_lower):
    below = jnp.where(pos[2] > 0, 1.0, 0.0)
    above = jnp.where(pos[2] < pos[5] - 1, 1.0, 0.0)
    lane = iota((BY, BZ), 1)
    half = BY // 2

    def slab(x):
        joined = jnp.where(lane < HALF, from_lower[x] * below, from_upper[x] * above)
        packed[x] = joined
        for tile in range(12):
            value = joined if tile == PACKED else main[tile if tile < PACKED else tile - 1, x]
            to_upper[tile, x] = value[half:]
            to_lower[tile, x] = value[:half]

    loop(0, BX, slab)


def pack_slabs(pos, main, packed, from_lower, from_upper, own, to_upper, to_lower):
    below = jnp.where(pos[1] > 0, 1.0, 0.0)
    above = jnp.where(pos[1] < pos[4] - 1, 1.0, 0.0)

    def slab(x):
        for tile in range(12):
            value = packed[x] if tile == PACKED else main[tile if tile < PACKED else tile - 1, x]
            own[tile, x] = jnp.concatenate([value, from_upper[tile, x] * above, from_lower[tile, x] * below], 0)

    loop(0, BX, slab)
    for tile in range(9):
        for j in range(HALO):
            to_upper[tile * HALO + j] = own[tile, j + 1]
            to_lower[tile * HALO + j] = own[tile, j]
    for c in range(3):
        for j in range(3):
            to_upper[9 * HALO + 3 * c + j] = own[9 + c, BX - 3 + j]
            to_lower[9 * HALO + 3 * c + j] = own[9 + c, j]


def neighbours(field, c, s, kx, ky, kyp, kz, kzp, at=None):
    at = s if at is None else at
    v = field[c, s]
    x = kx[at] * field[c, s - 1] + kx[at + 1] * field[c, s + 1]
    y = ky[at] * roll(v, 1, 0) + kyp[at] * roll(v, -1, 0)
    z = kz[at] * roll(v, 1, 1) + kzp[at] * roll(v, -1, 1)
    return x + y + z + (x, y, z)[c]


def coefficients(stiff, pen, s, scale, kx, ky, kyp, kz, kzp, inverse, diagonal):
    e = stiff[s]
    upper = scale * face(e, stiff[s + 1])
    kx[s + 1] = upper
    y = scale * face(e, roll(e, 1, 0))
    ky[s] = y
    yp = roll(y, -1, 0)
    kyp[s] = yp
    z = scale * face(e, roll(e, 1, 1))
    kz[s] = z
    zp = roll(z, -1, 1)
    kzp[s] = zp
    pairs = (kx[s] + upper, y + yp, z + zp)
    total = pairs[0] + pairs[1] + pairs[2] + pen[s]
    for c in range(3):
        value = total + pairs[c]
        diagonal[c, s] = value
        inverse[c, s] = jnp.where(e > 0.0, 1.0 / jnp.where(e > 0.0, value, 1.0), 0.0)


def descend(pos, own, lower, upper, coarse, low_lanes, high_lanes, *rest):
    far, rest = rest[:11], rest[11:]
    (v1, start, kx, ky, kyp, kz, kzp, inverse, u, weights, forward, stiff, load, pen, diagonal, v0, half_rows, rows, copied) = rest
    moves = []

    def send(*pairs):
        for source, target in pairs:
            move = pltpu.make_async_copy(source, far[target], copied.at[target])
            move.start()
            moves.append(move)

    below = jnp.where(pos[0] > 0, 1.0, 0.0)
    above = jnp.where(pos[0] < pos[3] - 1, 1.0, 0.0)
    lane = iota((ROWS, BZ), 1)

    def spread(raw, packed, field, store):
        tile, offset, width = field
        store[0][store[1] + (slice(None), slice(0, BZ))] = raw(tile)
        tail = jnp.where(lane >= BZ - width, roll(packed, BZ - width - offset, 1), 0.0)
        tail = jnp.where(lane < width, roll(packed, -(HALF + offset), 1), tail)
        store[0][store[1] + (slice(None), slice(BZ, LANES))] = tail

    def expand(raw, s):
        packed = raw(PACKED)
        spread(raw, packed, RHO, (weights, (s,)))
        spread(raw, packed, PEN, (pen, (s,)))
        for c in range(3):
            spread(raw, packed, ITERATE[c], (u, (c, s)))
            spread(raw, packed, LOAD[c], (load, (c, s)))

    def expand_state(raw, packed, s):
        for c in range(3):
            spread(raw, packed, STATE[c], (forward, (c, s)))

    loop(0, HALO, lambda s: expand(lambda t: lower[t * HALO + s] * below, s))
    loop(0, BX, lambda s: expand(lambda t: own[t, s], s + HALO))
    loop(0, HALO, lambda s: expand(lambda t: upper[t * HALO + s] * above, s + HALO + BX))
    loop(0, 3, lambda s: expand_state(lambda t: lower[9 * HALO + 3 * (t - 9) + s] * below, lower[PACKED * HALO + s + HALO - 3] * below, s))
    loop(0, BX, lambda s: expand_state(lambda t: own[t, s], own[PACKED, s], s + 3))
    loop(0, 3, lambda s: expand_state(lambda t: upper[9 * HALO + 3 * (t - 9) + s] * above, upper[PACKED * HALO + s] * above, s + 3 + BX))

    send((u.at[:, 4:18], 8), (weights.at[4:18], 9), (forward, 10))

    def cube(s):
        rho = weights[s]
        stiff[s] = rho * rho * rho

    loop(0, SLABS, cube)
    kx[1] = face(stiff[0], stiff[1])
    loop(1, SLABS - 1, lambda s: coefficients(stiff, pen, s, 1.0, kx, ky, kyp, kz, kzp, inverse, diagonal))
    faces = (kx, ky, kyp, kz, kzp)
    send((kx.at[3:20], 2), (ky.at[3:19], 3), (kyp.at[3:19], 4), (kz.at[3:19], 5), (kzp.at[3:19], 6), (inverse.at[:, 3:19], 7))

    def begin(s):
        for c in range(3):
            f = load[c, s] - (diagonal[c, s] * u[c, s] - neighbours(u, c, s, *faces))
            start[c, s] = f
            v0[c, s] = FIRST * f * inverse[c, s]

    loop(1, SLABS - 1, begin)
    send((start.at[:, 3:19], 1))

    def sweep(s):
        for c in range(3):
            v1[c, s] = (1.0 - SECOND) * v0[c, s] + SECOND * inverse[c, s] * (start[c, s] + neighbours(v0, c, s, *faces))

    loop(2, SLABS - 2, sweep)
    send((v1.at[:, 2:20], 0))

    def remainder(c, s):
        r = start[c, s] - diagonal[c, s] * v1[c, s] + neighbours(v1, c, s, *faces)
        return r[:, :BZ]

    def gather_rows(at, value):
        half_rows[...] = value
        n = ROWS // 2
        rows[pl.ds(pl.multiple_of(at * n, n), n), :] = half_rows[pl.ds(0, n, stride=2), :] + half_rows[pl.ds(1, n, stride=2), :]

    def pair(i):
        for c in range(3):
            gather_rows(c * 8 + i, remainder(c, 3 + 2 * i) + remainder(c, 4 + 2 * i))

    loop(0, 8, pair)

    def pair_up(i):
        s = 1 + 2 * i
        gather_rows(24 + i, (stiff[s] + stiff[s + 1])[:, :BZ] * 0.125)
        gather_rows(34 + i, (pen[s] + pen[s + 1])[:, :BZ])

    loop(0, 10, pair_up)
    halve = matrix((BZ, BZ), lambda l, k: (l >> 1) == (k & (HALF - 1)))
    coarse[...] = times(rows[...], halve).reshape(44, 16, BZ)
    quarter = iota((8, BZ), 1) >> 5

    def pack(g):
        for h in range(2):
            low = jnp.zeros((8, BZ), F32)
            high = jnp.zeros((8, BZ), F32)
            for q in range(4):
                value = coarse[4 * g + q, 8 * h:8 * h + 8]
                turned = roll(value, 32, 1)
                one, two = (value, turned) if q % 2 == 0 else (turned, value)
                low = jnp.where(quarter == q, one, low)
                high = jnp.where(quarter == q, two, high)
            low_lanes[2 * g + h] = low
            high_lanes[2 * g + h] = high

    loop(0, 11, pack)
    for move in moves:
        move.wait()


def join_lanes(pos, coarse, from_lower, from_upper, out, center):
    below = jnp.where(pos[2] > 0, 1.0, 0.0)
    above = jnp.where(pos[2] < pos[5] - 1, 1.0, 0.0)
    lane = iota((8, BZ), 1)

    def unpack(g):
        for h in range(2):
            low, high = from_lower[2 * g + h] * below, from_upper[2 * g + h] * above
            for q in range(4):
                halo = jnp.where(lane < 96, roll(high, 64 - 32 * q, 1), roll(low, 96 - 32 * q, 1))
                value = jnp.where(lane < 64, coarse[4 * g + q, 8 * h:8 * h + 8], halo)
                out[4 * g + q, 8 * h:8 * h + 8] = value
                if h == 0:
                    center[4 * g + q] = value

    loop(0, 11, unpack)


def join_rows(pos, coarse, from_lower, from_upper, after, to_upper, to_lower, center, out, copied):
    below = jnp.where(pos[1] > 0, 1.0, 0.0)
    above = jnp.where(pos[1] < pos[4] - 1, 1.0, 0.0)

    def join(i):
        out[i] = jnp.concatenate([coarse[i], from_upper[i] * above, from_lower[i] * below], 0)

    loop(0, 44, join)
    move = pltpu.make_async_copy(out, center, copied.at[0])
    move.start()
    at = 0
    for base, count in ((0, 6), (8, 6), (16, 6), (24, 7), (34, 7)):
        shift = 2 if count == 6 else 3
        for j in range(count):
            to_upper[at] = out[base + j]
            to_lower[at] = out[base + shift + j]
            at += 1
    move.wait()


def smooth_down(slabs, f, v0, v1, inverse, faces):
    def begin(s):
        for c in range(3):
            v0[c, s] = FIRST * f[c, s] * inverse[c, s]

    loop(1, slabs - 1, begin)

    def sweep(s):
        for c in range(3):
            v1[c, s] = (1.0 - SECOND) * v0[c, s] + SECOND * inverse[c, s] * (f[c, s] + neighbours(v0, c, s, *faces))

    loop(2, slabs - 2, sweep)


def level_one(pos, own, chunk, kx, ky, kyp, kz, kzp, inverse, diagonal, f, v0, v1, half_rows, rows, wide):
    stiff, pen = own.at[24:34], own.at[34:44]
    slabs = 10
    for c in range(3):
        for i in range(8):
            f[c, 1 + i] = own[8 * c + i]
    kx[1] = 2.0 * face(stiff[0], stiff[1])
    loop(1, slabs - 1, lambda s: coefficients(stiff, pen, s, 2.0, kx, ky, kyp, kz, kzp, inverse, diagonal))
    faces = (kx, ky, kyp, kz, kzp)
    smooth_down(slabs, f, v0, v1, inverse, faces)

    def gather_rows(at, value):
        half_rows[...] = value
        rows[pl.ds(at * 4, 4), :] = half_rows[pl.ds(0, 4, stride=2), :] + half_rows[pl.ds(1, 4, stride=2), :]

    for i in range(2):
        s = 3 + 2 * i
        for c in range(3):
            total = 0.0
            for at in (s, s + 1):
                total = total + (f[c, at] - diagonal[c, at] * v1[c, at] + neighbours(v1, c, at, *faces))[:8]
            gather_rows(2 * c + i, total)
        gather_rows(6 + i, (stiff[s] + stiff[s + 1])[:8] * 0.125)
        gather_rows(8 + i, (pen[s] + pen[s + 1])[:8])

    def rule(j, k):
        z = jnp.where(j < 96, j, j - BZ)
        return (z >> 1) == (k & 63) - 16

    wide[...] = times(rows[...], matrix((BZ, BZ), rule))
    lane = iota((4, BZ), 1)
    chunk[...] = jnp.zeros((24, BZ), F32)
    for field in range(5):
        chunk[4 * field:4 * field + 4] = jnp.where(lane < 64, wide[8 * field:8 * field + 4], wide[8 * field + 4:8 * field + 8])


def pack_column(pos, column, out):
    for i in range(out.shape[0]):
        for j in range(column.shape[0]):
            out[i, 20 * j:20 * j + 20] = column[j, 0:20]


def level_one_again(pos, own, lower, upper, v1, f, kx, ky, kyp, kz, kzp, inverse, stiff, pen, diagonal, v0):
    below = jnp.where(pos[0] > 0, 1.0, 0.0)
    above = jnp.where(pos[0] < pos[3] - 1, 1.0, 0.0)
    slabs = 18
    for field, at in ((stiff, 0), (pen, 1)):
        for j in range(7):
            field[j] = lower[18 + 7 * at + j] * below
            field[11 + j] = upper[18 + 7 * at + j] * above
        for j in range(4):
            field[7 + j] = own[24 + 10 * at + 3 + j]
    for c in range(3):
        for j in range(6):
            f[c, 1 + j] = lower[6 * c + j] * below
            f[c, 11 + j] = upper[6 * c + j] * above
        for j in range(4):
            f[c, 7 + j] = own[8 * c + 2 + j]
    kx[1] = 2.0 * face(stiff[0], stiff[1])
    loop(1, slabs - 1, lambda s: coefficients(stiff, pen, s, 2.0, kx, ky, kyp, kz, kzp, inverse, diagonal))
    smooth_down(slabs, f, v0, v1, inverse, (kx, ky, kyp, kz, kzp))


def coarse_levels(pos, gathered, out, nx, ny, work):
    (e2, p2, f2, kxm, kxp, kym, kyp, kzm, kzp, iv, dg, va, vb, tall, rows3, e3, p3, f3, jx, jym, jyp, jz, jzp, iv3, wa, wb, rows2) = work
    ys = 4 * ny
    pairs = nx
    lane = iota((ys, BZ), 1)
    row = iota((ys, BZ), 0)
    even = lane < 64
    zero = jnp.zeros((ys, BZ), F32)
    for field in (e2, p2):
        field[0] = zero
        field[pairs + 1] = zero
    for c in range(3):
        for field in (va, vb):
            field[c, 0] = zero
            field[c, pairs + 1] = zero

    def collect(g):
        for field in range(5):
            for yy in range(ny):
                value = gathered[g, 20 * yy + 4 * field:20 * yy + 4 * field + 4, :]
                if field < 3:
                    f2[field, g + 1, pl.ds(4 * yy, 4), :] = value
                else:
                    (e2, p2)[field - 3][g + 1, pl.ds(4 * yy, 4), :] = value

    loop(0, pairs, collect)

    def x_neighbours(below, mid, above):
        swapped = roll(mid, 64, 1)
        return jnp.where(even, roll(below, 64, 1), swapped), jnp.where(even, swapped, roll(above, 64, 1))

    def coefs(s):
        e = e2[s]
        xm, xp = x_neighbours(e2[s - 1], e, e2[s + 1])
        ym = jnp.where(row == 0, 0.0, roll(e, 1, 0))
        yp = jnp.where(row == ys - 1, 0.0, roll(e, -1, 0))
        a, b = 4.0 * face(e, xm), 4.0 * face(e, xp)
        c0, d = 4.0 * face(e, ym), 4.0 * face(e, yp)
        z = 4.0 * face(e, roll(e, 1, 1))
        zp = roll(z, -1, 1)
        kxm[s] = a
        kxp[s] = b
        kym[s] = jnp.where(row == 0, 0.0, c0)
        kyp[s] = jnp.where(row == ys - 1, 0.0, d)
        kzm[s] = z
        kzp[s] = zp
        sums = (a + b, c0 + d, z + zp)
        total = sums[0] + sums[1] + sums[2] + p2[s]
        for c in range(3):
            value = total + sums[c]
            dg[c, s] = value
            iv[c, s] = jnp.where(e > 0.0, 1.0 / jnp.where(e > 0.0, value, 1.0), 0.0)
            va[c, s] = FIRST * f2[c, s] * iv[c, s]

    loop(1, pairs + 1, coefs)

    def around(v, c, s):
        mid = v[c, s]
        below, above = x_neighbours(v[c, s - 1], mid, v[c, s + 1])
        x = kxm[s] * below + kxp[s] * above
        y = kym[s] * roll(mid, 1, 0) + kyp[s] * roll(mid, -1, 0)
        z = kzm[s] * roll(mid, 1, 1) + kzp[s] * roll(mid, -1, 1)
        return x + y + z + (x, y, z)[c]

    def sweep(source, target, weight):
        def step(s):
            for c in range(3):
                target[c, s] = (1.0 - weight) * source[c, s] + weight * iv[c, s] * (f2[c, s] + around(source, c, s))

        loop(1, pairs + 1, step)

    sweep(va, vb, SECOND)
    n3 = ys // 2

    def gather_rows(at, value):
        tall[...] = value
        rows3[pl.ds(pl.multiple_of(at * n3, 8), n3), :] = tall[pl.ds(0, n3, stride=2), :] + tall[pl.ds(1, n3, stride=2), :]

    def reduce(s):
        for c in range(3):
            gather_rows(c * pairs + s - 1, f2[c, s] - dg[c, s] * vb[c, s] + around(vb, c, s))
        gather_rows(3 * pairs + s - 1, e2[s] * 0.125)
        gather_rows(4 * pairs + s - 1, p2[s])

    loop(1, pairs + 1, reduce)
    down = matrix((BZ, BZ), lambda l, k: ((l & 63) >> 1) == (k & 31))
    rows3[...] = times(rows3[...], down)
    row3 = iota((n3, BZ), 0)
    zero3 = jnp.zeros((n3, BZ), F32)

    def third(at):
        return rows3[pl.ds(pl.multiple_of(at * n3, 8), n3), :]

    e3[0] = zero3
    e3[pairs + 1] = zero3
    for c in range(3):
        for field in (wa, wb):
            field[c, 0] = zero3
            field[c, pairs + 1] = zero3

    def place(s):
        e3[s] = third(3 * pairs + s - 1)

    loop(1, pairs + 1, place)

    def coefs3(s):
        e = e3[s]
        a, b = 8.0 * face(e, e3[s - 1]), 8.0 * face(e, e3[s + 1])
        c0 = 8.0 * face(e, jnp.where(row3 == 0, 0.0, roll(e, 1, 0)))
        d = 8.0 * face(e, jnp.where(row3 == n3 - 1, 0.0, roll(e, -1, 0)))
        z = 8.0 * face(e, roll(e, 1, 1))
        zp = roll(z, -1, 1)
        jx[s] = a
        jx[s + 1] = b
        jym[s] = jnp.where(row3 == 0, 0.0, c0)
        jyp[s] = jnp.where(row3 == n3 - 1, 0.0, d)
        jz[s] = z
        jzp[s] = zp
        sums = (a + b, c0 + d, z + zp)
        total = sums[0] + sums[1] + sums[2] + third(4 * pairs + s - 1)
        for c in range(3):
            value = total + sums[c]
            iv3[c, s] = jnp.where(e > 0.0, 1.0 / jnp.where(e > 0.0, value, 1.0), 0.0)
            wa[c, s] = COARSE * third(c * pairs + s - 1) * iv3[c, s]

    loop(1, pairs + 1, coefs3)
    source, target = wa, wb
    for sweep_at in range(3):
        def step(s, source=source, target=target):
            for c in range(3):
                near = neighbours(source, c, s, jx, jym, jyp, jz, jzp)
                target[c, s] = (1.0 - COARSE) * source[c, s] + COARSE * iv3[c, s] * (third(c * pairs + s - 1) + near)

        loop(1, pairs + 1, step)
        source, target = target, source
    up = matrix((BZ, BZ), lambda k, l: k == ((l & 63) >> 1))
    for c in range(3):
        rows2[...] = times(source[c, 1:pairs + 1].reshape(pairs * n3, BZ), up)

        def add(s, c=c):
            value = rows2[pl.ds(pl.multiple_of((s - 1) * n3, 8), n3), :]
            tall[pl.ds(0, n3, stride=2), :] = value
            tall[pl.ds(1, n3, stride=2), :] = value
            vb[c, s] = vb[c, s] + jnp.where(iv[c, s] > 0.0, tall[...], 0.0)

        loop(1, pairs + 1, add)
    sweep(vb, va, SECOND)

    for c in range(3):
        for at in (0, 1, pairs + 2, pairs + 3):
            out[c, at] = zero

    def last(s):
        for c in range(3):
            out[c, s + 1] = (1.0 - FIRST) * va[c, s] + FIRST * iv[c, s] * (f2[c, s] + around(va, c, s))

    loop(1, pairs + 1, last)


def ascend(pos, *rest, nx, ny):
    far, (sums, parts), rest = rest[:14], rest[14:16], rest[16:]
    near, rest = rest[:14], rest[14:]
    e2out, window, rows24, va1, vb1, rows32, spread, vb, precond, term, held = rest[:11]
    v1, f1, kx1, ky1, kyp1, kz1, kzp1, inverse1, stiff1, pen1, diagonal1, v01 = rest[11:23]
    work, copied = rest[23:-1], rest[-1]
    gathered, center, lower, upper = near[:4]
    va, start, kx, ky, kyp, kz, kzp, inverse, forward, weights = near[4:]
    arrivals = [pltpu.make_async_copy(source, target, copied.at[i]) for i, (source, target) in enumerate(zip(far, near))]
    for move in arrivals:
        move.start()
    departures = []

    def send(source, target):
        move = pltpu.make_async_copy(source, target, copied.at[14 + len(departures)])
        move.start()
        departures.append(move)

    for move in arrivals[1:4]:
        move.wait()
    level_one_again(
        pos, center, lower, upper, v1, f1, kx1, ky1, kyp1, kz1, kzp1, inverse1, stiff1, pen1, diagonal1, v01)
    arrivals[0].wait()
    coarse_levels(pos, gathered, e2out, nx, ny, work)
    gx, gy = pos[0], pos[1]
    ys = 4 * ny
    turn = lax.rem(ys - 4 * gy, ys)

    def rule(k, j):
        z = jnp.where((j & 127) < 96, j & 127, (j & 127) - BZ)
        return k == 64 * (j >> 7) + (z >> 1) + 16

    grow = matrix((BZ, LANES), rule)
    for c in range(3):
        for j in range(5):
            window[pl.ds((5 * c + j) * ys, ys), :] = times(pltpu.roll(e2out[c, gx + j], turn, 0), grow)
    for c in range(3):
        for s in range(2, 16):
            x2 = (s - 7) // 2
            j, part = (x2 + 4) // 2, (x2 + 4) % 2
            base = (5 * c + j) * ys
            cols = slice(128 * part, 128 * part + 128)
            if s % 2 == 1 or s == 2:
                low = window[base:base + 8, cols]
                high = window[base + ys - 4:base + ys, cols]
                for at in (0, 1):
                    rows24[pl.ds(at, 8, stride=2), :] = low
                    rows24[pl.ds(16 + at, 4, stride=2), :] = high
            va1[c, s] = v1[c, s] + jnp.where(inverse1[c, s] > 0.0, rows24[...], 0.0)
    faces1 = (kx1, ky1, kyp1, kz1, kzp1)

    def sweep1(source, target, weight, lower, upper):
        def step(s):
            for c in range(3):
                target[c, s] = (1.0 - weight) * source[c, s] + weight * inverse1[c, s] * (
                    f1[c, s] + neighbours(source, c, s, *faces1))

        loop(lower, upper, step)

    sweep1(va1, vb1, SECOND, 3, 15)
    sweep1(vb1, va1, FIRST, 4, 14)
    grow0 = matrix((BZ, LANES), lambda j, l: j == (l >> 1))
    for move in arrivals[4:]:
        move.wait()
    for c in range(3):
        spread[...] = times(va1[c, 4:14].reshape(240, BZ), grow0)
        for i in range(10):
            for half in (0, 1):
                cols = slice(BZ * half, BZ * half + BZ)
                value = spread[24 * i:24 * i + 24, cols]
                for at in (0, 1):
                    rows32[pl.ds(at, 12, stride=2), :] = value[:12]
                    rows32[pl.ds(24 + at, 4, stride=2), :] = value[20:]
                for s in (2 * i - 1, 2 * i):
                    if 0 <= s < 18:
                        va[c, s, :, cols] = va[c, s, :, cols] + rows32[...]
    faces = (kx, ky, kyp, kz, kzp)

    def sweep_one(t):
        for c in range(3):
            vb[c, t] = (1.0 - SECOND) * va[c, t + 1] + SECOND * inverse[c, t] * (
                start[c, t] + neighbours(va, c, t + 1, *faces, at=t))

    loop(0, 16, sweep_one)

    def sweep_two(t):
        for c in range(3):
            precond[c, t - 1] = (1.0 - FIRST) * vb[c, t] + FIRST * inverse[c, t] * (start[c, t] + neighbours(vb, c, t, *faces))

    loop(1, 15, sweep_two)

    def keep(x):
        for c in range(3):
            held[c, x] = precond[c, x + 3][:BY, :BZ]
            held[3 + c, x] = start[c, x + 4][:BY, :BZ]

    loop(0, BX, keep)
    send(held.at[0:6], parts.at[0:6])

    def inner(x, carry):
        one, two = carry
        for c in range(3):
            mid = held[c, x]
            value = mid / inverse[c, x + 4][:BY, :BZ] - neighbours(precond, c, x + 3, *faces, at=x + 4)[:BY, :BZ]
            held[6 + c, x] = value
            one = one + held[3 + c, x] * mid
            two = two + mid * value
        return one, two

    zero = jnp.zeros((BY, BZ), F32)
    one, two = lax.fori_loop(0, BX, inner, (zero, zero), unroll=4)
    send(held.at[6:9], parts.at[6:9])
    lane = iota((8, BZ), 1)
    sums[...] = jnp.where(lane == 0, jnp.sum(one), jnp.where(lane == 1, jnp.sum(two), 0.0))
    sensitivity(forward, precond, weights, term)

    def smooth(x):
        held[9, x] = weigh(term, x)

    loop(0, BX, smooth)
    send(held.at[9:10], parts.at[9:10])
    for move in departures:
        move.wait()


def distance_weight(square):
    return max(RADIUS - math.sqrt(square), 0.0)


def sensitivity(state, field, weights, term):
    def energy(i):
        s = i + 1
        total = jnp.zeros((ROWS, LANES), F32)
        for c in range(3):
            a, b = state[c, s], field[c, s]
            along = [(a - state[c, s - 1]) * (b - field[c, s - 1]) + (a - state[c, s + 1]) * (b - field[c, s + 1])]
            for axis in (0, 1):
                along.append(
                    (a - roll(a, 1, axis)) * (b - roll(b, 1, axis)) + (a - roll(a, -1, axis)) * (b - roll(b, -1, axis))
                )
            total = total + (along[0] + along[1] + along[2] + along[c])
        rho = weights[s]
        term[i] = rho * (-3.0 * rho * rho * (0.5 * total))

    loop(0, BX + 4, energy)


def weigh(field, x):
    classes = {}
    for a in range(-2, 3):
        t = field[x + 2 + a]
        for b, value in ((0, t), (1, roll(t, 1, 0) + roll(t, -1, 0)), (2, roll(t, 2, 0) + roll(t, -2, 0))):
            q = a * a + b * b
            classes[q] = value if q not in classes else classes[q] + value
    parts = []
    for z in (0, 1, 2):
        part = None
        for q, value in classes.items():
            w = distance_weight(q + z * z)
            if w > 0.0:
                part = w * value if part is None else part + w * value
        parts.append(part)
    result = parts[0] + roll(parts[1], 1, 1) + roll(parts[1], -1, 1) + roll(parts[2], 2, 1) + roll(parts[2], -2, 1)
    return result[:BY, :BZ]


def arrive(far, near, copied):
    moves = [pltpu.make_async_copy(source, target, copied.at[i]) for i, (source, target) in enumerate(zip(far, near))]
    for move in moves:
        move.start()
    for move in moves:
        move.wait()


def filter_iterate(pos, *rest):
    far, out, near, (term, inside, copied) = rest[:3], rest[3], rest[4:7], rest[7:]
    arrive(far, near, copied)
    iterate, state, weights = near
    sensitivity(state, iterate, weights, term)

    def mark(i):
        inside[i] = jnp.where(weights[i + 1] > 0.0, 1.0, 0.0)

    loop(0, BX + 4, mark)

    def smooth(x):
        factor = 1.0 / (weights[x + 3][:BY, :BZ] * weigh(inside, x))
        out[0, x] = factor * weigh(term, x)
        out[1, x] = factor

    loop(0, BX, smooth)


def finish(pos, totals, *rest):
    far, (solution, residual, filtered), near, copied = rest[:3], rest[3:6], rest[6:9], rest[9]
    moves = [pltpu.make_async_copy(source, target, copied.at[i]) for i, (source, target) in enumerate(zip(far, near))]
    for move in moves:
        move.start()
    iterate, parts, smooth = near
    total = jnp.sum(totals[...], axis=0, keepdims=True)
    lane = iota((1, BZ), 1)
    one = jnp.sum(jnp.where(lane == 0, total, 0.0), axis=1, keepdims=True)
    two = jnp.sum(jnp.where(lane == 1, total, 0.0), axis=1, keepdims=True)
    alpha = one / two
    for move in moves:
        move.wait()

    def update(x):
        for c in range(3):
            solution[c, x] = iterate[c, x] + alpha * parts[c, x]
            residual[c, x] = parts[3 + c, x] - alpha * parts[6 + c, x]
        filtered[x] = smooth[0, x] + alpha * (parts[9, x] * smooth[1, x])

    loop(0, BX, update)


def body(right_side, iterate, state, classes, load_mask, fixed_mask):
    nx, ny, nz = (lax.axis_size(axis) for axis in ("gx", "gy", "gz"))
    pos = jnp.stack([lax.axis_index("gx"), lax.axis_index("gy"), lax.axis_index("gz")]).astype(jnp.int32)
    pos = jnp.concatenate([pos, jnp.array([nx, ny, nz], jnp.int32)])
    cells = (BX, BY, BZ)
    field = (3,) + cells
    main, last, first = launch(
        4, prepare, [(11,) + cells, cells, cells], [field], [pos],
        far=[right_side, iterate, state, classes, load_mask, fixed_mask], copies=6)
    from_lower, from_upper = shift_along(last, "gz", 1), shift_along(first, "gz", -1)
    edge = (12, BX, BY // 2, BZ)
    packed, to_upper, to_lower = launch(4, pack_rows, [cells, edge, edge], [], [pos, main, from_lower, from_upper])
    from_lower, from_upper = shift_along(to_upper, "gy", 1), shift_along(to_lower, "gy", -1)
    sides = (9 * HALO + 9, ROWS, BZ)
    own, to_upper, to_lower = launch(
        8, pack_slabs, [(12, BX, ROWS, BZ), sides, sides], [], [pos, main, packed, from_lower, from_upper])
    from_lower, from_upper = shift_along(to_upper, "gx", 1), shift_along(to_lower, "gx", -1)

    wide = (ROWS, LANES)

    def slabs(n):
        return (n,) + wide

    def fields(n):
        return (3, n) + wide

    one, three = slabs(SLABS), fields(SLABS)
    quarters = (22, 8, BZ)
    coarse, low, high, v1, start, kx, ky, kyp, kz, kzp, inverse, u, weights, forward = launch(
        24, descend, [(44, 16, BZ), quarters, quarters],
        [three, three, one, one, one, one, one, three, three, one, fields(14), one, three, one, three, three, (ROWS, BZ), (44 * 16, BZ)],
        [pos, own, from_lower, from_upper],
        far_outs=[fields(18), fields(16), slabs(17)] + [slabs(16)] * 4 + [fields(16), fields(14), slabs(14), fields(14)],
        copies=11)
    smooth = launch(
        10, filter_iterate, [(2,) + cells], [fields(14), fields(14), slabs(14), slabs(12), slabs(12)], [pos],
        far=[u, forward, weights], copies=3,
        cost=pl.CostEstimate(flops=12_000_000, bytes_accessed=4_000_000, transcendentals=0))[0]

    from_lower, from_upper = shift_along(high, "gz", 1), shift_along(low, "gz", -1)
    coarse, center = launch(4, join_lanes, [(44, 16, BZ), (44, 8, BZ)], [], [pos, coarse, from_lower, from_upper])
    from_lower, from_upper = shift_along(center, "gy", 1), shift_along(center, "gy", -1)
    wide1 = (16, BZ)
    one1, three1 = (10,) + wide1, (3, 10) + wide1
    chunk = launch(
        4, level_one, [(24, BZ)], [one1] * 5 + [three1] * 5 + [(8, BZ), (40, BZ), (40, BZ)], [pos, coarse])[0]
    side = (32, 24, BZ)
    column = lax.all_to_all(jnp.broadcast_to(chunk[None], (ny, 24, BZ)), "gy", 0, 0, tiled=True)
    to_upper, to_lower, center = launch(
        4, join_rows, [side, side], [(44, 24, BZ)], [pos, center, from_lower, from_upper], far=[smooth],
        far_outs=[(44, 24, BZ)], copies=1)
    column = launch(8, pack_column, [(nx, 20 * ny, BZ)], [], [pos, column])[0]
    gathered = lax.all_to_all(column, "gx", 0, 0, tiled=True)
    from_lower, from_upper = shift_along(to_upper, "gx", 1), shift_along(to_lower, "gx", -1)

    wide1 = (24, BZ)
    one1, three1 = (18,) + wide1, (3, 18) + wide1
    wide2, wide3 = (4 * ny, BZ), (2 * ny, BZ)
    one2, three2 = (nx + 2,) + wide2, (3, nx + 2) + wide2
    one3, three3 = (nx + 2,) + wide3, (3, nx + 2) + wide3
    work = [one2, one2, three2] + [one2] * 6 + [three2] * 4 + [wide2, (5 * nx * 2 * ny, BZ)]
    work += [one3, one3, three3] + [one3] * 5 + [three3] * 3 + [(nx * 2 * ny, BZ)]
    parts = (10,) + cells
    far = [gathered, center, from_lower, from_upper, v1, start, kx, ky, kyp, kz, kzp, inverse, forward, weights]
    scratch = [x.shape for x in far] + [
        (3, nx + 4) + wide2, (15 * 4 * ny, LANES), wide1, three1, three1, (ROWS, BZ), (240, LANES), fields(16), fields(14), slabs(12), parts
    ] + [three1] * 2 + [one1] * 5 + [three1, one1, one1, three1, three1] + work
    sums, parts = launch(
        30, functools.partial(ascend, nx=nx, ny=ny), [(8, BZ)], scratch, [pos], far_outs=[parts], far=far, copies=17)

    total = lax.all_to_all(jnp.broadcast_to(sums[:1], (nx * ny, BZ)), ("gx", "gy"), 0, 0, tiled=True)
    total = jnp.sum(total, axis=0, keepdims=True)
    total = lax.all_to_all(jnp.broadcast_to(total, (nz, BZ)), "gz", 0, 0, tiled=True)
    return tuple(launch(
        4, finish, [field, field, cells], [field, parts.shape, smooth.shape], [pos, total],
        far=[iterate, parts, smooth], copies=3))


def solution(mesh):
    field, cells = P(None, "gx", "gy", "gz"), P("gx", "gy", "gz")
    return jax.shard_map(
        body,
        mesh=mesh,
        in_specs=(field, field, field, cells, cells, cells),
        out_specs=(field, field, cells),
        check_vma=False,
    )
```

```python
import functools
import math

import jax
import jax.numpy as jnp
from jax import lax
from jax.experimental import pallas as pl
from jax.experimental.pallas import tpu as pltpu
from jax.sharding import PartitionSpec as P

F32 = jnp.float32
FLOOR = 0.25
CLASSES = 16
PENALTY = 4.0
FIRST = 0.55
SECOND = 1.05
COARSE = 0.6
RADIUS = 3

BX, BY, BZ = 8, 16, 128
HALO = 7
SLABS = BX + 2 * HALO
ROWS = 2 * BY
LANES = 2 * BZ

PACKED = 8
ITERATE = ((0, 0, 7), (1, 7, 7), (2, 14, 7))
RHO = (3, 21, 7)
LOAD = ((4, 28, 6), (5, 34, 6), (6, 40, 6))
PEN = (7, 46, 6)
STATE = ((9, 52, 3), (10, 55, 3), (11, 58, 3))
FIELDS = ITERATE + (RHO,) + LOAD + (PEN,) + STATE
HALF = BZ // 2

MIB = 1024 * 1024


def iota(shape, dim):
    return lax.broadcasted_iota(jnp.int32, shape, dim)


def roll(x, shift, axis):
    return pltpu.roll(x, shift % x.shape[axis], axis)


def loop(lower, upper, step, unroll=4):
    def run(i, carry):
        step(i)
        return carry

    lax.fori_loop(lower, upper, run, 0, unroll=unroll)


def times(x, m):
    m = m.astype(jnp.bfloat16)
    high = x.astype(jnp.bfloat16)
    low = (x - high.astype(F32)).astype(jnp.bfloat16)
    return jnp.dot(high, m, preferred_element_type=F32) + jnp.dot(low, m, preferred_element_type=F32)


def matrix(shape, rule):
    return jnp.where(rule(iota(shape, 0), iota(shape, 1)), 1.0, 0.0).astype(F32)


def face(a, b):
    total = a + b
    both = (a > 0.0) & (b > 0.0)
    return jnp.where(both, 2.0 * a * b / jnp.where(both, total, 1.0), total)


def launch(limit, kernel, outs, scratch, operands, far_outs=(), far=(), copies=0, cost=None, pin=False):
    near_spec, far_spec = pl.BlockSpec(memory_space=pltpu.VMEM), pl.BlockSpec(memory_space=pltpu.HBM)
    specs = [pl.BlockSpec(memory_space=pltpu.SMEM)] + [near_spec] * (len(operands) - 1) + [far_spec] * len(far)
    return pl.pallas_call(
        kernel,
        out_shape=[pltpu.VMEM(shape, F32) if pin else jax.ShapeDtypeStruct(shape, F32) for shape in outs] + [pltpu.HBM(shape, F32) for shape in far_outs],
        in_specs=specs,
        out_specs=[near_spec] * len(outs) + [far_spec] * len(far_outs),
        scratch_shapes=[pltpu.VMEM(shape, F32) for shape in scratch] + ([pltpu.SemaphoreType.DMA((copies,))] if copies else []),
        compiler_params=pltpu.CompilerParams(vmem_limit_bytes=limit * MIB),
        cost_estimate=cost,
    )(*(operands[:1] + [pltpu.with_memory_space_constraint(x, pltpu.VMEM) for x in operands[1:]] if pin else operands), *[pltpu.with_memory_space_constraint(x, pltpu.HBM) for x in far])


def shift_along(x, axis, step):
    devices = lax.axis_size(axis)
    return lax.ppermute(x, axis, [(i, (i + step) % devices) for i in range(devices)])


def prepare(pos, right_far, iterate_far, state_far, classes_far, load_far, fixed_far, main, to_upper, to_lower, right, copied):
    def rest(classes, load_mask, fixed_mask):
        moves = [
            pltpu.make_async_copy(source, target, copied.at[i])
            for i, (source, target) in enumerate((
                (classes_far, classes), (load_far, load_mask), (fixed_far, fixed_mask), (right_far, right),
                (iterate_far, main.at[0:3]), (state_far, main.at[8:11])))
        ]
        for move in moves:
            move.start()
        for move in moves:
            move.wait()
        lane = iota((BY, BZ), 1)

        def slab(x):
            mask = load_mask[x].astype(F32)
            main[3, x] = FLOOR + (1.0 - FLOOR) * classes[x].astype(F32) / (CLASSES - 1)
            main[7, x] = PENALTY * fixed_mask[x].astype(F32)
            for c in range(3):
                main[4 + c, x] = right[c, x] * mask
            last = jnp.zeros((BY, BZ), F32)
            first = jnp.zeros((BY, BZ), F32)
            for tile, offset, width in FIELDS:
                value = main[tile if tile < PACKED else tile - 1, x]
                last = jnp.where((lane >= offset) & (lane < offset + width), roll(value, offset + width, 1), last)
                low = HALF + offset
                first = jnp.where((lane >= low) & (lane < low + width), roll(value, low, 1), first)
            to_upper[x] = last
            to_lower[x] = first

        loop(0, BX, slab)

    cells = pltpu.VMEM((BX, BY, BZ), jnp.int32)
    pl.run_scoped(rest, cells, cells, cells)


def pack_rows(pos, main, from_lower, from_upper, packed, to_upper, to_lower):
    below = jnp.where(pos[2] > 0, 1.0, 0.0)
    above = jnp.where(pos[2] < pos[5] - 1, 1.0, 0.0)
    lane = iota((BY, BZ), 1)
    half = BY // 2

    def slab(x):
        joined = jnp.where(lane < HALF, from_lower[x] * below, from_upper[x] * above)
        packed[x] = joined
        for tile in range(12):
            value = joined if tile == PACKED else main[tile if tile < PACKED else tile - 1, x]
            to_upper[tile, x] = value[half:]
            to_lower[tile, x] = value[:half]

    loop(0, BX, slab)


def neighbours(field, c, s, kx, ky, kyp, kz, kzp, at=None):
    at = s if at is None else at
    v = field[c, s]
    x = kx[at] * field[c, s - 1] + kx[at + 1] * field[c, s + 1]
    y = ky[at] * roll(v, 1, 0) + kyp[at] * roll(v, -1, 0)
    z = kz[at] * roll(v, 1, 1) + kzp[at] * roll(v, -1, 1)
    return x + y + z + (x, y, z)[c]


def coefficients(stiff, pen, s, scale, kx, ky, kyp, kz, kzp, inverse, diagonal):
    e = stiff[s]
    upper = scale * face(e, stiff[s + 1])
    kx[s + 1] = upper
    y = scale * face(e, roll(e, 1, 0))
    ky[s] = y
    yp = roll(y, -1, 0)
    kyp[s] = yp
    z = scale * face(e, roll(e, 1, 1))
    kz[s] = z
    zp = roll(z, -1, 1)
    kzp[s] = zp
    pairs = (kx[s] + upper, y + yp, z + zp)
    total = pairs[0] + pairs[1] + pairs[2] + pen[s]
    for c in range(3):
        value = total + pairs[c]
        diagonal[c, s] = value
        if inverse is not None:
            inverse[c, s] = jnp.where(e > 0.0, 1.0 / jnp.where(e > 0.0, value, 1.0), 0.0)


def spread(value, packed, field, ref, at):
    _, offset, width = field
    lane = iota((ROWS, BZ), 1)
    ref[at + (slice(None), slice(0, BZ))] = value
    tail = jnp.where(lane >= BZ - width, roll(packed, BZ - width - offset, 1), 0.0)
    tail = jnp.where(lane < width, roll(packed, -(HALF + offset), 1), tail)
    ref[at + (slice(None), slice(BZ, LANES))] = tail


LAYERS = ((RHO[0], 7), (PACKED, 7)) + tuple((f[0], 6) for f in LOAD + (PEN,)) + tuple((f[0], 3) for f in ITERATE + STATE)
PLACE = {}
SENT = 0
for _tile, _count in LAYERS:
    PLACE[_tile] = SENT
    SENT += _count


def pack_slabs(pos, main, packed, from_lower, from_upper, own, to_upper, to_lower,
               rho, stiff, pen, u, load, kx, ky, kyp, kz, kzp, diagonal):
    below = jnp.where(pos[1] > 0, 1.0, 0.0)
    above = jnp.where(pos[1] < pos[4] - 1, 1.0, 0.0)

    def slab(x):
        for tile in range(12):
            value = packed[x] if tile == PACKED else main[tile if tile < PACKED else tile - 1, x]
            own[tile, x] = jnp.concatenate([value, from_upper[tile, x] * above, from_lower[tile, x] * below], 0)

    loop(0, BX, slab)

    def expand(x):
        halo = own[PACKED, x]
        spread(own[RHO[0], x], halo, RHO, rho, (x,))
        spread(own[PEN[0], x], halo, PEN, pen, (x,))
        for c in range(3):
            spread(own[ITERATE[c][0], x], halo, ITERATE[c], u, (c, x))
            spread(own[LOAD[c][0], x], halo, LOAD[c], load, (c, x))
        stiff[x] = rho[x] * rho[x] * rho[x]

    loop(0, BX, expand)
    kx[1] = face(stiff[0], stiff[1])
    loop(1, BX - 1, lambda x: coefficients(stiff, pen, x, 1.0, kx, ky, kyp, kz, kzp, None, diagonal))
    lane = iota((ROWS, BZ), 1)

    def begin(x):
        halo = own[PACKED, x]
        for c in range(3):
            f = load[c, x] - (diagonal[c, x] * u[c, x] - neighbours(u, c, x, kx, ky, kyp, kz, kzp))
            tile, offset, width = LOAD[c]
            own[tile, x] = f[:, :BZ]
            tail = f[:, BZ:]
            halo = jnp.where((lane >= offset) & (lane < offset + width), roll(tail, offset + width, 1), halo)
            low = HALF + offset
            halo = jnp.where((lane >= low) & (lane < low + width), roll(tail, low, 1), halo)
        own[PACKED, x] = halo

    loop(1, BX - 1, begin)
    for tile, count in LAYERS:
        for j in range(count):
            to_upper[PLACE[tile] + j] = own[tile, BX - count + j]
            to_lower[PLACE[tile] + j] = own[tile, j]


def descend(pos, own, lower, upper, coarse, low_lanes, high_lanes, *rest):
    far, rest = rest[:11], rest[11:]
    (v1, start, kx, ky, kyp, kz, kzp, inverse, u, weights, forward, stiff, pen, diagonal, v0, half_rows, rows, copied) = rest
    moves = []

    def send(*pairs):
        for source, target in pairs:
            move = pltpu.make_async_copy(source, far[target], copied.at[target])
            move.start()
            moves.append(move)

    below = jnp.where(pos[0] > 0, 1.0, 0.0)
    above = jnp.where(pos[0] < pos[3] - 1, 1.0, 0.0)

    def expand(raw, s, fields):
        halo = raw(PACKED)
        for field, ref, at in fields:
            spread(raw(field[0]), halo, field, ref, at)

    def densities(s):
        return [(RHO, weights, (s,))]

    def loads(s):
        return [(PEN, pen, (s,))] + [(LOAD[c], start, (c, s)) for c in range(3)]

    def motions(s):
        return [(ITERATE[c], u, (c, s)) for c in range(3)] + [(STATE[c], forward, (c, s - 4)) for c in range(3)]

    def lower_raw(s):
        return lambda t: lower[PLACE[t] + s - (HALO - dict(LAYERS)[t])] * below

    def upper_raw(s):
        return lambda t: upper[PLACE[t] + s - (HALO + BX)] * above

    after = HALO + BX
    loop(0, HALO, lambda s: expand(lower_raw(s), s, densities(s)))
    loop(1, HALO, lambda s: expand(lower_raw(s), s, loads(s)))
    loop(4, HALO, lambda s: expand(lower_raw(s), s, motions(s)))
    loop(HALO, after, lambda s: expand(lambda t: own[t, s - HALO], s, densities(s) + loads(s) + motions(s)))
    loop(after, after + 7, lambda s: expand(upper_raw(s), s, densities(s)))
    loop(after, after + 6, lambda s: expand(upper_raw(s), s, loads(s)))
    loop(after, after + 3, lambda s: expand(upper_raw(s), s, motions(s)))
    send((u.at[:, 4:18], 8), (weights.at[4:18], 9), (forward, 10))

    def cube(s):
        rho = weights[s]
        stiff[s] = rho * rho * rho

    loop(0, SLABS, cube)
    kx[1] = face(stiff[0], stiff[1])
    loop(1, SLABS - 1, lambda s: coefficients(stiff, pen, s, 1.0, kx, ky, kyp, kz, kzp, inverse, diagonal))
    faces = (kx, ky, kyp, kz, kzp)
    send((kx.at[3:20], 2), (ky.at[3:19], 3), (kyp.at[3:19], 4), (kz.at[3:19], 5), (kzp.at[3:19], 6), (inverse.at[:, 3:19], 7))

    for s in (HALO - 1, HALO, HALO + BX - 1, HALO + BX):
        for c in range(3):
            start[c, s] = start[c, s] - (diagonal[c, s] * u[c, s] - neighbours(u, c, s, *faces))

    def begin(s):
        for c in range(3):
            v0[c, s] = FIRST * start[c, s] * inverse[c, s]

    loop(1, SLABS - 1, begin)
    send((start.at[:, 3:19], 1))

    def sweep(s):
        for c in range(3):
            v1[c, s] = (1.0 - SECOND) * v0[c, s] + SECOND * inverse[c, s] * (start[c, s] + neighbours(v0, c, s, *faces))

    loop(2, SLABS - 2, sweep)
    send((v1.at[:, 2:20], 0))

    def remainder(c, s):
        r = start[c, s] - diagonal[c, s] * v1[c, s] + neighbours(v1, c, s, *faces)
        return r[:, :BZ]

    def gather_rows(at, value):
        half_rows[...] = value
        n = ROWS // 2
        rows[pl.ds(pl.multiple_of(at * n, n), n), :] = half_rows[pl.ds(0, n, stride=2), :] + half_rows[pl.ds(1, n, stride=2), :]

    def pair(i):
        for c in range(3):
            gather_rows(c * 8 + i, remainder(c, 3 + 2 * i) + remainder(c, 4 + 2 * i))

    loop(0, 8, pair)

    def pair_up(i):
        s = 1 + 2 * i
        gather_rows(24 + i, (stiff[s] + stiff[s + 1])[:, :BZ] * 0.125)
        gather_rows(34 + i, (pen[s] + pen[s + 1])[:, :BZ])

    loop(0, 10, pair_up)
    halve = matrix((BZ, BZ), lambda l, k: (l >> 1) == (k & (HALF - 1)))
    coarse[...] = times(rows[...], halve).reshape(44, 16, BZ)
    quarter = iota((8, BZ), 1) >> 5

    def pack(g):
        for h in range(2):
            low = jnp.zeros((8, BZ), F32)
            high = jnp.zeros((8, BZ), F32)
            for q in range(4):
                value = coarse[4 * g + q, 8 * h:8 * h + 8]
                turned = roll(value, 32, 1)
                one, two = (value, turned) if q % 2 == 0 else (turned, value)
                low = jnp.where(quarter == q, one, low)
                high = jnp.where(quarter == q, two, high)
            low_lanes[2 * g + h] = low
            high_lanes[2 * g + h] = high

    loop(0, 11, pack)
    for move in moves:
        move.wait()


def join_lanes(pos, coarse, from_lower, from_upper, out, center):
    below = jnp.where(pos[2] > 0, 1.0, 0.0)
    above = jnp.where(pos[2] < pos[5] - 1, 1.0, 0.0)
    lane = iota((8, BZ), 1)

    def unpack(g):
        for h in range(2):
            low, high = from_lower[2 * g + h] * below, from_upper[2 * g + h] * above
            for q in range(4):
                halo = jnp.where(lane < 96, roll(high, 64 - 32 * q, 1), roll(low, 96 - 32 * q, 1))
                value = jnp.where(lane < 64, coarse[4 * g + q, 8 * h:8 * h + 8], halo)
                out[4 * g + q, 8 * h:8 * h + 8] = value
                if h == 0:
                    center[4 * g + q] = value

    loop(0, 11, unpack)


def join_rows(pos, coarse, from_lower, from_upper, to_upper, to_lower, center, out, copied):
    below = jnp.where(pos[1] > 0, 1.0, 0.0)
    above = jnp.where(pos[1] < pos[4] - 1, 1.0, 0.0)

    def join(i):
        out[i] = jnp.concatenate([coarse[i], from_upper[i] * above, from_lower[i] * below], 0)

    loop(0, 44, join)
    move = pltpu.make_async_copy(out, center, copied.at[0])
    move.start()
    at = 0
    for base, count in ((0, 6), (8, 6), (16, 6), (24, 7), (34, 7)):
        shift = 2 if count == 6 else 3
        for j in range(count):
            to_upper[at] = out[base + j]
            to_lower[at] = out[base + shift + j]
            at += 1
    move.wait()


def smooth_down(slabs, f, v0, v1, inverse, faces):
    def begin(s):
        for c in range(3):
            v0[c, s] = FIRST * f[c, s] * inverse[c, s]

    loop(1, slabs - 1, begin)

    def sweep(s):
        for c in range(3):
            v1[c, s] = (1.0 - SECOND) * v0[c, s] + SECOND * inverse[c, s] * (f[c, s] + neighbours(v0, c, s, *faces))

    loop(2, slabs - 2, sweep)


def level_one(pos, own, chunk, kx, ky, kyp, kz, kzp, inverse, diagonal, f, v0, v1, half_rows, rows, wide):
    stiff, pen = own.at[24:34], own.at[34:44]
    slabs = 10
    for c in range(3):
        for i in range(8):
            f[c, 1 + i] = own[8 * c + i]
    kx[1] = 2.0 * face(stiff[0], stiff[1])
    loop(1, slabs - 1, lambda s: coefficients(stiff, pen, s, 2.0, kx, ky, kyp, kz, kzp, inverse, diagonal))
    faces = (kx, ky, kyp, kz, kzp)
    smooth_down(slabs, f, v0, v1, inverse, faces)

    def gather_rows(at, value):
        half_rows[...] = value
        rows[pl.ds(at * 4, 4), :] = half_rows[pl.ds(0, 4, stride=2), :] + half_rows[pl.ds(1, 4, stride=2), :]

    for i in range(2):
        s = 3 + 2 * i
        for c in range(3):
            total = 0.0
            for at in (s, s + 1):
                total = total + (f[c, at] - diagonal[c, at] * v1[c, at] + neighbours(v1, c, at, *faces))[:8]
            gather_rows(2 * c + i, total)
        gather_rows(6 + i, (stiff[s] + stiff[s + 1])[:8] * 0.125)
        gather_rows(8 + i, (pen[s] + pen[s + 1])[:8])

    def rule(j, k):
        z = jnp.where(j < 96, j, j - BZ)
        return (z >> 1) == (k & 63) - 16

    wide[...] = times(rows[...], matrix((BZ, BZ), rule))
    lane = iota((4, BZ), 1)
    parts = [jnp.where(lane < 64, wide[8 * field:8 * field + 4], wide[8 * field + 4:8 * field + 8]) for field in range(5)]
    value = jnp.concatenate(parts + [jnp.zeros((4, BZ), F32)], 0)
    for i in range(chunk.shape[0]):
        chunk[i] = value


def pack_column(pos, column, out):
    for i in range(out.shape[0]):
        for j in range(column.shape[0]):
            out[i, 20 * j:20 * j + 20] = column[j, 0:20]


def level_one_again(pos, own, lower, upper, v1, f, kx, ky, kyp, kz, kzp, inverse, stiff, pen, diagonal, v0):
    below = jnp.where(pos[0] > 0, 1.0, 0.0)
    above = jnp.where(pos[0] < pos[3] - 1, 1.0, 0.0)
    slabs = 18
    for field, at in ((stiff, 0), (pen, 1)):
        for j in range(7):
            field[j] = lower[18 + 7 * at + j] * below
            field[11 + j] = upper[18 + 7 * at + j] * above
        for j in range(4):
            field[7 + j] = own[24 + 10 * at + 3 + j]
    for c in range(3):
        for j in range(6):
            f[c, 1 + j] = lower[6 * c + j] * below
            f[c, 11 + j] = upper[6 * c + j] * above
        for j in range(4):
            f[c, 7 + j] = own[8 * c + 2 + j]
    kx[1] = 2.0 * face(stiff[0], stiff[1])
    loop(1, slabs - 1, lambda s: coefficients(stiff, pen, s, 2.0, kx, ky, kyp, kz, kzp, inverse, diagonal))
    smooth_down(slabs, f, v0, v1, inverse, (kx, ky, kyp, kz, kzp))


def coarse_levels(pos, gathered, out, nx, ny, work):
    (e2, p2, f2, kxm, kxp, kym, kyp, kzm, kzp, iv, dg, va, vb, tall, rows3, e3, p3, f3, jx, jym, jyp, jz, jzp, iv3, wa, wb, rows2) = work
    ys = 4 * ny
    pairs = nx
    lane = iota((ys, BZ), 1)
    row = iota((ys, BZ), 0)
    even = lane < 64
    zero = jnp.zeros((ys, BZ), F32)
    for field in (e2, p2):
        field[0] = zero
        field[pairs + 1] = zero
    for c in range(3):
        for field in (va, vb):
            field[c, 0] = zero
            field[c, pairs + 1] = zero

    def collect(g):
        for field in range(5):
            for yy in range(ny):
                value = gathered[g, 20 * yy + 4 * field:20 * yy + 4 * field + 4, :]
                if field < 3:
                    f2[field, g + 1, pl.ds(4 * yy, 4), :] = value
                else:
                    (e2, p2)[field - 3][g + 1, pl.ds(4 * yy, 4), :] = value

    loop(0, pairs, collect)

    def x_neighbours(below, mid, above):
        swapped = roll(mid, 64, 1)
        return jnp.where(even, roll(below, 64, 1), swapped), jnp.where(even, swapped, roll(above, 64, 1))

    def coefs(s):
        e = e2[s]
        xm, xp = x_neighbours(e2[s - 1], e, e2[s + 1])
        ym = jnp.where(row == 0, 0.0, roll(e, 1, 0))
        yp = jnp.where(row == ys - 1, 0.0, roll(e, -1, 0))
        a, b = 4.0 * face(e, xm), 4.0 * face(e, xp)
        c0, d = 4.0 * face(e, ym), 4.0 * face(e, yp)
        z = 4.0 * face(e, roll(e, 1, 1))
        zp = roll(z, -1, 1)
        kxm[s] = a
        kxp[s] = b
        kym[s] = jnp.where(row == 0, 0.0, c0)
        kyp[s] = jnp.where(row == ys - 1, 0.0, d)
        kzm[s] = z
        kzp[s] = zp
        sums = (a + b, c0 + d, z + zp)
        total = sums[0] + sums[1] + sums[2] + p2[s]
        for c in range(3):
            value = total + sums[c]
            dg[c, s] = value
            iv[c, s] = jnp.where(e > 0.0, 1.0 / jnp.where(e > 0.0, value, 1.0), 0.0)
            va[c, s] = FIRST * f2[c, s] * iv[c, s]

    loop(1, pairs + 1, coefs)

    def around(v, c, s):
        mid = v[c, s]
        below, above = x_neighbours(v[c, s - 1], mid, v[c, s + 1])
        x = kxm[s] * below + kxp[s] * above
        y = kym[s] * roll(mid, 1, 0) + kyp[s] * roll(mid, -1, 0)
        z = kzm[s] * roll(mid, 1, 1) + kzp[s] * roll(mid, -1, 1)
        return x + y + z + (x, y, z)[c]

    def sweep(source, target, weight):
        def step(s):
            for c in range(3):
                target[c, s] = (1.0 - weight) * source[c, s] + weight * iv[c, s] * (f2[c, s] + around(source, c, s))

        loop(1, pairs + 1, step)

    sweep(va, vb, SECOND)
    n3 = ys // 2

    def gather_rows(at, value):
        tall[...] = value
        rows3[pl.ds(pl.multiple_of(at * n3, 8), n3), :] = tall[pl.ds(0, n3, stride=2), :] + tall[pl.ds(1, n3, stride=2), :]

    def reduce(s):
        for c in range(3):
            gather_rows(c * pairs + s - 1, f2[c, s] - dg[c, s] * vb[c, s] + around(vb, c, s))
        gather_rows(3 * pairs + s - 1, e2[s] * 0.125)
        gather_rows(4 * pairs + s - 1, p2[s])

    loop(1, pairs + 1, reduce)
    down = matrix((BZ, BZ), lambda l, k: ((l & 63) >> 1) == (k & 31))
    rows3[...] = times(rows3[...], down)
    row3 = iota((n3, BZ), 0)
    zero3 = jnp.zeros((n3, BZ), F32)

    def third(at):
        return rows3[pl.ds(pl.multiple_of(at * n3, 8), n3), :]

    e3[0] = zero3
    e3[pairs + 1] = zero3
    for c in range(3):
        for field in (wa, wb):
            field[c, 0] = zero3
            field[c, pairs + 1] = zero3

    def place(s):
        e3[s] = third(3 * pairs + s - 1)

    loop(1, pairs + 1, place)

    def coefs3(s):
        e = e3[s]
        a, b = 8.0 * face(e, e3[s - 1]), 8.0 * face(e, e3[s + 1])
        c0 = 8.0 * face(e, jnp.where(row3 == 0, 0.0, roll(e, 1, 0)))
        d = 8.0 * face(e, jnp.where(row3 == n3 - 1, 0.0, roll(e, -1, 0)))
        z = 8.0 * face(e, roll(e, 1, 1))
        zp = roll(z, -1, 1)
        jx[s] = a
        jx[s + 1] = b
        jym[s] = jnp.where(row3 == 0, 0.0, c0)
        jyp[s] = jnp.where(row3 == n3 - 1, 0.0, d)
        jz[s] = z
        jzp[s] = zp
        sums = (a + b, c0 + d, z + zp)
        total = sums[0] + sums[1] + sums[2] + third(4 * pairs + s - 1)
        for c in range(3):
            value = total + sums[c]
            iv3[c, s] = jnp.where(e > 0.0, 1.0 / jnp.where(e > 0.0, value, 1.0), 0.0)
            wa[c, s] = COARSE * third(c * pairs + s - 1) * iv3[c, s]

    loop(1, pairs + 1, coefs3)
    source, target = wa, wb
    for sweep_at in range(3):
        def step(s, source=source, target=target):
            for c in range(3):
                near = neighbours(source, c, s, jx, jym, jyp, jz, jzp)
                target[c, s] = (1.0 - COARSE) * source[c, s] + COARSE * iv3[c, s] * (third(c * pairs + s - 1) + near)

        loop(1, pairs + 1, step)
        source, target = target, source
    up = matrix((BZ, BZ), lambda k, l: k == ((l & 63) >> 1))
    for c in range(3):
        rows2[...] = times(source[c, 1:pairs + 1].reshape(pairs * n3, BZ), up)

        def add(s, c=c):
            value = rows2[pl.ds(pl.multiple_of((s - 1) * n3, 8), n3), :]
            tall[pl.ds(0, n3, stride=2), :] = value
            tall[pl.ds(1, n3, stride=2), :] = value
            vb[c, s] = vb[c, s] + jnp.where(iv[c, s] > 0.0, tall[...], 0.0)

        loop(1, pairs + 1, add)
    sweep(vb, va, SECOND)

    for c in range(3):
        for at in (0, 1, pairs + 2, pairs + 3):
            out[c, at] = zero

    def last(s):
        for c in range(3):
            out[c, s + 1] = (1.0 - FIRST) * va[c, s] + FIRST * iv[c, s] * (f2[c, s] + around(va, c, s))

    loop(1, pairs + 1, last)


def ascend(pos, *rest, nx, ny):
    far, (sums, parts), rest = rest[:14], rest[15:17], rest[17:]
    near, rest = rest[:14], rest[14:]
    e2out, window, rows24, va1, vb1, rows32, spread, vb, precond, term, held = rest[:11]
    v1, f1, kx1, ky1, kyp1, kz1, kzp1, inverse1, stiff1, pen1, diagonal1, v01 = rest[11:23]
    work, copied = rest[23:-1], rest[-1]
    gathered, center, lower, upper = near[:4]
    va, start, kx, ky, kyp, kz, kzp, inverse, forward, weights = near[4:]
    arrivals = [pltpu.make_async_copy(source, target, copied.at[i]) for i, (source, target) in enumerate(zip(far, near))]
    for move in arrivals:
        move.start()
    departures = []

    def send(source, target):
        move = pltpu.make_async_copy(source, target, copied.at[14 + len(departures)])
        move.start()
        departures.append(move)

    for move in arrivals[1:4]:
        move.wait()
    level_one_again(
        pos, center, lower, upper, v1, f1, kx1, ky1, kyp1, kz1, kzp1, inverse1, stiff1, pen1, diagonal1, v01)
    arrivals[0].wait()
    coarse_levels(pos, gathered, e2out, nx, ny, work)
    gx, gy = pos[0], pos[1]
    ys = 4 * ny
    turn = lax.rem(ys - 4 * gy, ys)

    def rule(k, j):
        z = jnp.where((j & 127) < 96, j & 127, (j & 127) - BZ)
        return k == 64 * (j >> 7) + (z >> 1) + 16

    grow = matrix((BZ, LANES), rule)
    for c in range(3):
        for j in range(5):
            window[pl.ds((5 * c + j) * ys, ys), :] = times(pltpu.roll(e2out[c, gx + j], turn, 0), grow)
    for c in range(3):
        for s in range(2, 16):
            x2 = (s - 7) // 2
            j, part = (x2 + 4) // 2, (x2 + 4) % 2
            base = (5 * c + j) * ys
            cols = slice(128 * part, 128 * part + 128)
            if s % 2 == 1 or s == 2:
                low = window[base:base + 8, cols]
                high = window[base + ys - 4:base + ys, cols]
                for at in (0, 1):
                    rows24[pl.ds(at, 8, stride=2), :] = low
                    rows24[pl.ds(16 + at, 4, stride=2), :] = high
            va1[c, s] = v1[c, s] + jnp.where(inverse1[c, s] > 0.0, rows24[...], 0.0)
    faces1 = (kx1, ky1, kyp1, kz1, kzp1)

    def sweep1(source, target, weight, lower, upper):
        def step(s):
            for c in range(3):
                target[c, s] = (1.0 - weight) * source[c, s] + weight * inverse1[c, s] * (
                    f1[c, s] + neighbours(source, c, s, *faces1))

        loop(lower, upper, step)

    sweep1(va1, vb1, SECOND, 3, 15)
    sweep1(vb1, va1, FIRST, 4, 14)
    grow0 = matrix((BZ, LANES), lambda j, l: j == (l >> 1))
    for move in arrivals[4:]:
        move.wait()
    for c in range(3):
        spread[...] = times(va1[c, 4:14].reshape(240, BZ), grow0)
        for i in range(10):
            for half in (0, 1):
                cols = slice(BZ * half, BZ * half + BZ)
                value = spread[24 * i:24 * i + 24, cols]
                for at in (0, 1):
                    rows32[pl.ds(at, 12, stride=2), :] = value[:12]
                    rows32[pl.ds(24 + at, 4, stride=2), :] = value[20:]
                for s in (2 * i - 1, 2 * i):
                    if 0 <= s < 18:
                        va[c, s, :, cols] = va[c, s, :, cols] + rows32[...]
    faces = (kx, ky, kyp, kz, kzp)

    def sweep_one(t):
        for c in range(3):
            vb[c, t] = (1.0 - SECOND) * va[c, t + 1] + SECOND * inverse[c, t] * (
                start[c, t] + neighbours(va, c, t + 1, *faces, at=t))

    loop(0, 16, sweep_one)

    def sweep_two(t):
        for c in range(3):
            precond[c, t - 1] = (1.0 - FIRST) * vb[c, t] + FIRST * inverse[c, t] * (start[c, t] + neighbours(vb, c, t, *faces))

    loop(1, 15, sweep_two)

    def keep(x):
        for c in range(3):
            held[c, x] = precond[c, x + 3][:BY, :BZ]
            held[3 + c, x] = start[c, x + 4][:BY, :BZ]

    loop(0, BX, keep)
    send(held.at[0:6], parts.at[0:6])

    def inner(x, carry):
        one, two = carry
        for c in range(3):
            mid = held[c, x]
            value = mid / inverse[c, x + 4][:BY, :BZ] - neighbours(precond, c, x + 3, *faces, at=x + 4)[:BY, :BZ]
            held[6 + c, x] = value
            one = one + held[3 + c, x] * mid
            two = two + mid * value
        return one, two

    zero = jnp.zeros((BY, BZ), F32)
    one, two = lax.fori_loop(0, BX, inner, (zero, zero), unroll=4)
    send(held.at[6:9], parts.at[6:9])
    lane = iota((8, BZ), 1)
    sums[...] = jnp.where(lane == 0, jnp.sum(one), jnp.where(lane == 1, jnp.sum(two), 0.0))
    sensitivity(forward, precond, weights, term)

    def smooth(x):
        held[9, x] = weigh(term, x)

    loop(0, BX, smooth)
    send(held.at[9:10], parts.at[9:10])
    for move in departures:
        move.wait()


def distance_weight(square):
    return max(RADIUS - math.sqrt(square), 0.0)


def sensitivity(state, field, weights, term):
    def energy(i):
        s = i + 1
        total = jnp.zeros((ROWS, LANES), F32)
        for c in range(3):
            a, b = state[c, s], field[c, s]
            along = [(a - state[c, s - 1]) * (b - field[c, s - 1]) + (a - state[c, s + 1]) * (b - field[c, s + 1])]
            for axis in (0, 1):
                along.append(
                    (a - roll(a, 1, axis)) * (b - roll(b, 1, axis)) + (a - roll(a, -1, axis)) * (b - roll(b, -1, axis))
                )
            total = total + (along[0] + along[1] + along[2] + along[c])
        rho = weights[s]
        term[i] = rho * (-3.0 * rho * rho * (0.5 * total))

    loop(0, BX + 4, energy)


def weigh(field, x):
    classes = {}
    for a in range(-2, 3):
        t = field[x + 2 + a]
        for b, value in ((0, t), (1, roll(t, 1, 0) + roll(t, -1, 0)), (2, roll(t, 2, 0) + roll(t, -2, 0))):
            q = a * a + b * b
            classes[q] = value if q not in classes else classes[q] + value
    parts = []
    for z in (0, 1, 2):
        part = None
        for q, value in classes.items():
            w = distance_weight(q + z * z)
            if w > 0.0:
                part = w * value if part is None else part + w * value
        parts.append(part)
    result = parts[0] + roll(parts[1], 1, 1) + roll(parts[1], -1, 1) + roll(parts[2], 2, 1) + roll(parts[2], -2, 1)
    return result[:BY, :BZ]


def arrive(far, near, copied):
    moves = [pltpu.make_async_copy(source, target, copied.at[i]) for i, (source, target) in enumerate(zip(far, near))]
    for move in moves:
        move.start()
    for move in moves:
        move.wait()


def filter_iterate(pos, *rest):
    far, out, near, (term, inside, copied) = rest[:3], rest[3], rest[4:7], rest[7:]
    arrive(far, near, copied)
    iterate, state, weights = near
    sensitivity(state, iterate, weights, term)

    def mark(i):
        inside[i] = jnp.where(weights[i + 1] > 0.0, 1.0, 0.0)

    loop(0, BX + 4, mark)

    def smooth(x):
        factor = 1.0 / (weights[x + 3][:BY, :BZ] * weigh(inside, x))
        out[0, x] = factor * weigh(term, x)
        out[1, x] = factor

    loop(0, BX, smooth)


def finish(pos, totals, *rest):
    far, (solution, residual, filtered), near, copied = rest[:3], rest[3:6], rest[6:9], rest[9]
    moves = [pltpu.make_async_copy(source, target, copied.at[i]) for i, (source, target) in enumerate(zip(far, near))]
    for move in moves:
        move.start()
    iterate, parts, smooth = near
    total = jnp.sum(totals[...], axis=0, keepdims=True)
    lane = iota((1, BZ), 1)
    one = jnp.sum(jnp.where(lane == 0, total, 0.0), axis=1, keepdims=True)
    two = jnp.sum(jnp.where(lane == 1, total, 0.0), axis=1, keepdims=True)
    alpha = one / two
    for move in moves:
        move.wait()

    def update(x):
        for c in range(3):
            solution[c, x] = iterate[c, x] + alpha * parts[c, x]
            residual[c, x] = parts[3 + c, x] - alpha * parts[6 + c, x]
        filtered[x] = smooth[0, x] + alpha * (parts[9, x] * smooth[1, x])

    loop(0, BX, update)


def body(right_side, iterate, state, classes, load_mask, fixed_mask):
    nx, ny, nz = (lax.axis_size(axis) for axis in ("gx", "gy", "gz"))
    pos = jnp.stack([lax.axis_index("gx"), lax.axis_index("gy"), lax.axis_index("gz")]).astype(jnp.int32)
    pos = jnp.concatenate([pos, jnp.array([nx, ny, nz], jnp.int32)])
    cells = (BX, BY, BZ)
    field = (3,) + cells
    wide = (ROWS, LANES)

    def slabs(n):
        return (n,) + wide

    def fields(n):
        return (3, n) + wide

    main, last, first = launch(
        4, prepare, [(11,) + cells, cells, cells], [field], [pos],
        far=[right_side, iterate, state, classes, load_mask, fixed_mask], copies=6)
    from_lower, from_upper = shift_along(last, "gz", 1), shift_along(first, "gz", -1)
    edge = (12, BX, BY // 2, BZ)
    packed, to_upper, to_lower = launch(4, pack_rows, [cells, edge, edge], [], [pos, main, from_lower, from_upper])
    from_lower, from_upper = shift_along(to_upper, "gy", 1), shift_along(to_lower, "gy", -1)
    sides = (SENT, ROWS, BZ)
    own, to_upper, to_lower = launch(
        14, pack_slabs, [(12, BX, ROWS, BZ), sides, sides],
        [slabs(BX)] * 3 + [fields(BX)] * 2 + [slabs(BX)] * 5 + [fields(BX)], [pos, main, packed, from_lower, from_upper])
    from_lower, from_upper = shift_along(to_upper, "gx", 1), shift_along(to_lower, "gx", -1)

    one, three = slabs(SLABS), fields(SLABS)
    quarters = (22, 8, BZ)
    coarse, low, high, v1, start, kx, ky, kyp, kz, kzp, inverse, u, weights, forward = launch(
        24, descend, [(44, 16, BZ), quarters, quarters],
        [three, three, one, one, one, one, one, three, three, one, fields(14), one, one, three, three, (ROWS, BZ), (44 * 16, BZ)],
        [pos, own, from_lower, from_upper],
        far_outs=[fields(18), fields(16), slabs(17)] + [slabs(16)] * 4 + [fields(16), fields(14), slabs(14), fields(14)],
        copies=11)
    smooth = launch(
        10, filter_iterate, [(2,) + cells], [fields(14), fields(14), slabs(14), slabs(12), slabs(12)], [pos],
        far=[u, forward, weights], copies=3,
        cost=pl.CostEstimate(flops=12_000_000, bytes_accessed=4_000_000, transcendentals=0))[0]

    from_lower, from_upper = shift_along(high, "gz", 1), shift_along(low, "gz", -1)
    coarse, center = launch(4, join_lanes, [(44, 16, BZ), (44, 8, BZ)], [], [pos, coarse, from_lower, from_upper])
    from_lower, from_upper = shift_along(center, "gy", 1), shift_along(center, "gy", -1)
    wide1 = (16, BZ)
    one1, three1 = (10,) + wide1, (3, 10) + wide1
    chunk = launch(
        4, level_one, [(ny, 24, BZ)], [one1] * 5 + [three1] * 5 + [(8, BZ), (40, BZ), (40, BZ)], [pos, coarse])[0]
    side = (32, 24, BZ)
    column = lax.all_to_all(chunk, "gy", 0, 0, tiled=True)
    to_upper, to_lower, center = launch(
        4, join_rows, [side, side], [(44, 24, BZ)], [pos, center, from_lower, from_upper],
        far_outs=[(44, 24, BZ)], copies=1)
    column = launch(8, pack_column, [(nx, 20 * ny, BZ)], [], [pos, column])[0]
    gathered = lax.all_to_all(column, "gx", 0, 0, tiled=True)
    from_lower, from_upper = shift_along(to_upper, "gx", 1), shift_along(to_lower, "gx", -1)

    wide1 = (24, BZ)
    one1, three1 = (18,) + wide1, (3, 18) + wide1
    wide2, wide3 = (4 * ny, BZ), (2 * ny, BZ)
    one2, three2 = (nx + 2,) + wide2, (3, nx + 2) + wide2
    one3, three3 = (nx + 2,) + wide3, (3, nx + 2) + wide3
    work = [one2, one2, three2] + [one2] * 6 + [three2] * 4 + [wide2, (5 * nx * 2 * ny, BZ)]
    work += [one3, one3, three3] + [one3] * 5 + [three3] * 3 + [(nx * 2 * ny, BZ)]
    parts = (10,) + cells
    far = [gathered, center, from_lower, from_upper, v1, start, kx, ky, kyp, kz, kzp, inverse, forward, weights]
    scratch = [x.shape for x in far] + [
        (3, nx + 4) + wide2, (15 * 4 * ny, LANES), wide1, three1, three1, (ROWS, BZ), (240, LANES), fields(16), fields(14), slabs(12), parts
    ] + [three1] * 2 + [one1] * 5 + [three1, one1, one1, three1, three1] + work
    sums, parts = launch(
        30, functools.partial(ascend, nx=nx, ny=ny), [(8, BZ)], scratch, [pos], far_outs=[parts], far=far + [smooth], copies=17)

    total = lax.all_to_all(jnp.broadcast_to(sums[:1], (nx * ny, BZ)), ("gx", "gy"), 0, 0, tiled=True)
    total = jnp.sum(total, axis=0, keepdims=True)
    total = lax.all_to_all(jnp.broadcast_to(total, (nz, BZ)), "gz", 0, 0, tiled=True)
    return tuple(launch(
        4, finish, [field, field, cells], [field, parts.shape, smooth.shape], [pos, total],
        far=[iterate, parts, smooth], copies=3))


def solution(mesh):
    field, cells = P(None, "gx", "gy", "gz"), P("gx", "gy", "gz")
    return jax.shard_map(
        body,
        mesh=mesh,
        in_specs=(field, field, field, cells, cells, cells),
        out_specs=(field, field, cells),
        check_vma=False,
    )
```

```python
import functools
import math

import jax
import jax.numpy as jnp
from jax import lax
from jax.experimental import pallas as pl
from jax.experimental.pallas import tpu as pltpu
from jax.sharding import PartitionSpec as P

F32 = jnp.float32
FLOOR = 0.25
CLASSES = 16
PENALTY = 4.0
FIRST = 0.55
SECOND = 1.05
COARSE = 0.6
RADIUS = 3

BX, BY, BZ = 8, 16, 128
HALO = 7
SLABS = BX + 2 * HALO
ROWS = 2 * BY
LANES = 2 * BZ

PACKED = 8
ITERATE = ((0, 0, 7), (1, 7, 7), (2, 14, 7))
RHO = (3, 21, 7)
LOAD = ((4, 28, 6), (5, 34, 6), (6, 40, 6))
PEN = (7, 46, 6)
STATE = ((9, 52, 3), (10, 55, 3), (11, 58, 3))
FIELDS = ITERATE + (RHO,) + LOAD + (PEN,) + STATE
HALF = BZ // 2

MIB = 1024 * 1024


def iota(shape, dim):
    return lax.broadcasted_iota(jnp.int32, shape, dim)


def roll(x, shift, axis):
    return pltpu.roll(x, shift % x.shape[axis], axis)


def loop(lower, upper, step, unroll=4):
    def run(i, carry):
        step(i)
        return carry

    lax.fori_loop(lower, upper, run, 0, unroll=unroll)


def times(x, m):
    m = m.astype(jnp.bfloat16)
    high = x.astype(jnp.bfloat16)
    low = (x - high.astype(F32)).astype(jnp.bfloat16)
    return jnp.dot(high, m, preferred_element_type=F32) + jnp.dot(low, m, preferred_element_type=F32)


def matrix(shape, rule):
    return jnp.where(rule(iota(shape, 0), iota(shape, 1)), 1.0, 0.0).astype(F32)


def face(a, b):
    total = a + b
    both = (a > 0.0) & (b > 0.0)
    return jnp.where(both, 2.0 * a * b / jnp.where(both, total, 1.0), total)


def launch(limit, kernel, outs, scratch, operands, far_outs=(), far=(), copies=0, cost=None, pin=False):
    near_spec, far_spec = pl.BlockSpec(memory_space=pltpu.VMEM), pl.BlockSpec(memory_space=pltpu.HBM)
    specs = [pl.BlockSpec(memory_space=pltpu.SMEM)] + [near_spec] * (len(operands) - 1) + [far_spec] * len(far)
    return pl.pallas_call(
        kernel,
        out_shape=[pltpu.VMEM(shape, F32) if pin else jax.ShapeDtypeStruct(shape, F32) for shape in outs] + [pltpu.HBM(shape, F32) for shape in far_outs],
        in_specs=specs,
        out_specs=[near_spec] * len(outs) + [far_spec] * len(far_outs),
        scratch_shapes=[pltpu.VMEM(shape, F32) for shape in scratch] + ([pltpu.SemaphoreType.DMA((copies,))] if copies else []),
        compiler_params=pltpu.CompilerParams(vmem_limit_bytes=limit * MIB),
        cost_estimate=cost,
    )(*(operands[:1] + [pltpu.with_memory_space_constraint(x, pltpu.VMEM) for x in operands[1:]] if pin else operands), *[pltpu.with_memory_space_constraint(x, pltpu.HBM) for x in far])


def shift_along(x, axis, step):
    devices = lax.axis_size(axis)
    return lax.ppermute(x, axis, [(i, (i + step) % devices) for i in range(devices)])


def prepare(pos, right_far, iterate_far, state_far, classes_far, load_far, fixed_far, main, to_upper, to_lower, right, copied):
    def rest(classes, load_mask, fixed_mask):
        moves = [
            pltpu.make_async_copy(source, target, copied.at[i])
            for i, (source, target) in enumerate((
                (classes_far, classes), (load_far, load_mask), (fixed_far, fixed_mask), (right_far, right),
                (iterate_far, main.at[0:3]), (state_far, main.at[8:11])))
        ]
        for move in moves:
            move.start()
        for move in moves:
            move.wait()
        lane = iota((BY, BZ), 1)

        def slab(x):
            mask = load_mask[x].astype(F32)
            main[3, x] = FLOOR + (1.0 - FLOOR) * classes[x].astype(F32) / (CLASSES - 1)
            main[7, x] = PENALTY * fixed_mask[x].astype(F32)
            for c in range(3):
                main[4 + c, x] = right[c, x] * mask
            last = jnp.zeros((BY, BZ), F32)
            first = jnp.zeros((BY, BZ), F32)
            for tile, offset, width in FIELDS:
                value = main[tile if tile < PACKED else tile - 1, x]
                last = jnp.where((lane >= offset) & (lane < offset + width), roll(value, offset + width, 1), last)
                low = HALF + offset
                first = jnp.where((lane >= low) & (lane < low + width), roll(value, low, 1), first)
            to_upper[x] = last
            to_lower[x] = first

        loop(0, BX, slab)

    cells = pltpu.VMEM((BX, BY, BZ), jnp.int32)
    pl.run_scoped(rest, cells, cells, cells)


def pack_rows(pos, main, from_lower, from_upper, packed, to_upper, to_lower):
    below = jnp.where(pos[2] > 0, 1.0, 0.0)
    above = jnp.where(pos[2] < pos[5] - 1, 1.0, 0.0)
    lane = iota((BY, BZ), 1)
    half = BY // 2

    def slab(x):
        joined = jnp.where(lane < HALF, from_lower[x] * below, from_upper[x] * above)
        packed[x] = joined
        for tile in range(12):
            value = joined if tile == PACKED else main[tile if tile < PACKED else tile - 1, x]
            to_upper[tile, x] = value[half:]
            to_lower[tile, x] = value[:half]

    loop(0, BX, slab)


def neighbours(field, c, s, kx, ky, kz, at=None):
    at = s if at is None else at
    v = field[c, s]
    x = kx[at] * field[c, s - 1] + kx[at + 1] * field[c, s + 1]
    y = ky[at] * roll(v, 1, 0) + roll(ky[at] * v, -1, 0)
    z = kz[at] * roll(v, 1, 1) + roll(kz[at] * v, -1, 1)
    return x + y + z + (x, y, z)[c]


def coefficients(stiff, pen, s, scale, kx, ky, kz, inverse, diagonal):
    e = stiff[s]
    upper = scale * face(e, stiff[s + 1])
    kx[s + 1] = upper
    y = scale * face(e, roll(e, 1, 0))
    ky[s] = y
    yp = roll(y, -1, 0)
    z = scale * face(e, roll(e, 1, 1))
    kz[s] = z
    zp = roll(z, -1, 1)
    pairs = (kx[s] + upper, y + yp, z + zp)
    total = pairs[0] + pairs[1] + pairs[2] + pen[s]
    for c in range(3):
        value = total + pairs[c]
        diagonal[c, s] = value
        if inverse is not None:
            inverse[c, s] = jnp.where(e > 0.0, 1.0 / jnp.where(e > 0.0, value, 1.0), 0.0)


def spread(value, packed, field, ref, at):
    _, offset, width = field
    lane = iota((ROWS, BZ), 1)
    ref[at + (slice(None), slice(0, BZ))] = value
    tail = jnp.where(lane >= BZ - width, roll(packed, BZ - width - offset, 1), 0.0)
    tail = jnp.where(lane < width, roll(packed, -(HALF + offset), 1), tail)
    ref[at + (slice(None), slice(BZ, LANES))] = tail


LAYERS = ((RHO[0], 7), (PACKED, 7)) + tuple((f[0], 6) for f in LOAD + (PEN,)) + tuple((f[0], 3) for f in ITERATE + STATE)
PLACE = {}
SENT = 0
for _tile, _count in LAYERS:
    PLACE[_tile] = SENT
    SENT += _count


def pack_slabs(pos, main, packed, from_lower, from_upper, own, to_upper, to_lower,
               rho, stiff, pen, u, load, kx, ky, kz, diagonal):
    below = jnp.where(pos[1] > 0, 1.0, 0.0)
    above = jnp.where(pos[1] < pos[4] - 1, 1.0, 0.0)

    def slab(x):
        for tile in range(12):
            value = packed[x] if tile == PACKED else main[tile if tile < PACKED else tile - 1, x]
            own[tile, x] = jnp.concatenate([value, from_upper[tile, x] * above, from_lower[tile, x] * below], 0)

    loop(0, BX, slab)

    def expand(x):
        halo = own[PACKED, x]
        spread(own[RHO[0], x], halo, RHO, rho, (x,))
        spread(own[PEN[0], x], halo, PEN, pen, (x,))
        for c in range(3):
            spread(own[ITERATE[c][0], x], halo, ITERATE[c], u, (c, x))
            spread(own[LOAD[c][0], x], halo, LOAD[c], load, (c, x))
        stiff[x] = rho[x] * rho[x] * rho[x]

    loop(0, BX, expand)
    kx[1] = face(stiff[0], stiff[1])
    loop(1, BX - 1, lambda x: coefficients(stiff, pen, x, 1.0, kx, ky, kz, None, diagonal))
    lane = iota((ROWS, BZ), 1)

    def begin(x):
        halo = own[PACKED, x]
        for c in range(3):
            f = load[c, x] - (diagonal[c, x] * u[c, x] - neighbours(u, c, x, kx, ky, kz))
            tile, offset, width = LOAD[c]
            own[tile, x] = f[:, :BZ]
            tail = f[:, BZ:]
            halo = jnp.where((lane >= offset) & (lane < offset + width), roll(tail, offset + width, 1), halo)
            low = HALF + offset
            halo = jnp.where((lane >= low) & (lane < low + width), roll(tail, low, 1), halo)
        own[PACKED, x] = halo

    loop(1, BX - 1, begin)
    for tile, count in LAYERS:
        for j in range(count):
            to_upper[PLACE[tile] + j] = own[tile, BX - count + j]
            to_lower[PLACE[tile] + j] = own[tile, j]


def descend(pos, own, lower, upper, coarse, low_lanes, high_lanes, *rest):
    far, rest = rest[:9], rest[9:]
    (v1, start, kx, ky, kz, inverse, u, weights, forward, stiff, pen, diagonal, v0, half_rows, rows, copied) = rest
    moves = []

    def send(*pairs):
        for source, target in pairs:
            move = pltpu.make_async_copy(source, far[target], copied.at[target])
            move.start()
            moves.append(move)

    below = jnp.where(pos[0] > 0, 1.0, 0.0)
    above = jnp.where(pos[0] < pos[3] - 1, 1.0, 0.0)

    def expand(raw, s, fields):
        halo = raw(PACKED)
        for field, ref, at in fields:
            spread(raw(field[0]), halo, field, ref, at)

    def densities(s):
        return [(RHO, weights, (s,))]

    def loads(s):
        return [(PEN, pen, (s,))] + [(LOAD[c], start, (c, s)) for c in range(3)]

    def motions(s):
        return [(ITERATE[c], u, (c, s)) for c in range(3)] + [(STATE[c], forward, (c, s - 4)) for c in range(3)]

    def lower_raw(s):
        return lambda t: lower[PLACE[t] + s - (HALO - dict(LAYERS)[t])] * below

    def upper_raw(s):
        return lambda t: upper[PLACE[t] + s - (HALO + BX)] * above

    after = HALO + BX
    loop(0, HALO, lambda s: expand(lower_raw(s), s, densities(s)))
    loop(1, HALO, lambda s: expand(lower_raw(s), s, loads(s)))
    loop(4, HALO, lambda s: expand(lower_raw(s), s, motions(s)))
    loop(HALO, after, lambda s: expand(lambda t: own[t, s - HALO], s, densities(s) + loads(s) + motions(s)))
    loop(after, after + 7, lambda s: expand(upper_raw(s), s, densities(s)))
    loop(after, after + 6, lambda s: expand(upper_raw(s), s, loads(s)))
    loop(after, after + 3, lambda s: expand(upper_raw(s), s, motions(s)))
    send((u.at[:, 4:18], 6), (weights.at[4:18], 7), (forward, 8))

    def cube(s):
        rho = weights[s]
        stiff[s] = rho * rho * rho

    loop(0, SLABS, cube)
    kx[1] = face(stiff[0], stiff[1])
    loop(1, SLABS - 1, lambda s: coefficients(stiff, pen, s, 1.0, kx, ky, kz, inverse, diagonal))
    faces = (kx, ky, kz)
    send((kx.at[3:20], 2), (ky.at[3:19], 3), (kz.at[3:19], 4), (inverse.at[:, 3:19], 5))

    for s in (HALO - 1, HALO, HALO + BX - 1, HALO + BX):
        for c in range(3):
            start[c, s] = start[c, s] - (diagonal[c, s] * u[c, s] - neighbours(u, c, s, *faces))

    def begin(s):
        for c in range(3):
            v0[c, s] = FIRST * start[c, s] * inverse[c, s]

    loop(1, SLABS - 1, begin)
    send((start.at[:, 3:19], 1))

    def sweep(s):
        for c in range(3):
            v1[c, s] = (1.0 - SECOND) * v0[c, s] + SECOND * inverse[c, s] * (start[c, s] + neighbours(v0, c, s, *faces))

    loop(2, SLABS - 2, sweep)
    send((v1.at[:, 2:20], 0))

    def remainder(c, s):
        r = start[c, s] - diagonal[c, s] * v1[c, s] + neighbours(v1, c, s, *faces)
        return r[:, :BZ]

    def gather_rows(at, value):
        half_rows[...] = value
        n = ROWS // 2
        rows[pl.ds(pl.multiple_of(at * n, n), n), :] = half_rows[pl.ds(0, n, stride=2), :] + half_rows[pl.ds(1, n, stride=2), :]

    def pair(i):
        for c in range(3):
            gather_rows(c * 8 + i, remainder(c, 3 + 2 * i) + remainder(c, 4 + 2 * i))

    loop(0, 8, pair)

    def pair_up(i):
        s = 1 + 2 * i
        gather_rows(24 + i, (stiff[s] + stiff[s + 1])[:, :BZ] * 0.125)
        gather_rows(34 + i, (pen[s] + pen[s + 1])[:, :BZ])

    loop(0, 10, pair_up)
    halve = matrix((BZ, BZ), lambda l, k: (l >> 1) == (k & (HALF - 1)))
    coarse[...] = times(rows[...], halve).reshape(44, 16, BZ)
    quarter = iota((8, BZ), 1) >> 5

    def pack(g):
        for h in range(2):
            low = jnp.zeros((8, BZ), F32)
            high = jnp.zeros((8, BZ), F32)
            for q in range(4):
                value = coarse[4 * g + q, 8 * h:8 * h + 8]
                turned = roll(value, 32, 1)
                one, two = (value, turned) if q % 2 == 0 else (turned, value)
                low = jnp.where(quarter == q, one, low)
                high = jnp.where(quarter == q, two, high)
            low_lanes[2 * g + h] = low
            high_lanes[2 * g + h] = high

    loop(0, 11, pack)
    for move in moves:
        move.wait()


def join_lanes(pos, coarse, from_lower, from_upper, out, center):
    below = jnp.where(pos[2] > 0, 1.0, 0.0)
    above = jnp.where(pos[2] < pos[5] - 1, 1.0, 0.0)
    lane = iota((8, BZ), 1)

    def unpack(g):
        for h in range(2):
            low, high = from_lower[2 * g + h] * below, from_upper[2 * g + h] * above
            for q in range(4):
                halo = jnp.where(lane < 96, roll(high, 64 - 32 * q, 1), roll(low, 96 - 32 * q, 1))
                value = jnp.where(lane < 64, coarse[4 * g + q, 8 * h:8 * h + 8], halo)
                out[4 * g + q, 8 * h:8 * h + 8] = value
                if h == 0:
                    center[4 * g + q] = value

    loop(0, 11, unpack)


def join_rows(pos, coarse, from_lower, from_upper, to_upper, to_lower, center, out, copied):
    below = jnp.where(pos[1] > 0, 1.0, 0.0)
    above = jnp.where(pos[1] < pos[4] - 1, 1.0, 0.0)

    def join(i):
        out[i] = jnp.concatenate([coarse[i], from_upper[i] * above, from_lower[i] * below], 0)

    loop(0, 44, join)
    move = pltpu.make_async_copy(out, center, copied.at[0])
    move.start()
    at = 0
    for base, count in ((0, 6), (8, 6), (16, 6), (24, 7), (34, 7)):
        shift = 2 if count == 6 else 3
        for j in range(count):
            to_upper[at] = out[base + j]
            to_lower[at] = out[base + shift + j]
            at += 1
    move.wait()


def smooth_down(slabs, f, v0, v1, inverse, faces):
    def begin(s):
        for c in range(3):
            v0[c, s] = FIRST * f[c, s] * inverse[c, s]

    loop(1, slabs - 1, begin)

    def sweep(s):
        for c in range(3):
            v1[c, s] = (1.0 - SECOND) * v0[c, s] + SECOND * inverse[c, s] * (f[c, s] + neighbours(v0, c, s, *faces))

    loop(2, slabs - 2, sweep)


def level_one(pos, own, chunk, kx, ky, kz, inverse, diagonal, f, v0, v1, half_rows, rows, wide):
    stiff, pen = own.at[24:34], own.at[34:44]
    slabs = 10
    for c in range(3):
        for i in range(8):
            f[c, 1 + i] = own[8 * c + i]
    kx[1] = 2.0 * face(stiff[0], stiff[1])
    loop(1, slabs - 1, lambda s: coefficients(stiff, pen, s, 2.0, kx, ky, kz, inverse, diagonal))
    faces = (kx, ky, kz)
    smooth_down(slabs, f, v0, v1, inverse, faces)

    def gather_rows(at, value):
        half_rows[...] = value
        rows[pl.ds(at * 4, 4), :] = half_rows[pl.ds(0, 4, stride=2), :] + half_rows[pl.ds(1, 4, stride=2), :]

    for i in range(2):
        s = 3 + 2 * i
        for c in range(3):
            total = 0.0
            for at in (s, s + 1):
                total = total + (f[c, at] - diagonal[c, at] * v1[c, at] + neighbours(v1, c, at, *faces))[:8]
            gather_rows(2 * c + i, total)
        gather_rows(6 + i, (stiff[s] + stiff[s + 1])[:8] * 0.125)
        gather_rows(8 + i, (pen[s] + pen[s + 1])[:8])

    def rule(j, k):
        z = jnp.where(j < 96, j, j - BZ)
        return (z >> 1) == (k & 63) - 16

    wide[...] = times(rows[...], matrix((BZ, BZ), rule))
    lane = iota((4, BZ), 1)
    parts = [jnp.where(lane < 64, wide[8 * field:8 * field + 4], wide[8 * field + 4:8 * field + 8]) for field in range(5)]
    value = jnp.concatenate(parts + [jnp.zeros((4, BZ), F32)], 0)
    for i in range(chunk.shape[0]):
        chunk[i] = value


def pack_column(pos, column, out):
    for i in range(out.shape[0]):
        for j in range(column.shape[0]):
            out[i, 20 * j:20 * j + 20] = column[j, 0:20]


def level_one_again(pos, own, lower, upper, v1, f, kx, ky, kz, inverse, stiff, pen, diagonal, v0):
    below = jnp.where(pos[0] > 0, 1.0, 0.0)
    above = jnp.where(pos[0] < pos[3] - 1, 1.0, 0.0)
    slabs = 18
    for field, at in ((stiff, 0), (pen, 1)):
        for j in range(7):
            field[j] = lower[18 + 7 * at + j] * below
            field[11 + j] = upper[18 + 7 * at + j] * above
        for j in range(4):
            field[7 + j] = own[24 + 10 * at + 3 + j]
    for c in range(3):
        for j in range(6):
            f[c, 1 + j] = lower[6 * c + j] * below
            f[c, 11 + j] = upper[6 * c + j] * above
        for j in range(4):
            f[c, 7 + j] = own[8 * c + 2 + j]
    kx[1] = 2.0 * face(stiff[0], stiff[1])
    loop(1, slabs - 1, lambda s: coefficients(stiff, pen, s, 2.0, kx, ky, kz, inverse, diagonal))
    smooth_down(slabs, f, v0, v1, inverse, (kx, ky, kz))


def coarse_levels(pos, gathered, out, nx, ny, work):
    (e2, p2, f2, kxm, kxp, kym, kzm, iv, dg, va, vb, tall, rows3, e3, p3, f3, jx, jym, jz, iv3, wa, wb, rows2) = work
    ys = 4 * ny
    pairs = nx
    lane = iota((ys, BZ), 1)
    row = iota((ys, BZ), 0)
    even = lane < 64
    zero = jnp.zeros((ys, BZ), F32)
    for field in (e2, p2):
        field[0] = zero
        field[pairs + 1] = zero
    for c in range(3):
        for field in (va, vb):
            field[c, 0] = zero
            field[c, pairs + 1] = zero

    def collect(g):
        for field in range(5):
            for yy in range(ny):
                value = gathered[g, 20 * yy + 4 * field:20 * yy + 4 * field + 4, :]
                if field < 3:
                    f2[field, g + 1, pl.ds(4 * yy, 4), :] = value
                else:
                    (e2, p2)[field - 3][g + 1, pl.ds(4 * yy, 4), :] = value

    loop(0, pairs, collect)

    def x_neighbours(below, mid, above):
        swapped = roll(mid, 64, 1)
        return jnp.where(even, roll(below, 64, 1), swapped), jnp.where(even, swapped, roll(above, 64, 1))

    def coefs(s):
        e = e2[s]
        xm, xp = x_neighbours(e2[s - 1], e, e2[s + 1])
        ym = jnp.where(row == 0, 0.0, roll(e, 1, 0))
        yp = jnp.where(row == ys - 1, 0.0, roll(e, -1, 0))
        a, b = 4.0 * face(e, xm), 4.0 * face(e, xp)
        c0, d = 4.0 * face(e, ym), 4.0 * face(e, yp)
        z = 4.0 * face(e, roll(e, 1, 1))
        zp = roll(z, -1, 1)
        kxm[s] = a
        kxp[s] = b
        kym[s] = jnp.where(row == 0, 0.0, c0)
        kzm[s] = z
        sums = (a + b, c0 + d, z + zp)
        total = sums[0] + sums[1] + sums[2] + p2[s]
        for c in range(3):
            value = total + sums[c]
            dg[c, s] = value
            iv[c, s] = jnp.where(e > 0.0, 1.0 / jnp.where(e > 0.0, value, 1.0), 0.0)
            va[c, s] = FIRST * f2[c, s] * iv[c, s]

    loop(1, pairs + 1, coefs)

    def around(v, c, s):
        mid = v[c, s]
        below, above = x_neighbours(v[c, s - 1], mid, v[c, s + 1])
        x = kxm[s] * below + kxp[s] * above
        y = kym[s] * roll(mid, 1, 0) + roll(kym[s] * mid, -1, 0)
        z = kzm[s] * roll(mid, 1, 1) + roll(kzm[s] * mid, -1, 1)
        return x + y + z + (x, y, z)[c]

    def sweep(source, target, weight):
        def step(s):
            for c in range(3):
                target[c, s] = (1.0 - weight) * source[c, s] + weight * iv[c, s] * (f2[c, s] + around(source, c, s))

        loop(1, pairs + 1, step)

    sweep(va, vb, SECOND)
    n3 = ys // 2

    def gather_rows(at, value):
        tall[...] = value
        rows3[pl.ds(pl.multiple_of(at * n3, 8), n3), :] = tall[pl.ds(0, n3, stride=2), :] + tall[pl.ds(1, n3, stride=2), :]

    def reduce(s):
        for c in range(3):
            gather_rows(c * pairs + s - 1, f2[c, s] - dg[c, s] * vb[c, s] + around(vb, c, s))
        gather_rows(3 * pairs + s - 1, e2[s] * 0.125)
        gather_rows(4 * pairs + s - 1, p2[s])

    loop(1, pairs + 1, reduce)
    down = matrix((BZ, BZ), lambda l, k: ((l & 63) >> 1) == (k & 31))
    rows3[...] = times(rows3[...], down)
    row3 = iota((n3, BZ), 0)
    zero3 = jnp.zeros((n3, BZ), F32)

    def third(at):
        return rows3[pl.ds(pl.multiple_of(at * n3, 8), n3), :]

    e3[0] = zero3
    e3[pairs + 1] = zero3
    for c in range(3):
        for field in (wa, wb):
            field[c, 0] = zero3
            field[c, pairs + 1] = zero3

    def place(s):
        e3[s] = third(3 * pairs + s - 1)

    loop(1, pairs + 1, place)

    def coefs3(s):
        e = e3[s]
        a, b = 8.0 * face(e, e3[s - 1]), 8.0 * face(e, e3[s + 1])
        c0 = 8.0 * face(e, jnp.where(row3 == 0, 0.0, roll(e, 1, 0)))
        d = 8.0 * face(e, jnp.where(row3 == n3 - 1, 0.0, roll(e, -1, 0)))
        z = 8.0 * face(e, roll(e, 1, 1))
        zp = roll(z, -1, 1)
        jx[s] = a
        jx[s + 1] = b
        jym[s] = jnp.where(row3 == 0, 0.0, c0)
        jz[s] = z
        sums = (a + b, c0 + d, z + zp)
        total = sums[0] + sums[1] + sums[2] + third(4 * pairs + s - 1)
        for c in range(3):
            value = total + sums[c]
            iv3[c, s] = jnp.where(e > 0.0, 1.0 / jnp.where(e > 0.0, value, 1.0), 0.0)
            wa[c, s] = COARSE * third(c * pairs + s - 1) * iv3[c, s]

    loop(1, pairs + 1, coefs3)
    source, target = wa, wb
    for sweep_at in range(3):
        def step(s, source=source, target=target):
            for c in range(3):
                near = neighbours(source, c, s, jx, jym, jz)
                target[c, s] = (1.0 - COARSE) * source[c, s] + COARSE * iv3[c, s] * (third(c * pairs + s - 1) + near)

        loop(1, pairs + 1, step)
        source, target = target, source
    up = matrix((BZ, BZ), lambda k, l: k == ((l & 63) >> 1))
    for c in range(3):
        rows2[...] = times(source[c, 1:pairs + 1].reshape(pairs * n3, BZ), up)

        def add(s, c=c):
            value = rows2[pl.ds(pl.multiple_of((s - 1) * n3, 8), n3), :]
            tall[pl.ds(0, n3, stride=2), :] = value
            tall[pl.ds(1, n3, stride=2), :] = value
            vb[c, s] = vb[c, s] + jnp.where(iv[c, s] > 0.0, tall[...], 0.0)

        loop(1, pairs + 1, add)
    sweep(vb, va, SECOND)

    for c in range(3):
        for at in (0, 1, pairs + 2, pairs + 3):
            out[c, at] = zero

    def last(s):
        for c in range(3):
            out[c, s + 1] = (1.0 - FIRST) * va[c, s] + FIRST * iv[c, s] * (f2[c, s] + around(va, c, s))

    loop(1, pairs + 1, last)


def ascend(pos, lower, upper, *rest, nx, ny):
    far, (sums, parts, precond_far), rest = rest[:8], rest[9:12], rest[12:]
    near, rest = rest[:8], rest[8:]
    e2out, window, rows24, va1, vb1, rows32, spread, vb, precond, held = rest[:10]
    v1, f1, kx1, ky1, kz1, inverse1, stiff1, pen1, diagonal1, v01 = rest[10:20]
    work, copied = rest[20:-1], rest[-1]
    gathered, center = near[:2]
    va, start, kx, ky, kz, inverse = near[2:]
    arrivals = [pltpu.make_async_copy(source, target, copied.at[i]) for i, (source, target) in enumerate(zip(far, near))]
    for i in (1, 0):
        arrivals[i].start()
    departures = []

    def send(source, target):
        move = pltpu.make_async_copy(source, target, copied.at[8 + len(departures)])
        move.start()
        departures.append(move)

    arrivals[1].wait()
    for move in arrivals[2:]:
        move.start()
    level_one_again(
        pos, center, lower, upper, v1, f1, kx1, ky1, kz1, inverse1, stiff1, pen1, diagonal1, v01)
    arrivals[0].wait()
    coarse_levels(pos, gathered, e2out, nx, ny, work)
    gx, gy = pos[0], pos[1]
    ys = 4 * ny
    turn = lax.rem(ys - 4 * gy, ys)

    def rule(k, j):
        z = jnp.where((j & 127) < 96, j & 127, (j & 127) - BZ)
        return k == 64 * (j >> 7) + (z >> 1) + 16

    grow = matrix((BZ, LANES), rule)
    for c in range(3):
        for j in range(5):
            window[pl.ds((5 * c + j) * ys, ys), :] = times(pltpu.roll(e2out[c, gx + j], turn, 0), grow)
    for c in range(3):
        for s in range(2, 16):
            x2 = (s - 7) // 2
            j, part = (x2 + 4) // 2, (x2 + 4) % 2
            base = (5 * c + j) * ys
            cols = slice(128 * part, 128 * part + 128)
            if s % 2 == 1 or s == 2:
                low = window[base:base + 8, cols]
                high = window[base + ys - 4:base + ys, cols]
                for at in (0, 1):
                    rows24[pl.ds(at, 8, stride=2), :] = low
                    rows24[pl.ds(16 + at, 4, stride=2), :] = high
            va1[c, s] = v1[c, s] + jnp.where(inverse1[c, s] > 0.0, rows24[...], 0.0)
    faces1 = (kx1, ky1, kz1)

    def sweep1(source, target, weight, lower, upper):
        def step(s):
            for c in range(3):
                target[c, s] = (1.0 - weight) * source[c, s] + weight * inverse1[c, s] * (
                    f1[c, s] + neighbours(source, c, s, *faces1))

        loop(lower, upper, step)

    sweep1(va1, vb1, SECOND, 3, 15)
    sweep1(vb1, va1, FIRST, 4, 14)
    grow0 = matrix((BZ, LANES), lambda j, l: j == (l >> 1))
    for move in arrivals[2:]:
        move.wait()
    for c in range(3):
        spread[...] = times(va1[c, 4:14].reshape(240, BZ), grow0)
        for i in range(10):
            for half in (0, 1):
                cols = slice(BZ * half, BZ * half + BZ)
                value = spread[24 * i:24 * i + 24, cols]
                for at in (0, 1):
                    rows32[pl.ds(at, 12, stride=2), :] = value[:12]
                    rows32[pl.ds(24 + at, 4, stride=2), :] = value[20:]
                for s in (2 * i - 1, 2 * i):
                    if 0 <= s < 18:
                        va[c, s, :, cols] = va[c, s, :, cols] + rows32[...]
    faces = (kx, ky, kz)

    def sweep_one(t):
        for c in range(3):
            vb[c, t] = (1.0 - SECOND) * va[c, t + 1] + SECOND * inverse[c, t] * (
                start[c, t] + neighbours(va, c, t + 1, *faces, at=t))

    loop(0, 16, sweep_one)

    def sweep_two(t):
        for c in range(3):
            precond[c, t - 1] = (1.0 - FIRST) * vb[c, t] + FIRST * inverse[c, t] * (start[c, t] + neighbours(vb, c, t, *faces))

    loop(1, 15, sweep_two)

    def keep(x):
        for c in range(3):
            held[c, x] = precond[c, x + 3][:BY, :BZ]
            held[3 + c, x] = start[c, x + 4][:BY, :BZ]

    loop(0, BX, keep)
    send(held.at[0:6], parts.at[0:6])
    send(precond, precond_far)

    def inner(x, carry):
        one, two = carry
        for c in range(3):
            mid = held[c, x]
            value = mid / inverse[c, x + 4][:BY, :BZ] - neighbours(precond, c, x + 3, *faces, at=x + 4)[:BY, :BZ]
            held[6 + c, x] = value
            one = one + held[3 + c, x] * mid
            two = two + mid * value
        return one, two

    zero = jnp.zeros((BY, BZ), F32)
    one, two = lax.fori_loop(0, BX, inner, (zero, zero), unroll=4)
    send(held.at[6:9], parts.at[6:9])
    lane = iota((8, BZ), 1)
    sums[...] = jnp.where(lane == 0, jnp.sum(one), jnp.where(lane == 1, jnp.sum(two), 0.0))
    for move in departures:
        move.wait()


def distance_weight(square):
    return max(RADIUS - math.sqrt(square), 0.0)


def sensitivity(state, field, weights, term):
    def energy(i):
        s = i + 1
        total = jnp.zeros((ROWS, LANES), F32)
        sums = [0.0, 0.0]
        for c in range(3):
            a, b = state[c, s], field[c, s]
            x = (a - state[c, s - 1]) * (b - field[c, s - 1]) + (a - state[c, s + 1]) * (b - field[c, s + 1])
            total = total + (x + x if c == 0 else x)
            for axis in (0, 1):
                part = (a - roll(a, 1, axis)) * (b - roll(b, 1, axis))
                sums[axis] = sums[axis] + (part + part if c == axis + 1 else part)
        for axis in (0, 1):
            total = total + sums[axis] + roll(sums[axis], -1, axis)
        rho = weights[s]
        term[i] = rho * (-3.0 * rho * rho * (0.5 * total))

    loop(0, BX + 4, energy)


def weigh(field, x):
    classes = {}
    for a in range(-2, 3):
        t = field[x + 2 + a]
        for b, value in ((0, t), (1, roll(t, 1, 0) + roll(t, -1, 0)), (2, roll(t, 2, 0) + roll(t, -2, 0))):
            q = a * a + b * b
            classes[q] = value if q not in classes else classes[q] + value
    parts = []
    for z in (0, 1, 2):
        part = None
        for q, value in classes.items():
            w = distance_weight(q + z * z)
            if w > 0.0:
                part = w * value if part is None else part + w * value
        parts.append(part)
    result = parts[0] + roll(parts[1], 1, 1) + roll(parts[1], -1, 1) + roll(parts[2], 2, 1) + roll(parts[2], -2, 1)
    return result[:BY, :BZ]


def arrive(far, near, copied):
    moves = [pltpu.make_async_copy(source, target, copied.at[i]) for i, (source, target) in enumerate(zip(far, near))]
    for move in moves:
        move.start()
    for move in moves:
        move.wait()


def filter_iterate(pos, *rest):
    far, out, near, (term, inside, copied) = rest[:3], rest[3], rest[4:7], rest[7:]
    arrive(far, near, copied)
    iterate, state, weights = near
    sensitivity(state, iterate, weights, term)

    def mark(i):
        inside[i] = jnp.where(weights[i + 1] > 0.0, 1.0, 0.0)

    loop(0, BX + 4, mark)

    def smooth(x):
        factor = 1.0 / (weights[x + 3][:BY, :BZ] * weigh(inside, x))
        out[0, x] = factor * weigh(term, x)
        out[1, x] = factor

    loop(0, BX, smooth)


def filter_precond(pos, *rest):
    far, out, near, (term, copied) = rest[:6], rest[6], rest[7:13], rest[13:]
    arrive(far, near, copied)
    precond, state, weights = near[3:]
    sensitivity(state, precond, weights, term)

    def smooth(x):
        out[x] = weigh(term, x)

    loop(0, BX, smooth)


def finish(pos, totals, *rest):
    second, iterate, parts, smooth, solution, residual, filtered = rest
    total = jnp.sum(totals[...], axis=0, keepdims=True)
    lane = iota((1, BZ), 1)
    one = jnp.sum(jnp.where(lane == 0, total, 0.0), axis=1, keepdims=True)
    two = jnp.sum(jnp.where(lane == 1, total, 0.0), axis=1, keepdims=True)
    alpha = one / two

    def update(x):
        for c in range(3):
            solution[c, x] = iterate[c, x] + alpha * parts[c, x]
            residual[c, x] = parts[3 + c, x] - alpha * parts[6 + c, x]
        filtered[x] = smooth[0, x] + alpha * (second[x] * smooth[1, x])

    loop(0, BX, update)


def body(right_side, iterate, state, classes, load_mask, fixed_mask):
    nx, ny, nz = (lax.axis_size(axis) for axis in ("gx", "gy", "gz"))
    pos = jnp.stack([lax.axis_index("gx"), lax.axis_index("gy"), lax.axis_index("gz")]).astype(jnp.int32)
    pos = jnp.concatenate([pos, jnp.array([nx, ny, nz], jnp.int32)])
    cells = (BX, BY, BZ)
    field = (3,) + cells
    wide = (ROWS, LANES)

    def slabs(n):
        return (n,) + wide

    def fields(n):
        return (3, n) + wide

    main, last, first = launch(
        4, prepare, [(11,) + cells, cells, cells], [field], [pos],
        far=[right_side, iterate, state, classes, load_mask, fixed_mask], copies=6)
    from_lower, from_upper = shift_along(last, "gz", 1), shift_along(first, "gz", -1)
    edge = (12, BX, BY // 2, BZ)
    packed, to_upper, to_lower = launch(4, pack_rows, [cells, edge, edge], [], [pos, main, from_lower, from_upper])
    from_lower, from_upper = shift_along(to_upper, "gy", 1), shift_along(to_lower, "gy", -1)
    sides = (SENT, ROWS, BZ)
    own, to_upper, to_lower = launch(
        14, pack_slabs, [(12, BX, ROWS, BZ), sides, sides],
        [slabs(BX)] * 3 + [fields(BX)] * 2 + [slabs(BX)] * 3 + [fields(BX)], [pos, main, packed, from_lower, from_upper])
    from_lower, from_upper = shift_along(to_upper, "gx", 1), shift_along(to_lower, "gx", -1)

    one, three = slabs(SLABS), fields(SLABS)
    quarters = (22, 8, BZ)
    coarse, low, high, v1, start, kx, ky, kz, inverse, u, weights, forward = launch(
        24, descend, [(44, 16, BZ), quarters, quarters],
        [three, three, one, one, one, three, three, one, fields(14), one, one, three, three, (ROWS, BZ), (44 * 16, BZ)],
        [pos, own, from_lower, from_upper],
        far_outs=[fields(18), fields(16), slabs(17)] + [slabs(16)] * 2 + [fields(16), fields(14), slabs(14), fields(14)],
        copies=9)
    smooth = launch(
        10, filter_iterate, [(2,) + cells], [fields(14), fields(14), slabs(14), slabs(12), slabs(12)], [pos],
        far=[u, forward, weights], copies=3,
        cost=pl.CostEstimate(flops=12_000_000, bytes_accessed=4_000_000, transcendentals=0))[0]

    from_lower, from_upper = shift_along(high, "gz", 1), shift_along(low, "gz", -1)
    coarse, center = launch(4, join_lanes, [(44, 16, BZ), (44, 8, BZ)], [], [pos, coarse, from_lower, from_upper])
    from_lower, from_upper = shift_along(center, "gy", 1), shift_along(center, "gy", -1)
    wide1 = (16, BZ)
    one1, three1 = (10,) + wide1, (3, 10) + wide1
    chunk = launch(
        4, level_one, [(ny, 24, BZ)], [one1] * 3 + [three1] * 5 + [(8, BZ), (40, BZ), (40, BZ)], [pos, coarse])[0]
    side = (32, 24, BZ)
    column = lax.all_to_all(chunk, "gy", 0, 0, tiled=True)
    to_upper, to_lower, center = launch(
        4, join_rows, [side, side], [(44, 24, BZ)], [pos, center, from_lower, from_upper],
        far_outs=[(44, 24, BZ)], copies=1)
    column = launch(8, pack_column, [(nx, 20 * ny, BZ)], [], [pos, column])[0]
    gathered = lax.all_to_all(column, "gx", 0, 0, tiled=True)
    from_lower, from_upper = shift_along(to_upper, "gx", 1), shift_along(to_lower, "gx", -1)

    wide1 = (24, BZ)
    one1, three1 = (18,) + wide1, (3, 18) + wide1
    wide2, wide3 = (4 * ny, BZ), (2 * ny, BZ)
    one2, three2 = (nx + 2,) + wide2, (3, nx + 2) + wide2
    one3, three3 = (nx + 2,) + wide3, (3, nx + 2) + wide3
    work = [one2, one2, three2] + [one2] * 4 + [three2] * 4 + [wide2, (5 * nx * 2 * ny, BZ)]
    work += [one3, one3, three3] + [one3] * 3 + [three3] * 3 + [(nx * 2 * ny, BZ)]
    parts = (9,) + cells
    far = [gathered, center, v1, start, kx, ky, kz, inverse]
    scratch = [x.shape for x in far] + [
        (3, nx + 4) + wide2, (15 * 4 * ny, LANES), wide1, three1, three1, (ROWS, BZ), (240, LANES), fields(16), fields(14), parts
    ] + [three1] * 2 + [one1] * 3 + [three1, one1, one1, three1, three1] + work
    sums, parts, precond = launch(
        30, functools.partial(ascend, nx=nx, ny=ny), [(8, BZ)], scratch, [pos, from_lower, from_upper],
        far_outs=[parts, fields(14)], far=far + [smooth], copies=11)
    ready = launch(
        12, filter_precond, [cells, field, parts.shape, smooth.shape], [fields(14), fields(14), slabs(14), slabs(12)], [pos],
        far=[iterate, parts, smooth, precond, forward, weights], copies=6, pin=True,
        cost=pl.CostEstimate(flops=8_000_000, bytes_accessed=4_000_000, transcendentals=0))
    total = lax.all_to_all(jnp.broadcast_to(sums[:1], (nx * ny, BZ)), ("gx", "gy"), 0, 0, tiled=True)
    total = jnp.sum(total, axis=0, keepdims=True)
    total = lax.all_to_all(jnp.broadcast_to(total, (nz, BZ)), "gz", 0, 0, tiled=True)
    return tuple(launch(4, finish, [field, field, cells], [], [pos, total, *ready]))


def solution(mesh):
    field, cells = P(None, "gx", "gy", "gz"), P("gx", "gy", "gz")
    return jax.shard_map(
        body,
        mesh=mesh,
        in_specs=(field, field, field, cells, cells, cells),
        out_specs=(field, field, cells),
        check_vma=False,
    )
```

```python
import functools
import math

import jax
import jax.numpy as jnp
from jax import lax
from jax.experimental import pallas as pl
from jax.experimental.pallas import tpu as pltpu
from jax.sharding import PartitionSpec as P

F32 = jnp.float32
FLOOR = 0.25
CLASSES = 16
PENALTY = 4.0
FIRST = 0.55
SECOND = 1.05
COARSE = 0.6
RADIUS = 3

BX, BY, BZ = 8, 16, 128
HALO = 7
SLABS = BX + 2 * HALO
ROWS = 2 * BY
LANES = 2 * BZ

PACKED = 8
ITERATE = ((0, 0, 7), (1, 7, 7), (2, 14, 7))
RHO = (3, 21, 7)
LOAD = ((4, 28, 6), (5, 34, 6), (6, 40, 6))
PEN = (7, 46, 6)
STATE = ((9, 52, 3), (10, 55, 3), (11, 58, 3))
FIELDS = ITERATE + (RHO,) + LOAD + (PEN,) + STATE
HALF = BZ // 2

MIB = 1024 * 1024


def iota(shape, dim):
    return lax.broadcasted_iota(jnp.int32, shape, dim)


def roll(x, shift, axis):
    return pltpu.roll(x, shift % x.shape[axis], axis)


def loop(lower, upper, step, unroll=4):
    def run(i, carry):
        step(i)
        return carry

    lax.fori_loop(lower, upper, run, 0, unroll=unroll)


def times(x, m):
    m = m.astype(jnp.bfloat16)
    high = x.astype(jnp.bfloat16)
    low = (x - high.astype(F32)).astype(jnp.bfloat16)
    return jnp.dot(high, m, preferred_element_type=F32) + jnp.dot(low, m, preferred_element_type=F32)


def matrix(shape, rule):
    return jnp.where(rule(iota(shape, 0), iota(shape, 1)), 1.0, 0.0).astype(F32)


def face(a, b):
    total = a + b
    both = (a > 0.0) & (b > 0.0)
    return jnp.where(both, 2.0 * a * b / jnp.where(both, total, 1.0), total)


def launch(limit, kernel, outs, scratch, operands, far_outs=(), far=(), copies=0, cost=None, pin=False):
    near_spec, far_spec = pl.BlockSpec(memory_space=pltpu.VMEM), pl.BlockSpec(memory_space=pltpu.HBM)
    specs = [pl.BlockSpec(memory_space=pltpu.SMEM)] + [near_spec] * (len(operands) - 1) + [far_spec] * len(far)
    return pl.pallas_call(
        kernel,
        out_shape=[pltpu.VMEM(shape, F32) if pin else jax.ShapeDtypeStruct(shape, F32) for shape in outs] + [pltpu.HBM(shape, F32) for shape in far_outs],
        in_specs=specs,
        out_specs=[near_spec] * len(outs) + [far_spec] * len(far_outs),
        scratch_shapes=[pltpu.VMEM(shape, F32) for shape in scratch] + ([pltpu.SemaphoreType.DMA((copies,))] if copies else []),
        compiler_params=pltpu.CompilerParams(vmem_limit_bytes=limit * MIB),
        cost_estimate=cost,
    )(*(operands[:1] + [pltpu.with_memory_space_constraint(x, pltpu.VMEM) for x in operands[1:]] if pin else operands), *[pltpu.with_memory_space_constraint(x, pltpu.HBM) for x in far])


def shift_along(x, axis, step):
    devices = lax.axis_size(axis)
    return lax.ppermute(x, axis, [(i, (i + step) % devices) for i in range(devices)])


def prepare(pos, right_far, iterate_far, state_far, classes_far, load_far, fixed_far, main, to_upper, to_lower, right, copied):
    def rest(classes, load_mask, fixed_mask):
        moves = [
            pltpu.make_async_copy(source, target, copied.at[i])
            for i, (source, target) in enumerate((
                (classes_far, classes), (load_far, load_mask), (fixed_far, fixed_mask), (right_far, right),
                (iterate_far, main.at[0:3]), (state_far, main.at[8:11])))
        ]
        for move in moves:
            move.start()
        for move in moves:
            move.wait()
        lane = iota((BY, BZ), 1)

        def slab(x):
            mask = load_mask[x].astype(F32)
            main[3, x] = FLOOR + (1.0 - FLOOR) * classes[x].astype(F32) / (CLASSES - 1)
            main[7, x] = PENALTY * fixed_mask[x].astype(F32)
            for c in range(3):
                main[4 + c, x] = right[c, x] * mask
            last = jnp.zeros((BY, BZ), F32)
            first = jnp.zeros((BY, BZ), F32)
            for tile, offset, width in FIELDS:
                value = main[tile if tile < PACKED else tile - 1, x]
                last = jnp.where((lane >= offset) & (lane < offset + width), roll(value, offset + width, 1), last)
                low = HALF + offset
                first = jnp.where((lane >= low) & (lane < low + width), roll(value, low, 1), first)
            to_upper[x] = last
            to_lower[x] = first

        loop(0, BX, slab)

    cells = pltpu.VMEM((BX, BY, BZ), jnp.int32)
    pl.run_scoped(rest, cells, cells, cells)


def pack_rows(pos, main, from_lower, from_upper, packed, to_upper, to_lower):
    below = jnp.where(pos[2] > 0, 1.0, 0.0)
    above = jnp.where(pos[2] < pos[5] - 1, 1.0, 0.0)
    lane = iota((BY, BZ), 1)
    row = iota((BY // 2, BZ), 0)
    half = BY // 2

    def slab(x):
        joined = jnp.where(lane < HALF, from_lower[x] * below, from_upper[x] * above)
        packed[x] = joined
        values = [joined if tile == PACKED else main[tile if tile < PACKED else tile - 1, x] for tile in range(12)]
        uppers = [value[half:] for value in values]
        lowers = [value[:half] for value in values]
        for c in range(3):
            up, down = uppers[9 + c], lowers[9 + c]
            uppers[LOAD[c][0]] = jnp.where(row < 2, roll(up, 3, 0), uppers[LOAD[c][0]])
            uppers[ITERATE[c][0]] = jnp.where(row < 1, roll(up, 1, 0), uppers[ITERATE[c][0]])
            lowers[LOAD[c][0]] = jnp.where(row >= 6, roll(down, 6, 0), lowers[LOAD[c][0]])
            lowers[ITERATE[c][0]] = jnp.where(row >= 7, roll(down, 5, 0), lowers[ITERATE[c][0]])
        for tile in range(9):
            to_upper[tile, x] = uppers[tile]
            to_lower[tile, x] = lowers[tile]

    loop(0, BX, slab)


def neighbours(field, c, s, kx, ky, kz, at=None):
    at = s if at is None else at
    v = field[c, s]
    x = kx[at] * field[c, s - 1] + kx[at + 1] * field[c, s + 1]
    y = ky[at] * roll(v, 1, 0) + roll(ky[at] * v, -1, 0)
    z = kz[at] * roll(v, 1, 1) + roll(kz[at] * v, -1, 1)
    return x + y + z + (x, y, z)[c]


def coefficients(stiff, pen, s, scale, kx, ky, kz, inverse, diagonal):
    e = stiff[s]
    upper = scale * face(e, stiff[s + 1])
    kx[s + 1] = upper
    y = scale * face(e, roll(e, 1, 0))
    ky[s] = y
    yp = roll(y, -1, 0)
    z = scale * face(e, roll(e, 1, 1))
    kz[s] = z
    zp = roll(z, -1, 1)
    pairs = (kx[s] + upper, y + yp, z + zp)
    total = pairs[0] + pairs[1] + pairs[2] + pen[s]
    for c in range(3):
        value = total + pairs[c]
        diagonal[c, s] = value
        if inverse is not None:
            inverse[c, s] = jnp.where(e > 0.0, 1.0 / jnp.where(e > 0.0, value, 1.0), 0.0)


def spread(value, packed, field, ref, at):
    _, offset, width = field
    lane = iota((ROWS, BZ), 1)
    ref[at + (slice(None), slice(0, BZ))] = value
    tail = jnp.where(lane >= BZ - width, roll(packed, BZ - width - offset, 1), 0.0)
    tail = jnp.where(lane < width, roll(packed, -(HALF + offset), 1), tail)
    ref[at + (slice(None), slice(BZ, LANES))] = tail


LAYERS = ((RHO[0], 7), (PACKED, 7)) + tuple((f[0], 6) for f in LOAD + (PEN,)) + tuple((f[0], 3) for f in ITERATE + STATE)
PLACE = {}
SENT = 0
for _tile, _count in LAYERS:
    PLACE[_tile] = SENT
    SENT += _count


def pack_slabs(pos, main, packed, from_lower, from_upper, own, to_upper, to_lower,
               rho, stiff, pen, u, load, kx, ky, kz, diagonal):
    below = jnp.where(pos[1] > 0, 1.0, 0.0)
    above = jnp.where(pos[1] < pos[4] - 1, 1.0, 0.0)
    row = iota((BY // 2, BZ), 0)

    def slab(x):
        for tile in range(12):
            value = packed[x] if tile == PACKED else main[tile if tile < PACKED else tile - 1, x]
            if tile <= PACKED:
                high, low = from_upper[tile, x], from_lower[tile, x]
            else:
                load_at, iterate_at = LOAD[tile - 9][0], ITERATE[tile - 9][0]
                high = jnp.where(row < 2, roll(from_upper[load_at, x], 2, 0), roll(from_upper[iterate_at, x], 3, 0))
                low = jnp.where(row < 7, roll(from_lower[load_at, x], 5, 0), roll(from_lower[iterate_at, x], 7, 0))
            own[tile, x] = jnp.concatenate([value, high * above, low * below], 0)

    loop(0, BX, slab)

    def expand(x):
        halo = own[PACKED, x]
        spread(own[RHO[0], x], halo, RHO, rho, (x,))
        spread(own[PEN[0], x], halo, PEN, pen, (x,))
        for c in range(3):
            spread(own[ITERATE[c][0], x], halo, ITERATE[c], u, (c, x))
            spread(own[LOAD[c][0], x], halo, LOAD[c], load, (c, x))
        stiff[x] = rho[x] * rho[x] * rho[x]

    loop(0, BX, expand)
    kx[1] = face(stiff[0], stiff[1])
    loop(1, BX - 1, lambda x: coefficients(stiff, pen, x, 1.0, kx, ky, kz, None, diagonal))
    lane = iota((ROWS, BZ), 1)

    def begin(x):
        halo = own[PACKED, x]
        for c in range(3):
            f = load[c, x] - (diagonal[c, x] * u[c, x] - neighbours(u, c, x, kx, ky, kz))
            tile, offset, width = LOAD[c]
            own[tile, x] = f[:, :BZ]
            tail = f[:, BZ:]
            halo = jnp.where((lane >= offset) & (lane < offset + width), roll(tail, offset + width, 1), halo)
            low = HALF + offset
            halo = jnp.where((lane >= low) & (lane < low + width), roll(tail, low, 1), halo)
        own[PACKED, x] = halo

    loop(1, BX - 1, begin)
    for tile, count in LAYERS:
        for j in range(count):
            to_upper[PLACE[tile] + j] = own[tile, BX - count + j]
            to_lower[PLACE[tile] + j] = own[tile, j]


def descend(pos, own, lower, upper, coarse, low_lanes, high_lanes, *rest):
    far, rest = rest[:9], rest[9:]
    (v1, start, kx, ky, kz, inverse, u, weights, forward, stiff, pen, diagonal, v0, half_rows, rows, copied) = rest
    moves = []

    def send(*pairs):
        for source, target in pairs:
            move = pltpu.make_async_copy(source, far[target], copied.at[target])
            move.start()
            moves.append(move)

    below = jnp.where(pos[0] > 0, 1.0, 0.0)
    above = jnp.where(pos[0] < pos[3] - 1, 1.0, 0.0)

    def expand(raw, s, fields):
        halo = raw(PACKED)
        for field, ref, at in fields:
            spread(raw(field[0]), halo, field, ref, at)

    def densities(s):
        return [(RHO, weights, (s,))]

    def loads(s):
        return [(PEN, pen, (s,))] + [(LOAD[c], start, (c, s)) for c in range(3)]

    def motions(s):
        return [(ITERATE[c], u, (c, s)) for c in range(3)] + [(STATE[c], forward, (c, s - 4)) for c in range(3)]

    def lower_raw(s):
        return lambda t: lower[PLACE[t] + s - (HALO - dict(LAYERS)[t])] * below

    def upper_raw(s):
        return lambda t: upper[PLACE[t] + s - (HALO + BX)] * above

    after = HALO + BX
    loop(0, HALO, lambda s: expand(lower_raw(s), s, densities(s)))
    loop(1, HALO, lambda s: expand(lower_raw(s), s, loads(s)))
    loop(4, HALO, lambda s: expand(lower_raw(s), s, motions(s)))
    loop(HALO, after, lambda s: expand(lambda t: own[t, s - HALO], s, densities(s) + loads(s) + motions(s)))
    loop(after, after + 7, lambda s: expand(upper_raw(s), s, densities(s)))
    loop(after, after + 6, lambda s: expand(upper_raw(s), s, loads(s)))
    loop(after, after + 3, lambda s: expand(upper_raw(s), s, motions(s)))
    send((u.at[:, 4:18], 6), (weights.at[4:18], 7), (forward, 8))

    def cube(s):
        rho = weights[s]
        stiff[s] = rho * rho * rho

    loop(0, SLABS, cube)
    kx[1] = face(stiff[0], stiff[1])
    loop(1, SLABS - 1, lambda s: coefficients(stiff, pen, s, 1.0, kx, ky, kz, inverse, diagonal))
    faces = (kx, ky, kz)
    send((kx.at[3:20], 2), (ky.at[3:19], 3), (kz.at[3:19], 4), (inverse.at[:, 3:19], 5))

    for s in (HALO - 1, HALO, HALO + BX - 1, HALO + BX):
        for c in range(3):
            start[c, s] = start[c, s] - (diagonal[c, s] * u[c, s] - neighbours(u, c, s, *faces))

    def begin(s):
        for c in range(3):
            v0[c, s] = FIRST * start[c, s] * inverse[c, s]

    loop(1, SLABS - 1, begin)
    send((start.at[:, 3:19], 1))

    def sweep(s):
        for c in range(3):
            v1[c, s] = (1.0 - SECOND) * v0[c, s] + SECOND * inverse[c, s] * (start[c, s] + neighbours(v0, c, s, *faces))

    loop(2, SLABS - 2, sweep)
    send((v1.at[:, 2:20], 0))

    def remainder(c, s):
        r = start[c, s] - diagonal[c, s] * v1[c, s] + neighbours(v1, c, s, *faces)
        return r[:, :BZ]

    def gather_rows(at, value):
        half_rows[...] = value
        n = ROWS // 2
        rows[pl.ds(pl.multiple_of(at * n, n), n), :] = half_rows[pl.ds(0, n, stride=2), :] + half_rows[pl.ds(1, n, stride=2), :]

    def pair(i):
        for c in range(3):
            gather_rows(c * 8 + i, remainder(c, 3 + 2 * i) + remainder(c, 4 + 2 * i))

    loop(0, 8, pair)

    def pair_up(i):
        s = 1 + 2 * i
        gather_rows(24 + i, (stiff[s] + stiff[s + 1])[:, :BZ] * 0.125)
        gather_rows(34 + i, (pen[s] + pen[s + 1])[:, :BZ])

    loop(0, 10, pair_up)
    halve = matrix((BZ, BZ), lambda l, k: (l >> 1) == (k & (HALF - 1)))
    coarse[...] = times(rows[...], halve).reshape(44, 16, BZ)
    quarter = iota((8, BZ), 1) >> 5

    def pack(g):
        for h in range(2):
            low = jnp.zeros((8, BZ), F32)
            high = jnp.zeros((8, BZ), F32)
            for q in range(4):
                value = coarse[4 * g + q, 8 * h:8 * h + 8]
                turned = roll(value, 32, 1)
                one, two = (value, turned) if q % 2 == 0 else (turned, value)
                low = jnp.where(quarter == q, one, low)
                high = jnp.where(quarter == q, two, high)
            low_lanes[2 * g + h] = low
            high_lanes[2 * g + h] = high

    loop(0, 11, pack)
    for move in moves:
        move.wait()


def join_lanes(pos, coarse, from_lower, from_upper, out, center):
    below = jnp.where(pos[2] > 0, 1.0, 0.0)
    above = jnp.where(pos[2] < pos[5] - 1, 1.0, 0.0)
    lane = iota((8, BZ), 1)

    def unpack(g):
        for h in range(2):
            low, high = from_lower[2 * g + h] * below, from_upper[2 * g + h] * above
            for q in range(4):
                halo = jnp.where(lane < 96, roll(high, 64 - 32 * q, 1), roll(low, 96 - 32 * q, 1))
                value = jnp.where(lane < 64, coarse[4 * g + q, 8 * h:8 * h + 8], halo)
                out[4 * g + q, 8 * h:8 * h + 8] = value
                if h == 0:
                    center[4 * g + q] = value

    loop(0, 11, unpack)


def join_rows(pos, coarse, from_lower, from_upper, to_upper, to_lower, center, out, copied):
    below = jnp.where(pos[1] > 0, 1.0, 0.0)
    above = jnp.where(pos[1] < pos[4] - 1, 1.0, 0.0)

    def join(i):
        out[i] = jnp.concatenate([coarse[i], from_upper[i] * above, from_lower[i] * below], 0)

    loop(0, 44, join)
    move = pltpu.make_async_copy(out, center, copied.at[0])
    move.start()
    at = 0
    for base, count in ((0, 6), (8, 6), (16, 6), (24, 7), (34, 7)):
        shift = 2 if count == 6 else 3
        for j in range(count):
            to_upper[at] = out[base + j]
            to_lower[at] = out[base + shift + j]
            at += 1
    move.wait()


def smooth_down(slabs, f, v0, v1, inverse, faces):
    def begin(s):
        for c in range(3):
            v0[c, s] = FIRST * f[c, s] * inverse[c, s]

    loop(1, slabs - 1, begin)

    def sweep(s):
        for c in range(3):
            v1[c, s] = (1.0 - SECOND) * v0[c, s] + SECOND * inverse[c, s] * (f[c, s] + neighbours(v0, c, s, *faces))

    loop(2, slabs - 2, sweep)


def level_one(pos, own, chunk, kx, ky, kz, inverse, diagonal, f, v0, v1, half_rows, rows, wide):
    stiff, pen = own.at[24:34], own.at[34:44]
    slabs = 10
    for c in range(3):
        for i in range(8):
            f[c, 1 + i] = own[8 * c + i]
    kx[1] = 2.0 * face(stiff[0], stiff[1])
    loop(1, slabs - 1, lambda s: coefficients(stiff, pen, s, 2.0, kx, ky, kz, inverse, diagonal))
    faces = (kx, ky, kz)
    smooth_down(slabs, f, v0, v1, inverse, faces)

    def gather_rows(at, value):
        half_rows[...] = value
        rows[pl.ds(at * 4, 4), :] = half_rows[pl.ds(0, 4, stride=2), :] + half_rows[pl.ds(1, 4, stride=2), :]

    for i in range(2):
        s = 3 + 2 * i
        for c in range(3):
            total = 0.0
            for at in (s, s + 1):
                total = total + (f[c, at] - diagonal[c, at] * v1[c, at] + neighbours(v1, c, at, *faces))[:8]
            gather_rows(2 * c + i, total)
        gather_rows(6 + i, (stiff[s] + stiff[s + 1])[:8] * 0.125)
        gather_rows(8 + i, (pen[s] + pen[s + 1])[:8])

    def rule(j, k):
        z = jnp.where(j < 96, j, j - BZ)
        return (z >> 1) == (k & 63) - 16

    wide[...] = times(rows[...], matrix((BZ, BZ), rule))
    lane = iota((4, BZ), 1)
    parts = [jnp.where(lane < 64, wide[8 * field:8 * field + 4], wide[8 * field + 4:8 * field + 8]) for field in range(5)]
    value = jnp.concatenate(parts + [jnp.zeros((4, BZ), F32)], 0)
    for i in range(chunk.shape[0]):
        chunk[i] = value


def pack_column(pos, column, out):
    for i in range(out.shape[0]):
        for j in range(column.shape[0]):
            out[i, 20 * j:20 * j + 20] = column[j, 0:20]


def level_one_again(pos, own, lower, upper, v1, f, kx, ky, kz, inverse, stiff, pen, diagonal, v0):
    below = jnp.where(pos[0] > 0, 1.0, 0.0)
    above = jnp.where(pos[0] < pos[3] - 1, 1.0, 0.0)
    slabs = 18
    for field, at in ((stiff, 0), (pen, 1)):
        for j in range(7):
            field[j] = lower[18 + 7 * at + j] * below
            field[11 + j] = upper[18 + 7 * at + j] * above
        for j in range(4):
            field[7 + j] = own[24 + 10 * at + 3 + j]
    for c in range(3):
        for j in range(6):
            f[c, 1 + j] = lower[6 * c + j] * below
            f[c, 11 + j] = upper[6 * c + j] * above
        for j in range(4):
            f[c, 7 + j] = own[8 * c + 2 + j]
    kx[1] = 2.0 * face(stiff[0], stiff[1])
    loop(1, slabs - 1, lambda s: coefficients(stiff, pen, s, 2.0, kx, ky, kz, inverse, diagonal))
    smooth_down(slabs, f, v0, v1, inverse, (kx, ky, kz))


def coarse_levels(pos, gathered, out, nx, ny, work):
    (e2, p2, f2, kxm, kxp, kym, kzm, iv, dg, va, vb, tall, rows3, e3, p3, f3, jx, jym, jz, iv3, wa, wb, rows2) = work
    ys = 4 * ny
    pairs = nx
    lane = iota((ys, BZ), 1)
    row = iota((ys, BZ), 0)
    even = lane < 64
    zero = jnp.zeros((ys, BZ), F32)
    for field in (e2, p2):
        field[0] = zero
        field[pairs + 1] = zero
    for c in range(3):
        for field in (va, vb):
            field[c, 0] = zero
            field[c, pairs + 1] = zero

    def collect(g):
        for field in range(5):
            for yy in range(ny):
                value = gathered[g, 20 * yy + 4 * field:20 * yy + 4 * field + 4, :]
                if field < 3:
                    f2[field, g + 1, pl.ds(4 * yy, 4), :] = value
                else:
                    (e2, p2)[field - 3][g + 1, pl.ds(4 * yy, 4), :] = value

    loop(0, pairs, collect)

    def x_neighbours(below, mid, above):
        swapped = roll(mid, 64, 1)
        return jnp.where(even, roll(below, 64, 1), swapped), jnp.where(even, swapped, roll(above, 64, 1))

    def coefs(s):
        e = e2[s]
        xm, xp = x_neighbours(e2[s - 1], e, e2[s + 1])
        ym = jnp.where(row == 0, 0.0, roll(e, 1, 0))
        yp = jnp.where(row == ys - 1, 0.0, roll(e, -1, 0))
        a, b = 4.0 * face(e, xm), 4.0 * face(e, xp)
        c0, d = 4.0 * face(e, ym), 4.0 * face(e, yp)
        z = 4.0 * face(e, roll(e, 1, 1))
        zp = roll(z, -1, 1)
        kxm[s] = a
        kxp[s] = b
        kym[s] = jnp.where(row == 0, 0.0, c0)
        kzm[s] = z
        sums = (a + b, c0 + d, z + zp)
        total = sums[0] + sums[1] + sums[2] + p2[s]
        for c in range(3):
            value = total + sums[c]
            dg[c, s] = value
            iv[c, s] = jnp.where(e > 0.0, 1.0 / jnp.where(e > 0.0, value, 1.0), 0.0)
            va[c, s] = FIRST * f2[c, s] * iv[c, s]

    loop(1, pairs + 1, coefs)

    def around(v, c, s):
        mid = v[c, s]
        below, above = x_neighbours(v[c, s - 1], mid, v[c, s + 1])
        x = kxm[s] * below + kxp[s] * above
        y = kym[s] * roll(mid, 1, 0) + roll(kym[s] * mid, -1, 0)
        z = kzm[s] * roll(mid, 1, 1) + roll(kzm[s] * mid, -1, 1)
        return x + y + z + (x, y, z)[c]

    def sweep(source, target, weight):
        def step(s):
            for c in range(3):
                target[c, s] = (1.0 - weight) * source[c, s] + weight * iv[c, s] * (f2[c, s] + around(source, c, s))

        loop(1, pairs + 1, step)

    sweep(va, vb, SECOND)
    n3 = ys // 2

    def gather_rows(at, value):
        tall[...] = value
        rows3[pl.ds(pl.multiple_of(at * n3, 8), n3), :] = tall[pl.ds(0, n3, stride=2), :] + tall[pl.ds(1, n3, stride=2), :]

    def reduce(s):
        for c in range(3):
            gather_rows(c * pairs + s - 1, f2[c, s] - dg[c, s] * vb[c, s] + around(vb, c, s))
        gather_rows(3 * pairs + s - 1, e2[s] * 0.125)
        gather_rows(4 * pairs + s - 1, p2[s])

    loop(1, pairs + 1, reduce)
    down = matrix((BZ, BZ), lambda l, k: ((l & 63) >> 1) == (k & 31))
    rows3[...] = times(rows3[...], down)
    row3 = iota((n3, BZ), 0)
    zero3 = jnp.zeros((n3, BZ), F32)

    def third(at):
        return rows3[pl.ds(pl.multiple_of(at * n3, 8), n3), :]

    e3[0] = zero3
    e3[pairs + 1] = zero3
    for c in range(3):
        for field in (wa, wb):
            field[c, 0] = zero3
            field[c, pairs + 1] = zero3

    def place(s):
        e3[s] = third(3 * pairs + s - 1)

    loop(1, pairs + 1, place)

    def coefs3(s):
        e = e3[s]
        a, b = 8.0 * face(e, e3[s - 1]), 8.0 * face(e, e3[s + 1])
        c0 = 8.0 * face(e, jnp.where(row3 == 0, 0.0, roll(e, 1, 0)))
        d = 8.0 * face(e, jnp.where(row3 == n3 - 1, 0.0, roll(e, -1, 0)))
        z = 8.0 * face(e, roll(e, 1, 1))
        zp = roll(z, -1, 1)
        jx[s] = a
        jx[s + 1] = b
        jym[s] = jnp.where(row3 == 0, 0.0, c0)
        jz[s] = z
        sums = (a + b, c0 + d, z + zp)
        total = sums[0] + sums[1] + sums[2] + third(4 * pairs + s - 1)
        for c in range(3):
            value = total + sums[c]
            iv3[c, s] = jnp.where(e > 0.0, 1.0 / jnp.where(e > 0.0, value, 1.0), 0.0)
            wa[c, s] = COARSE * third(c * pairs + s - 1) * iv3[c, s]

    loop(1, pairs + 1, coefs3)
    source, target = wa, wb
    for sweep_at in range(3):
        def step(s, source=source, target=target):
            for c in range(3):
                near = neighbours(source, c, s, jx, jym, jz)
                target[c, s] = (1.0 - COARSE) * source[c, s] + COARSE * iv3[c, s] * (third(c * pairs + s - 1) + near)

        loop(1, pairs + 1, step)
        source, target = target, source
    up = matrix((BZ, BZ), lambda k, l: k == ((l & 63) >> 1))
    for c in range(3):
        rows2[...] = times(source[c, 1:pairs + 1].reshape(pairs * n3, BZ), up)

        def add(s, c=c):
            value = rows2[pl.ds(pl.multiple_of((s - 1) * n3, 8), n3), :]
            tall[pl.ds(0, n3, stride=2), :] = value
            tall[pl.ds(1, n3, stride=2), :] = value
            vb[c, s] = vb[c, s] + jnp.where(iv[c, s] > 0.0, tall[...], 0.0)

        loop(1, pairs + 1, add)
    sweep(vb, va, SECOND)

    for c in range(3):
        for at in (0, 1, pairs + 2, pairs + 3):
            out[c, at] = zero

    def last(s):
        for c in range(3):
            out[c, s + 1] = (1.0 - FIRST) * va[c, s] + FIRST * iv[c, s] * (f2[c, s] + around(va, c, s))

    loop(1, pairs + 1, last)


def ascend(pos, lower, upper, gathered, *rest, nx, ny):
    far, (sums, parts, precond_far), rest = rest[:7], rest[8:11], rest[11:]
    near, rest = rest[:7], rest[7:]
    e2out, window, rows24, va1, vb1, rows32, spread, vb, precond, held = rest[:10]
    v1, f1, kx1, ky1, kz1, inverse1, stiff1, pen1, diagonal1, v01 = rest[10:20]
    work, copied = rest[20:-1], rest[-1]
    center = near[0]
    va, start, kx, ky, kz, inverse = near[1:]
    arrivals = [pltpu.make_async_copy(source, target, copied.at[i]) for i, (source, target) in enumerate(zip(far, near))]
    for move in arrivals:
        move.start()
    departures = []

    def send(source, target):
        move = pltpu.make_async_copy(source, target, copied.at[7 + len(departures)])
        move.start()
        departures.append(move)

    coarse_levels(pos, gathered, e2out, nx, ny, work)
    arrivals[0].wait()
    level_one_again(
        pos, center, lower, upper, v1, f1, kx1, ky1, kz1, inverse1, stiff1, pen1, diagonal1, v01)
    gx, gy = pos[0], pos[1]
    ys = 4 * ny
    turn = lax.rem(ys - 4 * gy, ys)

    def rule(k, j):
        z = jnp.where((j & 127) < 96, j & 127, (j & 127) - BZ)
        return k == 64 * (j >> 7) + (z >> 1) + 16

    grow = matrix((BZ, LANES), rule)
    for c in range(3):
        for j in range(5):
            window[pl.ds((5 * c + j) * ys, ys), :] = times(pltpu.roll(e2out[c, gx + j], turn, 0), grow)
    for c in range(3):
        for s in range(2, 16):
            x2 = (s - 7) // 2
            j, part = (x2 + 4) // 2, (x2 + 4) % 2
            base = (5 * c + j) * ys
            cols = slice(128 * part, 128 * part + 128)
            if s % 2 == 1 or s == 2:
                low = window[base:base + 8, cols]
                high = window[base + ys - 4:base + ys, cols]
                for at in (0, 1):
                    rows24[pl.ds(at, 8, stride=2), :] = low
                    rows24[pl.ds(16 + at, 4, stride=2), :] = high
            va1[c, s] = v1[c, s] + jnp.where(inverse1[c, s] > 0.0, rows24[...], 0.0)
    faces1 = (kx1, ky1, kz1)

    def sweep1(source, target, weight, lower, upper):
        def step(s):
            for c in range(3):
                target[c, s] = (1.0 - weight) * source[c, s] + weight * inverse1[c, s] * (
                    f1[c, s] + neighbours(source, c, s, *faces1))

        loop(lower, upper, step)

    sweep1(va1, vb1, SECOND, 3, 15)
    sweep1(vb1, va1, FIRST, 4, 14)
    grow0 = matrix((BZ, LANES), lambda j, l: j == (l >> 1))
    for move in arrivals[1:]:
        move.wait()
    for c in range(3):
        spread[...] = times(va1[c, 4:14].reshape(240, BZ), grow0)
        for i in range(10):
            for half in (0, 1):
                cols = slice(BZ * half, BZ * half + BZ)
                value = spread[24 * i:24 * i + 24, cols]
                for at in (0, 1):
                    rows32[pl.ds(at, 12, stride=2), :] = value[:12]
                    rows32[pl.ds(24 + at, 4, stride=2), :] = value[20:]
                for s in (2 * i - 1, 2 * i):
                    if 0 <= s < 18:
                        va[c, s, :, cols] = va[c, s, :, cols] + rows32[...]
    faces = (kx, ky, kz)

    def sweep_one(t):
        for c in range(3):
            vb[c, t] = (1.0 - SECOND) * va[c, t + 1] + SECOND * inverse[c, t] * (
                start[c, t] + neighbours(va, c, t + 1, *faces, at=t))

    loop(0, 16, sweep_one)

    def sweep_two(t):
        for c in range(3):
            precond[c, t - 1] = (1.0 - FIRST) * vb[c, t] + FIRST * inverse[c, t] * (start[c, t] + neighbours(vb, c, t, *faces))

    loop(1, 15, sweep_two)

    def keep(x):
        for c in range(3):
            held[c, x] = precond[c, x + 3][:BY, :BZ]
            held[3 + c, x] = start[c, x + 4][:BY, :BZ]

    loop(0, BX, keep)
    send(held.at[0:6], parts.at[0:6])
    send(precond, precond_far)

    def inner(x, carry):
        one, two = carry
        for c in range(3):
            mid = held[c, x]
            value = mid / inverse[c, x + 4][:BY, :BZ] - neighbours(precond, c, x + 3, *faces, at=x + 4)[:BY, :BZ]
            held[6 + c, x] = value
            one = one + held[3 + c, x] * mid
            two = two + mid * value
        return one, two

    zero = jnp.zeros((BY, BZ), F32)
    one, two = lax.fori_loop(0, BX, inner, (zero, zero), unroll=4)
    send(held.at[6:9], parts.at[6:9])
    lane = iota((8, BZ), 1)
    sums[...] = jnp.where(lane == 0, jnp.sum(one), jnp.where(lane == 1, jnp.sum(two), 0.0))
    for move in departures:
        move.wait()


def distance_weight(square):
    return max(RADIUS - math.sqrt(square), 0.0)


def sensitivity(state, field, weights, term):
    def energy(i):
        s = i + 1
        total = jnp.zeros((ROWS, LANES), F32)
        sums = [0.0, 0.0]
        for c in range(3):
            a, b = state[c, s], field[c, s]
            x = (a - state[c, s - 1]) * (b - field[c, s - 1]) + (a - state[c, s + 1]) * (b - field[c, s + 1])
            total = total + (x + x if c == 0 else x)
            for axis in (0, 1):
                part = (a - roll(a, 1, axis)) * (b - roll(b, 1, axis))
                sums[axis] = sums[axis] + (part + part if c == axis + 1 else part)
        for axis in (0, 1):
            total = total + sums[axis] + roll(sums[axis], -1, axis)
        rho = weights[s]
        term[i] = rho * (-3.0 * rho * rho * (0.5 * total))

    loop(0, BX + 4, energy)


def weigh(field, x):
    classes = {}
    for a in range(-2, 3):
        t = field[x + 2 + a]
        for b, value in ((0, t), (1, roll(t, 1, 0) + roll(t, -1, 0)), (2, roll(t, 2, 0) + roll(t, -2, 0))):
            q = a * a + b * b
            classes[q] = value if q not in classes else classes[q] + value
    parts = []
    for z in (0, 1, 2):
        part = None
        for q, value in classes.items():
            w = distance_weight(q + z * z)
            if w > 0.0:
                part = w * value if part is None else part + w * value
        parts.append(part)
    result = parts[0] + roll(parts[1], 1, 1) + roll(parts[1], -1, 1) + roll(parts[2], 2, 1) + roll(parts[2], -2, 1)
    return result[:BY, :BZ]


def arrive(far, near, copied):
    moves = [pltpu.make_async_copy(source, target, copied.at[i]) for i, (source, target) in enumerate(zip(far, near))]
    for move in moves:
        move.start()
    for move in moves:
        move.wait()


def filter_iterate(pos, *rest):
    far, out, near, (term, inside, copied) = rest[:3], rest[3], rest[4:7], rest[7:]
    arrive(far, near, copied)
    iterate, state, weights = near
    sensitivity(state, iterate, weights, term)

    def mark(i):
        inside[i] = jnp.where(weights[i + 1] > 0.0, 1.0, 0.0)

    loop(0, BX + 4, mark)

    def smooth(x):
        factor = 1.0 / (weights[x + 3][:BY, :BZ] * weigh(inside, x))
        out[0, x] = factor * weigh(term, x)
        out[1, x] = factor

    loop(0, BX, smooth)


def filter_precond(pos, *rest):
    far, out, near, (term, copied) = rest[:6], rest[6], rest[7:13], rest[13:]
    moves = [pltpu.make_async_copy(source, target, copied.at[i]) for i, (source, target) in enumerate(zip(far, near))]
    for move in moves[3:] + moves[:3]:
        move.start()
    for move in moves[3:]:
        move.wait()
    precond, state, weights = near[3:]
    sensitivity(state, precond, weights, term)

    def smooth(x):
        out[x] = weigh(term, x)

    loop(0, BX, smooth)
    for move in moves[:3]:
        move.wait()


def finish(pos, totals, *rest):
    second, iterate, parts, smooth, solution, residual, filtered = rest
    total = jnp.sum(totals[...], axis=0, keepdims=True)
    lane = iota((1, BZ), 1)
    one = jnp.sum(jnp.where(lane == 0, total, 0.0), axis=1, keepdims=True)
    two = jnp.sum(jnp.where(lane == 1, total, 0.0), axis=1, keepdims=True)
    alpha = one / two

    def update(x):
        for c in range(3):
            solution[c, x] = iterate[c, x] + alpha * parts[c, x]
            residual[c, x] = parts[3 + c, x] - alpha * parts[6 + c, x]
        filtered[x] = smooth[0, x] + alpha * (second[x] * smooth[1, x])

    loop(0, BX, update)


def body(right_side, iterate, state, classes, load_mask, fixed_mask):
    nx, ny, nz = (lax.axis_size(axis) for axis in ("gx", "gy", "gz"))
    pos = jnp.stack([lax.axis_index("gx"), lax.axis_index("gy"), lax.axis_index("gz")]).astype(jnp.int32)
    pos = jnp.concatenate([pos, jnp.array([nx, ny, nz], jnp.int32)])
    cells = (BX, BY, BZ)
    field = (3,) + cells
    wide = (ROWS, LANES)

    def slabs(n):
        return (n,) + wide

    def fields(n):
        return (3, n) + wide

    main, last, first = launch(
        4, prepare, [(11,) + cells, cells, cells], [field], [pos],
        far=[right_side, iterate, state, classes, load_mask, fixed_mask], copies=6)
    from_lower, from_upper = shift_along(last, "gz", 1), shift_along(first, "gz", -1)
    edge = (9, BX, BY // 2, BZ)
    packed, to_upper, to_lower = launch(4, pack_rows, [cells, edge, edge], [], [pos, main, from_lower, from_upper])
    from_lower, from_upper = shift_along(to_upper, "gy", 1), shift_along(to_lower, "gy", -1)
    sides = (SENT, ROWS, BZ)
    own, to_upper, to_lower = launch(
        14, pack_slabs, [(12, BX, ROWS, BZ), sides, sides],
        [slabs(BX)] * 3 + [fields(BX)] * 2 + [slabs(BX)] * 3 + [fields(BX)], [pos, main, packed, from_lower, from_upper])
    from_lower, from_upper = shift_along(to_upper, "gx", 1), shift_along(to_lower, "gx", -1)

    one, three = slabs(SLABS), fields(SLABS)
    quarters = (22, 8, BZ)
    coarse, low, high, v1, start, kx, ky, kz, inverse, u, weights, forward = launch(
        24, descend, [(44, 16, BZ), quarters, quarters],
        [three, three, one, one, one, three, three, one, fields(14), one, one, three, three, (ROWS, BZ), (44 * 16, BZ)],
        [pos, own, from_lower, from_upper],
        far_outs=[fields(18), fields(16), slabs(17)] + [slabs(16)] * 2 + [fields(16), fields(14), slabs(14), fields(14)],
        copies=9)
    smooth = launch(
        10, filter_iterate, [(2,) + cells], [fields(14), fields(14), slabs(14), slabs(12), slabs(12)], [pos],
        far=[u, forward, weights], copies=3,
        cost=pl.CostEstimate(flops=12_000_000, bytes_accessed=4_000_000, transcendentals=0))[0]

    from_lower, from_upper = shift_along(high, "gz", 1), shift_along(low, "gz", -1)
    coarse, center = launch(4, join_lanes, [(44, 16, BZ), (44, 8, BZ)], [], [pos, coarse, from_lower, from_upper])
    from_lower, from_upper = shift_along(center, "gy", 1), shift_along(center, "gy", -1)
    wide1 = (16, BZ)
    one1, three1 = (10,) + wide1, (3, 10) + wide1
    chunk = launch(
        4, level_one, [(ny, 24, BZ)], [one1] * 3 + [three1] * 5 + [(8, BZ), (40, BZ), (40, BZ)], [pos, coarse])[0]
    side = (32, 24, BZ)
    column = lax.all_to_all(chunk, "gy", 0, 0, tiled=True)
    to_upper, to_lower, center = launch(
        4, join_rows, [side, side], [(44, 24, BZ)], [pos, center, from_lower, from_upper],
        far_outs=[(44, 24, BZ)], copies=1)
    column = launch(8, pack_column, [(nx, 20 * ny, BZ)], [], [pos, column])[0]
    gathered = lax.all_to_all(column, "gx", 0, 0, tiled=True)
    from_lower, from_upper = shift_along(to_upper, "gx", 1), shift_along(to_lower, "gx", -1)

    wide1 = (24, BZ)
    one1, three1 = (18,) + wide1, (3, 18) + wide1
    wide2, wide3 = (4 * ny, BZ), (2 * ny, BZ)
    one2, three2 = (nx + 2,) + wide2, (3, nx + 2) + wide2
    one3, three3 = (nx + 2,) + wide3, (3, nx + 2) + wide3
    work = [one2, one2, three2] + [one2] * 4 + [three2] * 4 + [wide2, (5 * nx * 2 * ny, BZ)]
    work += [one3, one3, three3] + [one3] * 3 + [three3] * 3 + [(nx * 2 * ny, BZ)]
    parts = (9,) + cells
    far = [center, v1, start, kx, ky, kz, inverse]
    scratch = [x.shape for x in far] + [
        (3, nx + 4) + wide2, (15 * 4 * ny, LANES), wide1, three1, three1, (ROWS, BZ), (240, LANES), fields(16), fields(14), parts
    ] + [three1] * 2 + [one1] * 3 + [three1, one1, one1, three1, three1] + work
    sums, parts, precond = launch(
        30, functools.partial(ascend, nx=nx, ny=ny), [(8, BZ)], scratch, [pos, from_lower, from_upper, gathered],
        far_outs=[parts, fields(14)], far=far + [smooth], copies=10)
    ready = launch(
        12, filter_precond, [cells, field, parts.shape, smooth.shape], [fields(14), fields(14), slabs(14), slabs(12)], [pos],
        far=[iterate, parts, smooth, precond, forward, weights], copies=6, pin=True,
        cost=pl.CostEstimate(flops=8_000_000, bytes_accessed=4_000_000, transcendentals=0))
    total = lax.all_to_all(jnp.broadcast_to(sums[:1], (nx * ny, BZ)), ("gx", "gy"), 0, 0, tiled=True)
    total = jnp.sum(total, axis=0, keepdims=True)
    total = lax.all_to_all(jnp.broadcast_to(total, (nz, BZ)), "gz", 0, 0, tiled=True)
    return tuple(launch(4, finish, [field, field, cells], [], [pos, total, *ready]))


def solution(mesh):
    field, cells = P(None, "gx", "gy", "gz"), P("gx", "gy", "gz")
    return jax.shard_map(
        body,
        mesh=mesh,
        in_specs=(field, field, field, cells, cells, cells),
        out_specs=(field, field, cells),
        check_vma=False,
    )
```

```python
import functools
import math

import jax
import jax.numpy as jnp
from jax import lax
from jax.experimental import pallas as pl
from jax.experimental.pallas import tpu as pltpu
from jax.sharding import PartitionSpec as P

F32 = jnp.float32
FLOOR = 0.25
CLASSES = 16
PENALTY = 4.0
FIRST = 0.55
SECOND = 1.05
COARSE = 0.6
RADIUS = 3

BX, BY, BZ = 8, 16, 128
HALO = 7
SLABS = BX + 2 * HALO
ROWS = 2 * BY
LANES = 2 * BZ

PACKED = 8
ITERATE = ((0, 0, 7), (1, 7, 7), (2, 14, 7))
RHO = (3, 21, 7)
LOAD = ((4, 28, 6), (5, 34, 6), (6, 40, 6))
PEN = (7, 46, 6)
STATE = ((9, 52, 3), (10, 55, 3), (11, 58, 3))
FIELDS = ITERATE + (RHO,) + LOAD + (PEN,) + STATE
HALF = BZ // 2

MIB = 1024 * 1024


def iota(shape, dim):
    return lax.broadcasted_iota(jnp.int32, shape, dim)


def roll(x, shift, axis):
    return pltpu.roll(x, shift % x.shape[axis], axis)


def loop(lower, upper, step, unroll=4):
    def run(i, carry):
        step(i)
        return carry

    lax.fori_loop(lower, upper, run, 0, unroll=unroll)


def steps(lower, upper, step):
    loop(lower, upper, step, unroll=8)


def times(x, m):
    m = m.astype(jnp.bfloat16)
    high = x.astype(jnp.bfloat16)
    low = (x - high.astype(F32)).astype(jnp.bfloat16)
    return jnp.dot(high, m, preferred_element_type=F32) + jnp.dot(low, m, preferred_element_type=F32)


def matrix(shape, rule):
    return jnp.where(rule(iota(shape, 0), iota(shape, 1)), 1.0, 0.0).astype(F32)


def face(a, b):
    total = a + b
    both = (a > 0.0) & (b > 0.0)
    return jnp.where(both, 2.0 * a * b / jnp.where(both, total, 1.0), total)


def launch(limit, kernel, outs, scratch, operands, far_outs=(), far=(), copies=0, cost=None, pin=False):
    near_spec, far_spec = pl.BlockSpec(memory_space=pltpu.VMEM), pl.BlockSpec(memory_space=pltpu.HBM)
    specs = [pl.BlockSpec(memory_space=pltpu.SMEM)] + [near_spec] * (len(operands) - 1) + [far_spec] * len(far)
    return pl.pallas_call(
        kernel,
        out_shape=[pltpu.VMEM(shape, F32) if pin else jax.ShapeDtypeStruct(shape, F32) for shape in outs] + [pltpu.HBM(shape, F32) for shape in far_outs],
        in_specs=specs,
        out_specs=[near_spec] * len(outs) + [far_spec] * len(far_outs),
        scratch_shapes=[pltpu.VMEM(shape, F32) for shape in scratch] + ([pltpu.SemaphoreType.DMA((copies,))] if copies else []),
        compiler_params=pltpu.CompilerParams(vmem_limit_bytes=limit * MIB),
        cost_estimate=cost,
    )(*(operands[:1] + [pltpu.with_memory_space_constraint(x, pltpu.VMEM) for x in operands[1:]] if pin else operands), *[pltpu.with_memory_space_constraint(x, pltpu.HBM) for x in far])


def shift_along(x, axis, step):
    devices = lax.axis_size(axis)
    return lax.ppermute(x, axis, [(i, (i + step) % devices) for i in range(devices)])


def prepare(pos, right_far, iterate_far, state_far, classes_far, load_far, fixed_far, main, to_upper, to_lower, right, copied):
    def rest(classes, load_mask, fixed_mask):
        moves = [
            pltpu.make_async_copy(source, target, copied.at[i])
            for i, (source, target) in enumerate((
                (classes_far, classes), (load_far, load_mask), (fixed_far, fixed_mask), (right_far, right),
                (iterate_far, main.at[0:3]), (state_far, main.at[8:11])))
        ]
        for move in moves:
            move.start()
        for move in moves:
            move.wait()
        lane = iota((BY, BZ), 1)

        def slab(x):
            mask = load_mask[x].astype(F32)
            main[3, x] = FLOOR + (1.0 - FLOOR) * classes[x].astype(F32) / (CLASSES - 1)
            main[7, x] = PENALTY * fixed_mask[x].astype(F32)
            for c in range(3):
                main[4 + c, x] = right[c, x] * mask
            last = jnp.zeros((BY, BZ), F32)
            first = jnp.zeros((BY, BZ), F32)
            for tile, offset, width in FIELDS:
                value = main[tile if tile < PACKED else tile - 1, x]
                last = jnp.where((lane >= offset) & (lane < offset + width), roll(value, offset + width, 1), last)
                low = HALF + offset
                first = jnp.where((lane >= low) & (lane < low + width), roll(value, low, 1), first)
            to_upper[x] = last
            to_lower[x] = first

        loop(0, BX, slab)

    cells = pltpu.VMEM((BX, BY, BZ), jnp.int32)
    pl.run_scoped(rest, cells, cells, cells)


def pack_rows(pos, main, from_lower, from_upper, packed, to_upper, to_lower):
    below = jnp.where(pos[2] > 0, 1.0, 0.0)
    above = jnp.where(pos[2] < pos[5] - 1, 1.0, 0.0)
    lane = iota((BY, BZ), 1)
    row = iota((BY // 2, BZ), 0)
    half = BY // 2

    def slab(x):
        joined = jnp.where(lane < HALF, from_lower[x] * below, from_upper[x] * above)
        packed[x] = joined
        values = [joined if tile == PACKED else main[tile if tile < PACKED else tile - 1, x] for tile in range(12)]
        uppers = [value[half:] for value in values]
        lowers = [value[:half] for value in values]
        for c in range(3):
            up, down = uppers[9 + c], lowers[9 + c]
            uppers[LOAD[c][0]] = jnp.where(row < 2, roll(up, 3, 0), uppers[LOAD[c][0]])
            uppers[ITERATE[c][0]] = jnp.where(row < 1, roll(up, 1, 0), uppers[ITERATE[c][0]])
            lowers[LOAD[c][0]] = jnp.where(row >= 6, roll(down, 6, 0), lowers[LOAD[c][0]])
            lowers[ITERATE[c][0]] = jnp.where(row >= 7, roll(down, 5, 0), lowers[ITERATE[c][0]])
        for tile in range(9):
            to_upper[tile, x] = uppers[tile]
            to_lower[tile, x] = lowers[tile]

    loop(0, BX, slab)


def neighbours(field, c, s, kx, ky, kz, at=None):
    at = s if at is None else at
    v = field[c, s]
    x = kx[at] * field[c, s - 1] + kx[at + 1] * field[c, s + 1]
    y = ky[at] * roll(v, 1, 0) + roll(ky[at] * v, -1, 0)
    z = kz[at] * roll(v, 1, 1) + roll(kz[at] * v, -1, 1)
    return x + y + z + (x, y, z)[c]


def coefficients(stiff, pen, s, scale, kx, ky, kz, inverse, diagonal):
    e = stiff[s]
    upper = scale * face(e, stiff[s + 1])
    kx[s + 1] = upper
    y = scale * face(e, roll(e, 1, 0))
    ky[s] = y
    yp = roll(y, -1, 0)
    z = scale * face(e, roll(e, 1, 1))
    kz[s] = z
    zp = roll(z, -1, 1)
    pairs = (kx[s] + upper, y + yp, z + zp)
    total = pairs[0] + pairs[1] + pairs[2] + pen[s]
    for c in range(3):
        value = total + pairs[c]
        diagonal[c, s] = value
        if inverse is not None:
            inverse[c, s] = jnp.where(e > 0.0, 1.0 / jnp.where(e > 0.0, value, 1.0), 0.0)


def spread(value, packed, field, ref, at):
    _, offset, width = field
    lane = iota((ROWS, BZ), 1)
    ref[at + (slice(None), slice(0, BZ))] = value
    tail = jnp.where(lane >= BZ - width, roll(packed, BZ - width - offset, 1), 0.0)
    tail = jnp.where(lane < width, roll(packed, -(HALF + offset), 1), tail)
    ref[at + (slice(None), slice(BZ, LANES))] = tail


LAYERS = ((RHO[0], 7), (PACKED, 7)) + tuple((f[0], 6) for f in LOAD + (PEN,)) + tuple((f[0], 3) for f in ITERATE + STATE)
PLACE = {}
SENT = 0
for _tile, _count in LAYERS:
    PLACE[_tile] = SENT
    SENT += _count


def pack_slabs(pos, main, packed, from_lower, from_upper, own, to_upper, to_lower,
               rho, stiff, pen, u, load, kx, ky, kz, diagonal):
    below = jnp.where(pos[1] > 0, 1.0, 0.0)
    above = jnp.where(pos[1] < pos[4] - 1, 1.0, 0.0)
    row = iota((BY // 2, BZ), 0)

    def slab(x):
        for tile in range(12):
            value = packed[x] if tile == PACKED else main[tile if tile < PACKED else tile - 1, x]
            if tile <= PACKED:
                high, low = from_upper[tile, x], from_lower[tile, x]
            else:
                load_at, iterate_at = LOAD[tile - 9][0], ITERATE[tile - 9][0]
                high = jnp.where(row < 2, roll(from_upper[load_at, x], 2, 0), roll(from_upper[iterate_at, x], 3, 0))
                low = jnp.where(row < 7, roll(from_lower[load_at, x], 5, 0), roll(from_lower[iterate_at, x], 7, 0))
            own[tile, x] = jnp.concatenate([value, high * above, low * below], 0)

    loop(0, BX, slab)

    def expand(x):
        halo = own[PACKED, x]
        spread(own[RHO[0], x], halo, RHO, rho, (x,))
        spread(own[PEN[0], x], halo, PEN, pen, (x,))
        for c in range(3):
            spread(own[ITERATE[c][0], x], halo, ITERATE[c], u, (c, x))
            spread(own[LOAD[c][0], x], halo, LOAD[c], load, (c, x))
        stiff[x] = rho[x] * rho[x] * rho[x]

    loop(0, BX, expand)
    kx[1] = face(stiff[0], stiff[1])
    loop(1, BX - 1, lambda x: coefficients(stiff, pen, x, 1.0, kx, ky, kz, None, diagonal))
    lane = iota((ROWS, BZ), 1)

    def begin(x):
        halo = own[PACKED, x]
        for c in range(3):
            f = load[c, x] - (diagonal[c, x] * u[c, x] - neighbours(u, c, x, kx, ky, kz))
            tile, offset, width = LOAD[c]
            own[tile, x] = f[:, :BZ]
            tail = f[:, BZ:]
            halo = jnp.where((lane >= offset) & (lane < offset + width), roll(tail, offset + width, 1), halo)
            low = HALF + offset
            halo = jnp.where((lane >= low) & (lane < low + width), roll(tail, low, 1), halo)
        own[PACKED, x] = halo

    loop(1, BX - 1, begin)
    for tile, count in LAYERS:
        for j in range(count):
            to_upper[PLACE[tile] + j] = own[tile, BX - count + j]
            to_lower[PLACE[tile] + j] = own[tile, j]


def descend(pos, own, lower, upper, coarse, low_lanes, high_lanes, *rest):
    far, rest = rest[:9], rest[9:]
    (v1, start, kx, ky, kz, inverse, u, weights, forward, stiff, pen, diagonal, v0, half_rows, rows, copied) = rest
    moves = []

    def send(*pairs):
        for source, target in pairs:
            move = pltpu.make_async_copy(source, far[target], copied.at[target])
            move.start()
            moves.append(move)

    below = jnp.where(pos[0] > 0, 1.0, 0.0)
    above = jnp.where(pos[0] < pos[3] - 1, 1.0, 0.0)

    def expand(raw, s, fields):
        halo = raw(PACKED)
        for field, ref, at in fields:
            spread(raw(field[0]), halo, field, ref, at)

    def densities(s):
        return [(RHO, weights, (s,))]

    def loads(s):
        return [(PEN, pen, (s,))] + [(LOAD[c], start, (c, s)) for c in range(3)]

    def motions(s):
        return [(ITERATE[c], u, (c, s)) for c in range(3)] + [(STATE[c], forward, (c, s - 4)) for c in range(3)]

    def lower_raw(s):
        return lambda t: lower[PLACE[t] + s - (HALO - dict(LAYERS)[t])] * below

    def upper_raw(s):
        return lambda t: upper[PLACE[t] + s - (HALO + BX)] * above

    after = HALO + BX
    loop(0, HALO, lambda s: expand(lower_raw(s), s, densities(s)))
    loop(1, HALO, lambda s: expand(lower_raw(s), s, loads(s)))
    loop(4, HALO, lambda s: expand(lower_raw(s), s, motions(s)))
    loop(HALO, after, lambda s: expand(lambda t: own[t, s - HALO], s, densities(s) + loads(s) + motions(s)))
    loop(after, after + 7, lambda s: expand(upper_raw(s), s, densities(s)))
    loop(after, after + 6, lambda s: expand(upper_raw(s), s, loads(s)))
    loop(after, after + 3, lambda s: expand(upper_raw(s), s, motions(s)))
    send((u.at[:, 4:18], 6), (weights.at[4:18], 7), (forward, 8))

    def cube(s):
        rho = weights[s]
        stiff[s] = rho * rho * rho

    loop(0, SLABS, cube)
    kx[1] = face(stiff[0], stiff[1])

    def prepare_slab(s):
        coefficients(stiff, pen, s, 1.0, kx, ky, kz, inverse, diagonal)
        for c in range(3):
            v0[c, s] = FIRST * start[c, s] * inverse[c, s]

    loop(1, SLABS - 1, prepare_slab)
    faces = (kx, ky, kz)
    send((kx.at[3:20], 2), (ky.at[3:19], 3), (kz.at[3:19], 4), (inverse.at[:, 3:19], 5))

    for s in (HALO - 1, HALO, HALO + BX - 1, HALO + BX):
        for c in range(3):
            start[c, s] = start[c, s] - (diagonal[c, s] * u[c, s] - neighbours(u, c, s, *faces))
            v0[c, s] = FIRST * start[c, s] * inverse[c, s]
    send((start.at[:, 3:19], 1))

    def sweep(s):
        for c in range(3):
            v1[c, s] = (1.0 - SECOND) * v0[c, s] + SECOND * inverse[c, s] * (start[c, s] + neighbours(v0, c, s, *faces))

    loop(2, SLABS - 2, sweep)
    send((v1.at[:, 2:20], 0))

    def remainder(c, s):
        r = start[c, s] - diagonal[c, s] * v1[c, s] + neighbours(v1, c, s, *faces)
        return r[:, :BZ]

    def gather_rows(at, value):
        half_rows[...] = value
        n = ROWS // 2
        rows[pl.ds(pl.multiple_of(at * n, n), n), :] = half_rows[pl.ds(0, n, stride=2), :] + half_rows[pl.ds(1, n, stride=2), :]

    def pair(i):
        for c in range(3):
            gather_rows(c * 8 + i, remainder(c, 3 + 2 * i) + remainder(c, 4 + 2 * i))

    loop(0, 8, pair)

    def pair_up(i):
        s = 1 + 2 * i
        gather_rows(24 + i, (stiff[s] + stiff[s + 1])[:, :BZ] * 0.125)
        gather_rows(34 + i, (pen[s] + pen[s + 1])[:, :BZ])

    loop(0, 10, pair_up)
    halve = matrix((BZ, BZ), lambda l, k: (l >> 1) == (k & (HALF - 1)))
    coarse[...] = times(rows[...], halve).reshape(44, 16, BZ)
    quarter = iota((8, BZ), 1) >> 5

    def pack(g):
        for h in range(2):
            low = jnp.zeros((8, BZ), F32)
            high = jnp.zeros((8, BZ), F32)
            for q in range(4):
                value = coarse[4 * g + q, 8 * h:8 * h + 8]
                turned = roll(value, 32, 1)
                one, two = (value, turned) if q % 2 == 0 else (turned, value)
                low = jnp.where(quarter == q, one, low)
                high = jnp.where(quarter == q, two, high)
            low_lanes[2 * g + h] = low
            high_lanes[2 * g + h] = high

    loop(0, 11, pack)
    for move in moves:
        move.wait()


def join_lanes(pos, coarse, from_lower, from_upper, out, center):
    below = jnp.where(pos[2] > 0, 1.0, 0.0)
    above = jnp.where(pos[2] < pos[5] - 1, 1.0, 0.0)
    lane = iota((8, BZ), 1)

    def unpack(g):
        for h in range(2):
            low, high = from_lower[2 * g + h] * below, from_upper[2 * g + h] * above
            for q in range(4):
                halo = jnp.where(lane < 96, roll(high, 64 - 32 * q, 1), roll(low, 96 - 32 * q, 1))
                value = jnp.where(lane < 64, coarse[4 * g + q, 8 * h:8 * h + 8], halo)
                out[4 * g + q, 8 * h:8 * h + 8] = value
                if h == 0:
                    center[4 * g + q] = value

    loop(0, 11, unpack)


def join_rows(pos, coarse, from_lower, from_upper, to_upper, to_lower, center, out, copied):
    below = jnp.where(pos[1] > 0, 1.0, 0.0)
    above = jnp.where(pos[1] < pos[4] - 1, 1.0, 0.0)

    def join(i):
        out[i] = jnp.concatenate([coarse[i], from_upper[i] * above, from_lower[i] * below], 0)

    loop(0, 44, join)
    move = pltpu.make_async_copy(out, center, copied.at[0])
    move.start()
    at = 0
    for base, count in ((0, 6), (8, 6), (16, 6), (24, 7), (34, 7)):
        shift = 2 if count == 6 else 3
        for j in range(count):
            to_upper[at] = out[base + j]
            to_lower[at] = out[base + shift + j]
            at += 1
    move.wait()


def smooth_down(slabs, f, v0, v1, inverse, faces):
    def begin(s):
        for c in range(3):
            v0[c, s] = FIRST * f[c, s] * inverse[c, s]

    steps(1, slabs - 1, begin)

    def sweep(s):
        for c in range(3):
            v1[c, s] = (1.0 - SECOND) * v0[c, s] + SECOND * inverse[c, s] * (f[c, s] + neighbours(v0, c, s, *faces))

    steps(2, slabs - 2, sweep)


def level_one(pos, own, chunk, kx, ky, kz, inverse, diagonal, f, v0, v1, half_rows, rows, wide):
    stiff, pen = own.at[24:34], own.at[34:44]
    slabs = 10
    for c in range(3):
        for i in range(8):
            f[c, 1 + i] = own[8 * c + i]
    kx[1] = 2.0 * face(stiff[0], stiff[1])
    steps(1, slabs - 1, lambda s: coefficients(stiff, pen, s, 2.0, kx, ky, kz, inverse, diagonal))
    faces = (kx, ky, kz)
    smooth_down(slabs, f, v0, v1, inverse, faces)

    def gather_rows(at, value):
        half_rows[...] = value
        rows[pl.ds(at * 4, 4), :] = half_rows[pl.ds(0, 4, stride=2), :] + half_rows[pl.ds(1, 4, stride=2), :]

    for i in range(2):
        s = 3 + 2 * i
        for c in range(3):
            total = 0.0
            for at in (s, s + 1):
                total = total + (f[c, at] - diagonal[c, at] * v1[c, at] + neighbours(v1, c, at, *faces))[:8]
            gather_rows(2 * c + i, total)
        gather_rows(6 + i, (stiff[s] + stiff[s + 1])[:8] * 0.125)
        gather_rows(8 + i, (pen[s] + pen[s + 1])[:8])

    def rule(j, k):
        z = jnp.where(j < 96, j, j - BZ)
        return (z >> 1) == (k & 63) - 16

    wide[...] = times(rows[...], matrix((BZ, BZ), rule))
    lane = iota((4, BZ), 1)
    parts = [jnp.where(lane < 64, wide[8 * field:8 * field + 4], wide[8 * field + 4:8 * field + 8]) for field in range(5)]
    value = jnp.concatenate(parts + [jnp.zeros((4, BZ), F32)], 0)
    for i in range(chunk.shape[0]):
        chunk[i] = value


def pack_column(pos, column, out):
    for i in range(out.shape[0]):
        for j in range(column.shape[0]):
            out[i, 20 * j:20 * j + 20] = column[j, 0:20]


def level_one_again(pos, own, lower, upper, v1, f, kx, ky, kz, inverse, stiff, pen, diagonal, v0):
    below = jnp.where(pos[0] > 0, 1.0, 0.0)
    above = jnp.where(pos[0] < pos[3] - 1, 1.0, 0.0)
    slabs = 18
    for field, at in ((stiff, 0), (pen, 1)):
        for j in range(7):
            field[j] = lower[18 + 7 * at + j] * below
            field[11 + j] = upper[18 + 7 * at + j] * above
        for j in range(4):
            field[7 + j] = own[24 + 10 * at + 3 + j]
    for c in range(3):
        for j in range(6):
            f[c, 1 + j] = lower[6 * c + j] * below
            f[c, 11 + j] = upper[6 * c + j] * above
        for j in range(4):
            f[c, 7 + j] = own[8 * c + 2 + j]
    kx[1] = 2.0 * face(stiff[0], stiff[1])
    steps(1, slabs - 1, lambda s: coefficients(stiff, pen, s, 2.0, kx, ky, kz, inverse, diagonal))
    smooth_down(slabs, f, v0, v1, inverse, (kx, ky, kz))


def coarse_levels(pos, gathered, out, nx, ny, work):
    (e2, p2, f2, kxm, kxp, kym, kzm, iv, dg, va, vb, tall, rows3, e3, p3, f3, jx, jym, jz, iv3, wa, wb, rows2) = work
    ys = 4 * ny
    pairs = nx
    lane = iota((ys, BZ), 1)
    row = iota((ys, BZ), 0)
    even = lane < 64
    zero = jnp.zeros((ys, BZ), F32)
    for field in (e2, p2):
        field[0] = zero
        field[pairs + 1] = zero
    for c in range(3):
        for field in (va, vb):
            field[c, 0] = zero
            field[c, pairs + 1] = zero

    def collect(g):
        for field in range(5):
            for yy in range(ny):
                value = gathered[g, 20 * yy + 4 * field:20 * yy + 4 * field + 4, :]
                if field < 3:
                    f2[field, g + 1, pl.ds(4 * yy, 4), :] = value
                else:
                    (e2, p2)[field - 3][g + 1, pl.ds(4 * yy, 4), :] = value

    steps(0, pairs, collect)

    def x_neighbours(below, mid, above):
        swapped = roll(mid, 64, 1)
        return jnp.where(even, roll(below, 64, 1), swapped), jnp.where(even, swapped, roll(above, 64, 1))

    def coefs(s):
        e = e2[s]
        xm, xp = x_neighbours(e2[s - 1], e, e2[s + 1])
        ym = jnp.where(row == 0, 0.0, roll(e, 1, 0))
        yp = jnp.where(row == ys - 1, 0.0, roll(e, -1, 0))
        a, b = 4.0 * face(e, xm), 4.0 * face(e, xp)
        c0, d = 4.0 * face(e, ym), 4.0 * face(e, yp)
        z = 4.0 * face(e, roll(e, 1, 1))
        zp = roll(z, -1, 1)
        kxm[s] = a
        kxp[s] = b
        kym[s] = jnp.where(row == 0, 0.0, c0)
        kzm[s] = z
        sums = (a + b, c0 + d, z + zp)
        total = sums[0] + sums[1] + sums[2] + p2[s]
        for c in range(3):
            value = total + sums[c]
            dg[c, s] = value
            iv[c, s] = jnp.where(e > 0.0, 1.0 / jnp.where(e > 0.0, value, 1.0), 0.0)
            va[c, s] = FIRST * f2[c, s] * iv[c, s]

    steps(1, pairs + 1, coefs)

    def around(v, c, s):
        mid = v[c, s]
        below, above = x_neighbours(v[c, s - 1], mid, v[c, s + 1])
        x = kxm[s] * below + kxp[s] * above
        y = kym[s] * roll(mid, 1, 0) + roll(kym[s] * mid, -1, 0)
        z = kzm[s] * roll(mid, 1, 1) + roll(kzm[s] * mid, -1, 1)
        return x + y + z + (x, y, z)[c]

    def sweep(source, target, weight):
        def step(s):
            for c in range(3):
                target[c, s] = (1.0 - weight) * source[c, s] + weight * iv[c, s] * (f2[c, s] + around(source, c, s))

        steps(1, pairs + 1, step)

    sweep(va, vb, SECOND)
    n3 = ys // 2

    def gather_rows(at, value):
        tall[...] = value
        rows3[pl.ds(pl.multiple_of(at * n3, 8), n3), :] = tall[pl.ds(0, n3, stride=2), :] + tall[pl.ds(1, n3, stride=2), :]

    def reduce(s):
        for c in range(3):
            gather_rows(c * pairs + s - 1, f2[c, s] - dg[c, s] * vb[c, s] + around(vb, c, s))
        gather_rows(3 * pairs + s - 1, e2[s] * 0.125)
        gather_rows(4 * pairs + s - 1, p2[s])

    steps(1, pairs + 1, reduce)
    down = matrix((BZ, BZ), lambda l, k: ((l & 63) >> 1) == (k & 31))
    rows3[...] = times(rows3[...], down)
    row3 = iota((n3, BZ), 0)
    zero3 = jnp.zeros((n3, BZ), F32)

    def third(at):
        return rows3[pl.ds(pl.multiple_of(at * n3, 8), n3), :]

    e3[0] = zero3
    e3[pairs + 1] = zero3
    for c in range(3):
        for field in (wa, wb):
            field[c, 0] = zero3
            field[c, pairs + 1] = zero3

    def place(s):
        e3[s] = third(3 * pairs + s - 1)

    steps(1, pairs + 1, place)

    def coefs3(s):
        e = e3[s]
        a, b = 8.0 * face(e, e3[s - 1]), 8.0 * face(e, e3[s + 1])
        c0 = 8.0 * face(e, jnp.where(row3 == 0, 0.0, roll(e, 1, 0)))
        d = 8.0 * face(e, jnp.where(row3 == n3 - 1, 0.0, roll(e, -1, 0)))
        z = 8.0 * face(e, roll(e, 1, 1))
        zp = roll(z, -1, 1)
        jx[s] = a
        jx[s + 1] = b
        jym[s] = jnp.where(row3 == 0, 0.0, c0)
        jz[s] = z
        sums = (a + b, c0 + d, z + zp)
        total = sums[0] + sums[1] + sums[2] + third(4 * pairs + s - 1)
        for c in range(3):
            value = total + sums[c]
            iv3[c, s] = jnp.where(e > 0.0, 1.0 / jnp.where(e > 0.0, value, 1.0), 0.0)
            wa[c, s] = COARSE * third(c * pairs + s - 1) * iv3[c, s]

    steps(1, pairs + 1, coefs3)
    source, target = wa, wb
    for sweep_at in range(3):
        def step(s, source=source, target=target):
            for c in range(3):
                near = neighbours(source, c, s, jx, jym, jz)
                target[c, s] = (1.0 - COARSE) * source[c, s] + COARSE * iv3[c, s] * (third(c * pairs + s - 1) + near)

        steps(1, pairs + 1, step)
        source, target = target, source
    up = matrix((BZ, BZ), lambda k, l: k == ((l & 63) >> 1))
    for c in range(3):
        rows2[...] = times(source[c, 1:pairs + 1].reshape(pairs * n3, BZ), up)

        def add(s, c=c):
            value = rows2[pl.ds(pl.multiple_of((s - 1) * n3, 8), n3), :]
            tall[pl.ds(0, n3, stride=2), :] = value
            tall[pl.ds(1, n3, stride=2), :] = value
            vb[c, s] = vb[c, s] + jnp.where(iv[c, s] > 0.0, tall[...], 0.0)

        steps(1, pairs + 1, add)
    sweep(vb, va, SECOND)

    for c in range(3):
        for at in (0, 1, pairs + 2, pairs + 3):
            out[c, at] = zero

    def last(s):
        for c in range(3):
            out[c, s + 1] = (1.0 - FIRST) * va[c, s] + FIRST * iv[c, s] * (f2[c, s] + around(va, c, s))

    steps(1, pairs + 1, last)


def ascend(pos, lower, upper, gathered, *rest, nx, ny):
    far, (sums, parts, precond_far), rest = rest[:7], rest[8:11], rest[11:]
    near, rest = rest[:7], rest[7:]
    e2out, window, rows24, va1, vb1, rows32, spread, vb, precond, held = rest[:10]
    v1, f1, kx1, ky1, kz1, inverse1, stiff1, pen1, diagonal1, v01 = rest[10:20]
    work, copied = rest[20:-1], rest[-1]
    center = near[0]
    va, start, kx, ky, kz, inverse = near[1:]
    arrivals = [pltpu.make_async_copy(source, target, copied.at[i]) for i, (source, target) in enumerate(zip(far, near))]
    for move in arrivals:
        move.start()
    departures = []

    def send(source, target):
        move = pltpu.make_async_copy(source, target, copied.at[7 + len(departures)])
        move.start()
        departures.append(move)

    coarse_levels(pos, gathered, e2out, nx, ny, work)
    arrivals[0].wait()
    level_one_again(
        pos, center, lower, upper, v1, f1, kx1, ky1, kz1, inverse1, stiff1, pen1, diagonal1, v01)
    gx, gy = pos[0], pos[1]
    ys = 4 * ny
    turn = lax.rem(ys - 4 * gy, ys)

    def rule(k, j):
        z = jnp.where((j & 127) < 96, j & 127, (j & 127) - BZ)
        return k == 64 * (j >> 7) + (z >> 1) + 16

    grow = matrix((BZ, LANES), rule)
    for c in range(3):
        for j in range(5):
            window[pl.ds((5 * c + j) * ys, ys), :] = times(pltpu.roll(e2out[c, gx + j], turn, 0), grow)
    for c in range(3):
        for s in range(2, 16):
            x2 = (s - 7) // 2
            j, part = (x2 + 4) // 2, (x2 + 4) % 2
            base = (5 * c + j) * ys
            cols = slice(128 * part, 128 * part + 128)
            if s % 2 == 1 or s == 2:
                low = window[base:base + 8, cols]
                high = window[base + ys - 4:base + ys, cols]
                for at in (0, 1):
                    rows24[pl.ds(at, 8, stride=2), :] = low
                    rows24[pl.ds(16 + at, 4, stride=2), :] = high
            va1[c, s] = v1[c, s] + jnp.where(inverse1[c, s] > 0.0, rows24[...], 0.0)
    faces1 = (kx1, ky1, kz1)

    def sweep1(source, target, weight, lower, upper):
        def step(s):
            for c in range(3):
                target[c, s] = (1.0 - weight) * source[c, s] + weight * inverse1[c, s] * (
                    f1[c, s] + neighbours(source, c, s, *faces1))

        steps(lower, upper, step)

    sweep1(va1, vb1, SECOND, 3, 15)
    sweep1(vb1, va1, FIRST, 4, 14)
    grow0 = matrix((BZ, LANES), lambda j, l: j == (l >> 1))
    for move in arrivals[1:]:
        move.wait()
    for c in range(3):
        spread[...] = times(va1[c, 4:14].reshape(240, BZ), grow0)
        for i in range(10):
            for half in (0, 1):
                cols = slice(BZ * half, BZ * half + BZ)
                value = spread[24 * i:24 * i + 24, cols]
                for at in (0, 1):
                    rows32[pl.ds(at, 12, stride=2), :] = value[:12]
                    rows32[pl.ds(24 + at, 4, stride=2), :] = value[20:]
                for s in (2 * i - 1, 2 * i):
                    if 0 <= s < 18:
                        va[c, s, :, cols] = va[c, s, :, cols] + rows32[...]
    faces = (kx, ky, kz)

    def sweep_one(t):
        for c in range(3):
            vb[c, t] = (1.0 - SECOND) * va[c, t + 1] + SECOND * inverse[c, t] * (
                start[c, t] + neighbours(va, c, t + 1, *faces, at=t))

    loop(0, 16, sweep_one)

    def sweep_two(t):
        for c in range(3):
            precond[c, t - 1] = (1.0 - FIRST) * vb[c, t] + FIRST * inverse[c, t] * (start[c, t] + neighbours(vb, c, t, *faces))

    loop(1, 15, sweep_two)

    def keep(x):
        for c in range(3):
            held[c, x] = precond[c, x + 3][:BY, :BZ]
            held[3 + c, x] = start[c, x + 4][:BY, :BZ]

    loop(0, BX, keep)
    send(held.at[0:6], parts.at[0:6])
    send(precond, precond_far)

    def inner(x, carry):
        one, two = carry
        for c in range(3):
            mid = held[c, x]
            value = mid / inverse[c, x + 4][:BY, :BZ] - neighbours(precond, c, x + 3, *faces, at=x + 4)[:BY, :BZ]
            held[6 + c, x] = value
            one = one + held[3 + c, x] * mid
            two = two + mid * value
        return one, two

    zero = jnp.zeros((BY, BZ), F32)
    one, two = lax.fori_loop(0, BX, inner, (zero, zero), unroll=4)
    send(held.at[6:9], parts.at[6:9])
    lane = iota((8, BZ), 1)
    sums[...] = jnp.where(lane == 0, jnp.sum(one), jnp.where(lane == 1, jnp.sum(two), 0.0))
    for move in departures:
        move.wait()


def distance_weight(square):
    return max(RADIUS - math.sqrt(square), 0.0)


def sensitivity(state, field, weights, term):
    def energy(i):
        s = i + 1
        total = jnp.zeros((ROWS, LANES), F32)
        sums = [0.0, 0.0]
        for c in range(3):
            a, b = state[c, s], field[c, s]
            x = (a - state[c, s - 1]) * (b - field[c, s - 1]) + (a - state[c, s + 1]) * (b - field[c, s + 1])
            total = total + (x + x if c == 0 else x)
            for axis in (0, 1):
                part = (a - roll(a, 1, axis)) * (b - roll(b, 1, axis))
                sums[axis] = sums[axis] + (part + part if c == axis + 1 else part)
        for axis in (0, 1):
            total = total + sums[axis] + roll(sums[axis], -1, axis)
        rho = weights[s]
        term[i] = rho * (-3.0 * rho * rho * (0.5 * total))

    loop(0, BX + 4, energy)


def weigh(field, x):
    classes = {}
    for a in range(-2, 3):
        t = field[x + 2 + a]
        for b, value in ((0, t), (1, roll(t, 1, 0) + roll(t, -1, 0)), (2, roll(t, 2, 0) + roll(t, -2, 0))):
            q = a * a + b * b
            classes[q] = value if q not in classes else classes[q] + value
    parts = []
    for z in (0, 1, 2):
        part = None
        for q, value in classes.items():
            w = distance_weight(q + z * z)
            if w > 0.0:
                part = w * value if part is None else part + w * value
        parts.append(part)
    result = parts[0] + roll(parts[1], 1, 1) + roll(parts[1], -1, 1) + roll(parts[2], 2, 1) + roll(parts[2], -2, 1)
    return result[:BY, :BZ]


def arrive(far, near, copied):
    moves = [pltpu.make_async_copy(source, target, copied.at[i]) for i, (source, target) in enumerate(zip(far, near))]
    for move in moves:
        move.start()
    for move in moves:
        move.wait()


def filter_iterate(pos, *rest):
    far, out, near, (term, inside, copied) = rest[:3], rest[3], rest[4:7], rest[7:]
    arrive(far, near, copied)
    iterate, state, weights = near
    sensitivity(state, iterate, weights, term)

    def mark(i):
        inside[i] = jnp.where(weights[i + 1] > 0.0, 1.0, 0.0)

    loop(0, BX + 4, mark)

    def smooth(x):
        factor = 1.0 / (weights[x + 3][:BY, :BZ] * weigh(inside, x))
        out[0, x] = factor * weigh(term, x)
        out[1, x] = factor

    loop(0, BX, smooth)


def filter_precond(pos, *rest):
    far, out, near, (term, copied) = rest[:6], rest[6], rest[7:13], rest[13:]
    moves = [pltpu.make_async_copy(source, target, copied.at[i]) for i, (source, target) in enumerate(zip(far, near))]
    for move in moves[3:] + moves[:3]:
        move.start()
    for move in moves[3:]:
        move.wait()
    precond, state, weights = near[3:]
    sensitivity(state, precond, weights, term)

    def smooth(x):
        out[x] = weigh(term, x)

    loop(0, BX, smooth)
    for move in moves[:3]:
        move.wait()


def finish(pos, totals, *rest):
    second, iterate, parts, smooth, solution, residual, filtered = rest
    total = jnp.sum(totals[...], axis=0, keepdims=True)
    lane = iota((1, BZ), 1)
    one = jnp.sum(jnp.where(lane == 0, total, 0.0), axis=1, keepdims=True)
    two = jnp.sum(jnp.where(lane == 1, total, 0.0), axis=1, keepdims=True)
    alpha = one / two

    def update(x):
        for c in range(3):
            solution[c, x] = iterate[c, x] + alpha * parts[c, x]
            residual[c, x] = parts[3 + c, x] - alpha * parts[6 + c, x]
        filtered[x] = smooth[0, x] + alpha * (second[x] * smooth[1, x])

    loop(0, BX, update)


def body(right_side, iterate, state, classes, load_mask, fixed_mask):
    nx, ny, nz = (lax.axis_size(axis) for axis in ("gx", "gy", "gz"))
    pos = jnp.stack([lax.axis_index("gx"), lax.axis_index("gy"), lax.axis_index("gz")]).astype(jnp.int32)
    pos = jnp.concatenate([pos, jnp.array([nx, ny, nz], jnp.int32)])
    cells = (BX, BY, BZ)
    field = (3,) + cells
    wide = (ROWS, LANES)

    def slabs(n):
        return (n,) + wide

    def fields(n):
        return (3, n) + wide

    main, last, first = launch(
        4, prepare, [(11,) + cells, cells, cells], [field], [pos],
        far=[right_side, iterate, state, classes, load_mask, fixed_mask], copies=6)
    from_lower, from_upper = shift_along(last, "gz", 1), shift_along(first, "gz", -1)
    edge = (9, BX, BY // 2, BZ)
    packed, to_upper, to_lower = launch(4, pack_rows, [cells, edge, edge], [], [pos, main, from_lower, from_upper])
    from_lower, from_upper = shift_along(to_upper, "gy", 1), shift_along(to_lower, "gy", -1)
    sides = (SENT, ROWS, BZ)
    own, to_upper, to_lower = launch(
        14, pack_slabs, [(12, BX, ROWS, BZ), sides, sides],
        [slabs(BX)] * 3 + [fields(BX)] * 2 + [slabs(BX)] * 3 + [fields(BX)], [pos, main, packed, from_lower, from_upper])
    from_lower, from_upper = shift_along(to_upper, "gx", 1), shift_along(to_lower, "gx", -1)

    one, three = slabs(SLABS), fields(SLABS)
    quarters = (22, 8, BZ)
    coarse, low, high, v1, start, kx, ky, kz, inverse, u, weights, forward = launch(
        24, descend, [(44, 16, BZ), quarters, quarters],
        [three, three, one, one, one, three, three, one, fields(14), one, one, three, three, (ROWS, BZ), (44 * 16, BZ)],
        [pos, own, from_lower, from_upper],
        far_outs=[fields(18), fields(16), slabs(17)] + [slabs(16)] * 2 + [fields(16), fields(14), slabs(14), fields(14)],
        copies=9)
    smooth = launch(
        10, filter_iterate, [(2,) + cells], [fields(14), fields(14), slabs(14), slabs(12), slabs(12)], [pos],
        far=[u, forward, weights], copies=3,
        cost=pl.CostEstimate(flops=12_000_000, bytes_accessed=4_000_000, transcendentals=0))[0]

    from_lower, from_upper = shift_along(high, "gz", 1), shift_along(low, "gz", -1)
    coarse, center = launch(4, join_lanes, [(44, 16, BZ), (44, 8, BZ)], [], [pos, coarse, from_lower, from_upper])
    from_lower, from_upper = shift_along(center, "gy", 1), shift_along(center, "gy", -1)
    wide1 = (16, BZ)
    one1, three1 = (10,) + wide1, (3, 10) + wide1
    chunk = launch(
        4, level_one, [(ny, 24, BZ)], [one1] * 3 + [three1] * 5 + [(8, BZ), (40, BZ), (40, BZ)], [pos, coarse])[0]
    side = (32, 24, BZ)
    column = lax.all_to_all(chunk, "gy", 0, 0, tiled=True)
    to_upper, to_lower, center = launch(
        4, join_rows, [side, side], [(44, 24, BZ)], [pos, center, from_lower, from_upper],
        far_outs=[(44, 24, BZ)], copies=1)
    column = launch(8, pack_column, [(nx, 20 * ny, BZ)], [], [pos, column])[0]
    gathered = lax.all_to_all(column, "gx", 0, 0, tiled=True)
    from_lower, from_upper = shift_along(to_upper, "gx", 1), shift_along(to_lower, "gx", -1)

    wide1 = (24, BZ)
    one1, three1 = (18,) + wide1, (3, 18) + wide1
    wide2, wide3 = (4 * ny, BZ), (2 * ny, BZ)
    one2, three2 = (nx + 2,) + wide2, (3, nx + 2) + wide2
    one3, three3 = (nx + 2,) + wide3, (3, nx + 2) + wide3
    work = [one2, one2, three2] + [one2] * 4 + [three2] * 4 + [wide2, (5 * nx * 2 * ny, BZ)]
    work += [one3, one3, three3] + [one3] * 3 + [three3] * 3 + [(nx * 2 * ny, BZ)]
    parts = (9,) + cells
    far = [center, v1, start, kx, ky, kz, inverse]
    scratch = [x.shape for x in far] + [
        (3, nx + 4) + wide2, (15 * 4 * ny, LANES), wide1, three1, three1, (ROWS, BZ), (240, LANES), fields(16), fields(14), parts
    ] + [three1] * 2 + [one1] * 3 + [three1, one1, one1, three1, three1] + work
    sums, parts, precond = launch(
        30, functools.partial(ascend, nx=nx, ny=ny), [(8, BZ)], scratch, [pos, from_lower, from_upper, gathered],
        far_outs=[parts, fields(14)], far=far + [smooth], copies=10)
    ready = launch(
        12, filter_precond, [cells, field, parts.shape, smooth.shape], [fields(14), fields(14), slabs(14), slabs(12)], [pos],
        far=[iterate, parts, smooth, precond, forward, weights], copies=6, pin=True,
        cost=pl.CostEstimate(flops=8_000_000, bytes_accessed=4_000_000, transcendentals=0))
    total = lax.all_to_all(jnp.broadcast_to(sums[:1], (nx * ny, BZ)), ("gx", "gy"), 0, 0, tiled=True)
    total = jnp.sum(total, axis=0, keepdims=True)
    total = lax.all_to_all(jnp.broadcast_to(total, (nz, BZ)), "gz", 0, 0, tiled=True)
    return tuple(launch(4, finish, [field, field, cells], [], [pos, total, *ready]))


def solution(mesh):
    field, cells = P(None, "gx", "gy", "gz"), P("gx", "gy", "gz")
    return jax.shard_map(
        body,
        mesh=mesh,
        in_specs=(field, field, field, cells, cells, cells),
        out_specs=(field, field, cells),
        check_vma=False,
    )
```

```python
import functools
import math

import jax
import jax.numpy as jnp
from jax import lax
from jax.experimental import pallas as pl
from jax.experimental.pallas import tpu as pltpu
from jax.sharding import PartitionSpec as P

F32 = jnp.float32
FLOOR = 0.25
CLASSES = 16
PENALTY = 4.0
FIRST = 0.55
SECOND = 1.05
COARSE = 0.6
RADIUS = 3

BX, BY, BZ = 8, 16, 128
HALO = 7
SLABS = BX + 2 * HALO
ROWS = 2 * BY
LANES = 2 * BZ

PACKED = 8
ITERATE = ((0, 0, 7), (1, 7, 7), (2, 14, 7))
RHO = (3, 21, 7)
LOAD = ((4, 28, 6), (5, 34, 6), (6, 40, 6))
PEN = (7, 46, 6)
STATE = ((9, 52, 3), (10, 55, 3), (11, 58, 3))
FIELDS = ITERATE + (RHO,) + LOAD + (PEN,) + STATE
HALF = BZ // 2

MIB = 1024 * 1024


def iota(shape, dim):
    return lax.broadcasted_iota(jnp.int32, shape, dim)


def roll(x, shift, axis):
    return pltpu.roll(x, shift % x.shape[axis], axis)


def loop(lower, upper, step, unroll=4):
    def run(i, carry):
        step(i)
        return carry

    lax.fori_loop(lower, upper, run, 0, unroll=unroll)


def steps(lower, upper, step):
    loop(lower, upper, step, unroll=8)


def times(x, m):
    m = m.astype(jnp.bfloat16)
    high = x.astype(jnp.bfloat16)
    low = (x - high.astype(F32)).astype(jnp.bfloat16)
    return jnp.dot(high, m, preferred_element_type=F32) + jnp.dot(low, m, preferred_element_type=F32)


def matrix(shape, rule):
    return jnp.where(rule(iota(shape, 0), iota(shape, 1)), 1.0, 0.0).astype(F32)


def face(a, b):
    total = a + b
    both = (a > 0.0) & (b > 0.0)
    return jnp.where(both, 2.0 * a * b / jnp.where(both, total, 1.0), total)


def launch(limit, kernel, outs, scratch, operands, far_outs=(), far=(), copies=0, cost=None, pin=False):
    near_spec, far_spec = pl.BlockSpec(memory_space=pltpu.VMEM), pl.BlockSpec(memory_space=pltpu.HBM)
    specs = [pl.BlockSpec(memory_space=pltpu.SMEM)] + [near_spec] * (len(operands) - 1) + [far_spec] * len(far)
    return pl.pallas_call(
        kernel,
        out_shape=[pltpu.VMEM(shape, F32) if pin else jax.ShapeDtypeStruct(shape, F32) for shape in outs] + [pltpu.HBM(shape, F32) for shape in far_outs],
        in_specs=specs,
        out_specs=[near_spec] * len(outs) + [far_spec] * len(far_outs),
        scratch_shapes=[pltpu.VMEM(shape, F32) for shape in scratch] + ([pltpu.SemaphoreType.DMA((copies,))] if copies else []),
        compiler_params=pltpu.CompilerParams(vmem_limit_bytes=limit * MIB),
        cost_estimate=cost,
    )(*(operands[:1] + [pltpu.with_memory_space_constraint(x, pltpu.VMEM) for x in operands[1:]] if pin else operands), *[pltpu.with_memory_space_constraint(x, pltpu.HBM) for x in far])


def shift_along(x, axis, step):
    devices = lax.axis_size(axis)
    return lax.ppermute(x, axis, [(i, (i + step) % devices) for i in range(devices)])


def prepare(pos, right_far, iterate_far, state_far, classes_far, load_far, fixed_far, main, to_upper, to_lower, right, copied):
    def rest(classes, load_mask, fixed_mask):
        moves = [
            pltpu.make_async_copy(source, target, copied.at[i])
            for i, (source, target) in enumerate((
                (classes_far, classes), (load_far, load_mask), (fixed_far, fixed_mask), (right_far, right),
                (iterate_far, main.at[0:3]), (state_far, main.at[8:11])))
        ]
        for move in moves:
            move.start()
        for move in moves:
            move.wait()
        lane = iota((BY, BZ), 1)

        def slab(x):
            mask = load_mask[x].astype(F32)
            main[3, x] = FLOOR + (1.0 - FLOOR) * classes[x].astype(F32) / (CLASSES - 1)
            main[7, x] = PENALTY * fixed_mask[x].astype(F32)
            for c in range(3):
                main[4 + c, x] = right[c, x] * mask
            last = jnp.zeros((BY, BZ), F32)
            first = jnp.zeros((BY, BZ), F32)
            for tile, offset, width in FIELDS:
                value = main[tile if tile < PACKED else tile - 1, x]
                last = jnp.where((lane >= offset) & (lane < offset + width), roll(value, offset + width, 1), last)
                low = HALF + offset
                first = jnp.where((lane >= low) & (lane < low + width), roll(value, low, 1), first)
            to_upper[x] = last
            to_lower[x] = first

        loop(0, BX, slab)

    cells = pltpu.VMEM((BX, BY, BZ), jnp.int32)
    pl.run_scoped(rest, cells, cells, cells)


def pack_rows(pos, main, from_lower, from_upper, packed, to_upper, to_lower):
    below = jnp.where(pos[2] > 0, 1.0, 0.0)
    above = jnp.where(pos[2] < pos[5] - 1, 1.0, 0.0)
    lane = iota((BY, BZ), 1)
    row = iota((BY // 2, BZ), 0)
    half = BY // 2

    def slab(x):
        joined = jnp.where(lane < HALF, from_lower[x] * below, from_upper[x] * above)
        packed[x] = joined
        values = [joined if tile == PACKED else main[tile if tile < PACKED else tile - 1, x] for tile in range(12)]
        uppers = [value[half:] for value in values]
        lowers = [value[:half] for value in values]
        for c in range(3):
            up, down = uppers[9 + c], lowers[9 + c]
            uppers[LOAD[c][0]] = jnp.where(row < 2, roll(up, 3, 0), uppers[LOAD[c][0]])
            uppers[ITERATE[c][0]] = jnp.where(row < 1, roll(up, 1, 0), uppers[ITERATE[c][0]])
            lowers[LOAD[c][0]] = jnp.where(row >= 6, roll(down, 6, 0), lowers[LOAD[c][0]])
            lowers[ITERATE[c][0]] = jnp.where(row >= 7, roll(down, 5, 0), lowers[ITERATE[c][0]])
        for tile in range(9):
            to_upper[tile, x] = uppers[tile]
            to_lower[tile, x] = lowers[tile]

    loop(0, BX, slab)


def neighbours(field, c, s, kx, ky, kz, at=None):
    at = s if at is None else at
    v = field[c, s]
    x = kx[at] * field[c, s - 1] + kx[at + 1] * field[c, s + 1]
    y = ky[at] * roll(v, 1, 0) + roll(ky[at] * v, -1, 0)
    z = kz[at] * roll(v, 1, 1) + roll(kz[at] * v, -1, 1)
    return x + y + z + (x, y, z)[c]


def coefficients(stiff, pen, s, scale, kx, ky, kz, inverse, diagonal):
    e = stiff[s]
    upper = scale * face(e, stiff[s + 1])
    kx[s + 1] = upper
    y = scale * face(e, roll(e, 1, 0))
    ky[s] = y
    yp = roll(y, -1, 0)
    z = scale * face(e, roll(e, 1, 1))
    kz[s] = z
    zp = roll(z, -1, 1)
    pairs = (kx[s] + upper, y + yp, z + zp)
    total = pairs[0] + pairs[1] + pairs[2] + pen[s]
    for c in range(3):
        value = total + pairs[c]
        diagonal[c, s] = value
        if inverse is not None:
            inverse[c, s] = jnp.where(e > 0.0, 1.0 / jnp.where(e > 0.0, value, 1.0), 0.0)


def spread(value, packed, field, ref, at):
    _, offset, width = field
    lane = iota((ROWS, BZ), 1)
    ref[at + (slice(None), slice(0, BZ))] = value
    tail = jnp.where(lane >= BZ - width, roll(packed, BZ - width - offset, 1), 0.0)
    tail = jnp.where(lane < width, roll(packed, -(HALF + offset), 1), tail)
    ref[at + (slice(None), slice(BZ, LANES))] = tail


LAYERS = ((RHO[0], 7), (PACKED, 7)) + tuple((f[0], 6) for f in LOAD + (PEN,)) + tuple((f[0], 3) for f in ITERATE + STATE)
PLACE = {}
SENT = 0
for _tile, _count in LAYERS:
    PLACE[_tile] = SENT
    SENT += _count


def pack_slabs(pos, main, packed, from_lower, from_upper, own, to_upper, to_lower,
               rho, stiff, pen, u, load, kx, ky, kz, diagonal):
    below = jnp.where(pos[1] > 0, 1.0, 0.0)
    above = jnp.where(pos[1] < pos[4] - 1, 1.0, 0.0)
    row = iota((BY // 2, BZ), 0)

    def slab(x):
        for tile in range(12):
            value = packed[x] if tile == PACKED else main[tile if tile < PACKED else tile - 1, x]
            if tile <= PACKED:
                high, low = from_upper[tile, x], from_lower[tile, x]
            else:
                load_at, iterate_at = LOAD[tile - 9][0], ITERATE[tile - 9][0]
                high = jnp.where(row < 2, roll(from_upper[load_at, x], 2, 0), roll(from_upper[iterate_at, x], 3, 0))
                low = jnp.where(row < 7, roll(from_lower[load_at, x], 5, 0), roll(from_lower[iterate_at, x], 7, 0))
            own[tile, x] = jnp.concatenate([value, high * above, low * below], 0)

    loop(0, BX, slab)

    def expand(x):
        halo = own[PACKED, x]
        spread(own[RHO[0], x], halo, RHO, rho, (x,))
        spread(own[PEN[0], x], halo, PEN, pen, (x,))
        for c in range(3):
            spread(own[ITERATE[c][0], x], halo, ITERATE[c], u, (c, x))
            spread(own[LOAD[c][0], x], halo, LOAD[c], load, (c, x))
        stiff[x] = rho[x] * rho[x] * rho[x]

    loop(0, BX, expand)
    kx[1] = face(stiff[0], stiff[1])
    loop(1, BX - 1, lambda x: coefficients(stiff, pen, x, 1.0, kx, ky, kz, None, diagonal))
    lane = iota((ROWS, BZ), 1)

    def begin(x):
        halo = own[PACKED, x]
        for c in range(3):
            f = load[c, x] - (diagonal[c, x] * u[c, x] - neighbours(u, c, x, kx, ky, kz))
            tile, offset, width = LOAD[c]
            own[tile, x] = f[:, :BZ]
            tail = f[:, BZ:]
            halo = jnp.where((lane >= offset) & (lane < offset + width), roll(tail, offset + width, 1), halo)
            low = HALF + offset
            halo = jnp.where((lane >= low) & (lane < low + width), roll(tail, low, 1), halo)
        own[PACKED, x] = halo

    loop(1, BX - 1, begin)
    for tile, count in LAYERS:
        for j in range(count):
            to_upper[PLACE[tile] + j] = own[tile, BX - count + j]
            to_lower[PLACE[tile] + j] = own[tile, j]


def descend(pos, own, lower, upper, coarse, low_lanes, high_lanes, *rest):
    far, rest = rest[:9], rest[9:]
    (v1, start, kx, ky, kz, inverse, u, weights, forward, stiff, pen, diagonal, v0, half_rows, rows, copied) = rest
    moves = []

    def send(*pairs):
        for source, target in pairs:
            move = pltpu.make_async_copy(source, far[target], copied.at[target])
            move.start()
            moves.append(move)

    below = jnp.where(pos[0] > 0, 1.0, 0.0)
    above = jnp.where(pos[0] < pos[3] - 1, 1.0, 0.0)

    def expand(raw, s, fields):
        halo = raw(PACKED)
        for field, ref, at in fields:
            spread(raw(field[0]), halo, field, ref, at)

    def densities(s):
        return [(RHO, weights, (s,))]

    def loads(s):
        return [(PEN, pen, (s,))] + [(LOAD[c], start, (c, s)) for c in range(3)]

    def motions(s):
        return [(ITERATE[c], u, (c, s)) for c in range(3)] + [(STATE[c], forward, (c, s - 4)) for c in range(3)]

    def lower_raw(s):
        return lambda t: lower[PLACE[t] + s - (HALO - dict(LAYERS)[t])] * below

    def upper_raw(s):
        return lambda t: upper[PLACE[t] + s - (HALO + BX)] * above

    after = HALO + BX
    loop(0, HALO, lambda s: expand(lower_raw(s), s, densities(s)))
    loop(1, HALO, lambda s: expand(lower_raw(s), s, loads(s)))
    loop(4, HALO, lambda s: expand(lower_raw(s), s, motions(s)))
    loop(HALO, after, lambda s: expand(lambda t: own[t, s - HALO], s, densities(s) + loads(s) + motions(s)))
    loop(after, after + 7, lambda s: expand(upper_raw(s), s, densities(s)))
    loop(after, after + 6, lambda s: expand(upper_raw(s), s, loads(s)))
    loop(after, after + 3, lambda s: expand(upper_raw(s), s, motions(s)))
    send((u.at[:, 4:18], 6), (weights.at[4:18], 7), (forward, 8))

    def cube(s):
        rho = weights[s]
        stiff[s] = rho * rho * rho

    loop(0, SLABS, cube)
    kx[1] = face(stiff[0], stiff[1])

    def prepare_slab(s):
        coefficients(stiff, pen, s, 1.0, kx, ky, kz, inverse, diagonal)
        for c in range(3):
            v0[c, s] = FIRST * start[c, s] * inverse[c, s]

    loop(1, SLABS - 1, prepare_slab)
    faces = (kx, ky, kz)
    send((kx.at[3:20], 2), (ky.at[3:19], 3), (kz.at[3:19], 4), (inverse.at[:, 3:19], 5))

    for s in (HALO - 1, HALO, HALO + BX - 1, HALO + BX):
        for c in range(3):
            start[c, s] = start[c, s] - (diagonal[c, s] * u[c, s] - neighbours(u, c, s, *faces))
            v0[c, s] = FIRST * start[c, s] * inverse[c, s]
    send((start.at[:, 3:19], 1))

    def sweep(s):
        for c in range(3):
            v1[c, s] = (1.0 - SECOND) * v0[c, s] + SECOND * inverse[c, s] * (start[c, s] + neighbours(v0, c, s, *faces))

    loop(2, SLABS - 2, sweep)
    send((v1.at[:, 2:20], 0))

    def remainder(c, s):
        r = start[c, s] - diagonal[c, s] * v1[c, s] + neighbours(v1, c, s, *faces)
        return r[:, :BZ]

    def gather_rows(at, value):
        half_rows[...] = value
        n = ROWS // 2
        rows[pl.ds(pl.multiple_of(at * n, n), n), :] = half_rows[pl.ds(0, n, stride=2), :] + half_rows[pl.ds(1, n, stride=2), :]

    def pair(i):
        for c in range(3):
            gather_rows(c * 8 + i, remainder(c, 3 + 2 * i) + remainder(c, 4 + 2 * i))

    loop(0, 8, pair)

    def pair_up(i):
        s = 1 + 2 * i
        gather_rows(24 + i, (stiff[s] + stiff[s + 1])[:, :BZ] * 0.125)
        gather_rows(34 + i, (pen[s] + pen[s + 1])[:, :BZ])

    loop(0, 10, pair_up)
    halve = matrix((BZ, BZ), lambda l, k: (l >> 1) == (k & (HALF - 1)))
    coarse[...] = times(rows[...], halve).reshape(44, 16, BZ)
    quarter = iota((8, BZ), 1) >> 5

    def pack(g):
        for h in range(2):
            low = jnp.zeros((8, BZ), F32)
            high = jnp.zeros((8, BZ), F32)
            for q in range(4):
                value = coarse[4 * g + q, 8 * h:8 * h + 8]
                turned = roll(value, 32, 1)
                one, two = (value, turned) if q % 2 == 0 else (turned, value)
                low = jnp.where(quarter == q, one, low)
                high = jnp.where(quarter == q, two, high)
            low_lanes[2 * g + h] = low
            high_lanes[2 * g + h] = high

    loop(0, 11, pack)
    for move in moves:
        move.wait()


def join_lanes(pos, coarse, from_lower, from_upper, out, center):
    below = jnp.where(pos[2] > 0, 1.0, 0.0)
    above = jnp.where(pos[2] < pos[5] - 1, 1.0, 0.0)
    lane = iota((8, BZ), 1)

    def unpack(g):
        for h in range(2):
            low, high = from_lower[2 * g + h] * below, from_upper[2 * g + h] * above
            for q in range(4):
                halo = jnp.where(lane < 96, roll(high, 64 - 32 * q, 1), roll(low, 96 - 32 * q, 1))
                value = jnp.where(lane < 64, coarse[4 * g + q, 8 * h:8 * h + 8], halo)
                out[4 * g + q, 8 * h:8 * h + 8] = value
                if h == 0:
                    center[4 * g + q] = value

    loop(0, 11, unpack)


def join_rows(pos, coarse, from_lower, from_upper, to_upper, to_lower, center, out, copied):
    below = jnp.where(pos[1] > 0, 1.0, 0.0)
    above = jnp.where(pos[1] < pos[4] - 1, 1.0, 0.0)

    def join(i):
        out[i] = jnp.concatenate([coarse[i], from_upper[i] * above, from_lower[i] * below], 0)

    loop(0, 44, join)
    move = pltpu.make_async_copy(out, center, copied.at[0])
    move.start()
    at = 0
    for base, count in ((0, 6), (8, 6), (16, 6), (24, 7), (34, 7)):
        shift = 2 if count == 6 else 3
        for j in range(count):
            to_upper[at] = out[base + j]
            to_lower[at] = out[base + shift + j]
            at += 1
    move.wait()


def smooth_down(slabs, f, v0, v1, inverse, faces):
    def begin(s):
        for c in range(3):
            v0[c, s] = FIRST * f[c, s] * inverse[c, s]

    steps(1, slabs - 1, begin)

    def sweep(s):
        for c in range(3):
            v1[c, s] = (1.0 - SECOND) * v0[c, s] + SECOND * inverse[c, s] * (f[c, s] + neighbours(v0, c, s, *faces))

    steps(2, slabs - 2, sweep)


def level_one(pos, own, chunk, kx, ky, kz, inverse, diagonal, f, v0, v1, half_rows, rows, wide):
    stiff, pen = own.at[24:34], own.at[34:44]
    slabs = 10
    for c in range(3):
        for i in range(8):
            f[c, 1 + i] = own[8 * c + i]
    kx[1] = 2.0 * face(stiff[0], stiff[1])
    steps(1, slabs - 1, lambda s: coefficients(stiff, pen, s, 2.0, kx, ky, kz, inverse, diagonal))
    faces = (kx, ky, kz)
    smooth_down(slabs, f, v0, v1, inverse, faces)

    def gather_rows(at, value):
        half_rows[0:8] = value
        rows[pl.ds(at * 4, 4), :] = half_rows[pl.ds(0, 4, stride=2), :] + half_rows[pl.ds(1, 4, stride=2), :]

    for i in range(2):
        s = 3 + 2 * i
        for c in range(3):
            total = 0.0
            for at in (s, s + 1):
                total = total + (f[c, at] - diagonal[c, at] * v1[c, at] + neighbours(v1, c, at, *faces))[:8]
            gather_rows(2 * c + i, total)
        gather_rows(6 + i, (stiff[s] + stiff[s + 1])[:8] * 0.125)
        gather_rows(8 + i, (pen[s] + pen[s + 1])[:8])

    def rule(j, k):
        z = jnp.where(j < 96, j, j - BZ)
        return (z >> 1) == (k & 63) - 16

    wide[...] = times(rows[...], matrix((BZ, BZ), rule))
    lane = iota((4, BZ), 1)
    parts = [jnp.where(lane < 64, wide[8 * field:8 * field + 4], wide[8 * field + 4:8 * field + 8]) for field in range(5)]
    value = jnp.concatenate(parts + [jnp.zeros((4, BZ), F32)], 0)
    for i in range(chunk.shape[0]):
        chunk[i] = value


def pack_column(pos, column, out):
    for i in range(out.shape[0]):
        for j in range(column.shape[0]):
            out[i, 20 * j:20 * j + 20] = column[j, 0:20]


def level_one_again(pos, own, lower, upper, v1, f, kx, ky, kz, inverse, stiff, pen, diagonal, v0):
    below = jnp.where(pos[0] > 0, 1.0, 0.0)
    above = jnp.where(pos[0] < pos[3] - 1, 1.0, 0.0)
    slabs = 18
    for field, at in ((stiff, 0), (pen, 1)):
        for j in range(7):
            field[j] = lower[18 + 7 * at + j] * below
            field[11 + j] = upper[18 + 7 * at + j] * above
        for j in range(4):
            field[7 + j] = own[24 + 10 * at + 3 + j]
    for c in range(3):
        for j in range(6):
            f[c, 1 + j] = lower[6 * c + j] * below
            f[c, 11 + j] = upper[6 * c + j] * above
        for j in range(4):
            f[c, 7 + j] = own[8 * c + 2 + j]
    kx[1] = 2.0 * face(stiff[0], stiff[1])
    steps(1, slabs - 1, lambda s: coefficients(stiff, pen, s, 2.0, kx, ky, kz, inverse, diagonal))
    smooth_down(slabs, f, v0, v1, inverse, (kx, ky, kz))


def coarse_levels(pos, gathered, out, nx, ny, work):
    (e2, p2, f2, kxm, kxp, kym, kzm, iv, dg, va, vb, tall, rows3, e3, p3, f3, jx, jym, jz, iv3, wa, wb, rows2) = work
    ys = 4 * ny
    pairs = nx
    lane = iota((ys, BZ), 1)
    row = iota((ys, BZ), 0)
    even = lane < 64
    zero = jnp.zeros((ys, BZ), F32)
    for field in (e2, p2):
        field[0] = zero
        field[pairs + 1] = zero
    for c in range(3):
        for field in (va, vb):
            field[c, 0] = zero
            field[c, pairs + 1] = zero

    def collect(g):
        for field in range(5):
            for yy in range(ny):
                value = gathered[g, 20 * yy + 4 * field:20 * yy + 4 * field + 4, :]
                if field < 3:
                    f2[field, g + 1, pl.ds(4 * yy, 4), :] = value
                else:
                    (e2, p2)[field - 3][g + 1, pl.ds(4 * yy, 4), :] = value

    steps(0, pairs, collect)

    def x_neighbours(below, mid, above):
        swapped = roll(mid, 64, 1)
        return jnp.where(even, roll(below, 64, 1), swapped), jnp.where(even, swapped, roll(above, 64, 1))

    def coefs(s):
        e = e2[s]
        xm, xp = x_neighbours(e2[s - 1], e, e2[s + 1])
        ym = jnp.where(row == 0, 0.0, roll(e, 1, 0))
        yp = jnp.where(row == ys - 1, 0.0, roll(e, -1, 0))
        a, b = 4.0 * face(e, xm), 4.0 * face(e, xp)
        c0, d = 4.0 * face(e, ym), 4.0 * face(e, yp)
        z = 4.0 * face(e, roll(e, 1, 1))
        zp = roll(z, -1, 1)
        kxm[s] = a
        kxp[s] = b
        kym[s] = jnp.where(row == 0, 0.0, c0)
        kzm[s] = z
        sums = (a + b, c0 + d, z + zp)
        total = sums[0] + sums[1] + sums[2] + p2[s]
        for c in range(3):
            value = total + sums[c]
            dg[c, s] = value
            iv[c, s] = jnp.where(e > 0.0, 1.0 / jnp.where(e > 0.0, value, 1.0), 0.0)
            va[c, s] = FIRST * f2[c, s] * iv[c, s]

    steps(1, pairs + 1, coefs)

    def around(v, c, s):
        mid = v[c, s]
        below, above = x_neighbours(v[c, s - 1], mid, v[c, s + 1])
        x = kxm[s] * below + kxp[s] * above
        y = kym[s] * roll(mid, 1, 0) + roll(kym[s] * mid, -1, 0)
        z = kzm[s] * roll(mid, 1, 1) + roll(kzm[s] * mid, -1, 1)
        return x + y + z + (x, y, z)[c]

    def sweep(source, target, weight):
        def step(s):
            for c in range(3):
                target[c, s] = (1.0 - weight) * source[c, s] + weight * iv[c, s] * (f2[c, s] + around(source, c, s))

        steps(1, pairs + 1, step)

    sweep(va, vb, SECOND)
    n3 = ys // 2

    def gather_rows(at, value):
        tall[...] = value
        rows3[pl.ds(pl.multiple_of(at * n3, 8), n3), :] = tall[pl.ds(0, n3, stride=2), :] + tall[pl.ds(1, n3, stride=2), :]

    def reduce(s):
        for c in range(3):
            gather_rows(c * pairs + s - 1, f2[c, s] - dg[c, s] * vb[c, s] + around(vb, c, s))
        gather_rows(3 * pairs + s - 1, e2[s] * 0.125)
        gather_rows(4 * pairs + s - 1, p2[s])

    steps(1, pairs + 1, reduce)
    down = matrix((BZ, BZ), lambda l, k: ((l & 63) >> 1) == (k & 31))
    rows3[...] = times(rows3[...], down)
    row3 = iota((n3, BZ), 0)
    zero3 = jnp.zeros((n3, BZ), F32)

    def third(at):
        return rows3[pl.ds(pl.multiple_of(at * n3, 8), n3), :]

    e3[0] = zero3
    e3[pairs + 1] = zero3
    for c in range(3):
        for field in (wa, wb):
            field[c, 0] = zero3
            field[c, pairs + 1] = zero3

    def place(s):
        e3[s] = third(3 * pairs + s - 1)

    steps(1, pairs + 1, place)

    def coefs3(s):
        e = e3[s]
        a, b = 8.0 * face(e, e3[s - 1]), 8.0 * face(e, e3[s + 1])
        c0 = 8.0 * face(e, jnp.where(row3 == 0, 0.0, roll(e, 1, 0)))
        d = 8.0 * face(e, jnp.where(row3 == n3 - 1, 0.0, roll(e, -1, 0)))
        z = 8.0 * face(e, roll(e, 1, 1))
        zp = roll(z, -1, 1)
        jx[s] = a
        jx[s + 1] = b
        jym[s] = jnp.where(row3 == 0, 0.0, c0)
        jz[s] = z
        sums = (a + b, c0 + d, z + zp)
        total = sums[0] + sums[1] + sums[2] + third(4 * pairs + s - 1)
        for c in range(3):
            value = total + sums[c]
            iv3[c, s] = jnp.where(e > 0.0, 1.0 / jnp.where(e > 0.0, value, 1.0), 0.0)
            wa[c, s] = COARSE * third(c * pairs + s - 1) * iv3[c, s]

    steps(1, pairs + 1, coefs3)
    source, target = wa, wb
    for sweep_at in range(3):
        def step(s, source=source, target=target):
            for c in range(3):
                near = neighbours(source, c, s, jx, jym, jz)
                target[c, s] = (1.0 - COARSE) * source[c, s] + COARSE * iv3[c, s] * (third(c * pairs + s - 1) + near)

        steps(1, pairs + 1, step)
        source, target = target, source
    up = matrix((BZ, BZ), lambda k, l: k == ((l & 63) >> 1))
    for c in range(3):
        rows2[...] = times(source[c, 1:pairs + 1].reshape(pairs * n3, BZ), up)

        def add(s, c=c):
            value = rows2[pl.ds(pl.multiple_of((s - 1) * n3, 8), n3), :]
            tall[pl.ds(0, n3, stride=2), :] = value
            tall[pl.ds(1, n3, stride=2), :] = value
            vb[c, s] = vb[c, s] + jnp.where(iv[c, s] > 0.0, tall[...], 0.0)

        steps(1, pairs + 1, add)
    sweep(vb, va, SECOND)

    for c in range(3):
        for at in (0, 1, pairs + 2, pairs + 3):
            out[c, at] = zero

    def last(s):
        for c in range(3):
            out[c, s + 1] = (1.0 - FIRST) * va[c, s] + FIRST * iv[c, s] * (f2[c, s] + around(va, c, s))

    steps(1, pairs + 1, last)


def ascend(pos, lower, upper, gathered, *rest, nx, ny):
    far, (sums, parts, precond_far), rest = rest[:7], rest[8:11], rest[11:]
    near, rest = rest[:7], rest[7:]
    e2out, window, rows24, va1, vb1, rows32, spread, vb, precond, held = rest[:10]
    v1, f1, kx1, ky1, kz1, inverse1, stiff1, pen1, diagonal1, v01 = rest[10:20]
    work, copied = rest[20:-1], rest[-1]
    center = near[0]
    va, start, kx, ky, kz, inverse = near[1:]
    arrivals = [pltpu.make_async_copy(source, target, copied.at[i]) for i, (source, target) in enumerate(zip(far, near))]
    for move in arrivals:
        move.start()
    departures = []

    def send(source, target):
        move = pltpu.make_async_copy(source, target, copied.at[7 + len(departures)])
        move.start()
        departures.append(move)

    coarse_levels(pos, gathered, e2out, nx, ny, work)
    arrivals[0].wait()
    level_one_again(
        pos, center, lower, upper, v1, f1, kx1, ky1, kz1, inverse1, stiff1, pen1, diagonal1, v01)
    gx, gy = pos[0], pos[1]
    ys = 4 * ny
    turn = lax.rem(ys - 4 * gy, ys)

    def rule(k, j):
        z = jnp.where((j & 127) < 96, j & 127, (j & 127) - BZ)
        return k == 64 * (j >> 7) + (z >> 1) + 16

    grow = matrix((BZ, LANES), rule)
    for c in range(3):
        for j in range(5):
            window[pl.ds((5 * c + j) * ys, ys), :] = times(pltpu.roll(e2out[c, gx + j], turn, 0), grow)
    for c in range(3):
        for s in range(2, 16):
            x2 = (s - 7) // 2
            j, part = (x2 + 4) // 2, (x2 + 4) % 2
            base = (5 * c + j) * ys
            cols = slice(128 * part, 128 * part + 128)
            if s % 2 == 1 or s == 2:
                low = window[base:base + 8, cols]
                high = window[base + ys - 4:base + ys, cols]
                for at in (0, 1):
                    rows24[pl.ds(at, 8, stride=2), :] = low
                    rows24[pl.ds(16 + at, 4, stride=2), :] = high
            va1[c, s] = v1[c, s] + jnp.where(inverse1[c, s] > 0.0, rows24[0:24], 0.0)
    faces1 = (kx1, ky1, kz1)

    def sweep1(source, target, weight, lower, upper):
        def step(s):
            for c in range(3):
                target[c, s] = (1.0 - weight) * source[c, s] + weight * inverse1[c, s] * (
                    f1[c, s] + neighbours(source, c, s, *faces1))

        steps(lower, upper, step)

    sweep1(va1, vb1, SECOND, 3, 15)
    sweep1(vb1, va1, FIRST, 4, 14)
    grow0 = matrix((BZ, LANES), lambda j, l: j == (l >> 1))
    for move in arrivals[1:]:
        move.wait()
    for c in range(3):
        spread[...] = times(va1[c, 4:14].reshape(240, BZ), grow0)
        for i in range(10):
            for half in (0, 1):
                cols = slice(BZ * half, BZ * half + BZ)
                value = spread[24 * i:24 * i + 24, cols]
                for at in (0, 1):
                    rows32[pl.ds(at, 12, stride=2), :] = value[:12]
                    rows32[pl.ds(24 + at, 4, stride=2), :] = value[20:]
                for s in (2 * i - 1, 2 * i):
                    if 0 <= s < 18:
                        va[c, s, :, cols] = va[c, s, :, cols] + rows32[0:ROWS]
    faces = (kx, ky, kz)

    def sweep_one(t):
        for c in range(3):
            vb[c, t] = (1.0 - SECOND) * va[c, t + 1] + SECOND * inverse[c, t] * (
                start[c, t] + neighbours(va, c, t + 1, *faces, at=t))

    loop(0, 16, sweep_one)

    def sweep_two(t):
        for c in range(3):
            precond[c, t - 1] = (1.0 - FIRST) * vb[c, t] + FIRST * inverse[c, t] * (start[c, t] + neighbours(vb, c, t, *faces))

    loop(1, 15, sweep_two)

    def keep(x):
        for c in range(3):
            held[c, x] = precond[c, x + 3][:BY, :BZ]
            held[3 + c, x] = start[c, x + 4][:BY, :BZ]

    loop(0, BX, keep)
    send(held.at[0:6], parts.at[0:6])
    send(precond, precond_far)

    def inner(x, carry):
        one, two = carry
        for c in range(3):
            mid = held[c, x]
            value = mid / inverse[c, x + 4][:BY, :BZ] - neighbours(precond, c, x + 3, *faces, at=x + 4)[:BY, :BZ]
            held[6 + c, x] = value
            one = one + held[3 + c, x] * mid
            two = two + mid * value
        return one, two

    zero = jnp.zeros((BY, BZ), F32)
    one, two = lax.fori_loop(0, BX, inner, (zero, zero), unroll=4)
    send(held.at[6:9], parts.at[6:9])
    lane = iota((8, BZ), 1)
    sums[...] = jnp.where(lane == 0, jnp.sum(one), jnp.where(lane == 1, jnp.sum(two), 0.0))
    for move in departures:
        move.wait()


def distance_weight(square):
    return max(RADIUS - math.sqrt(square), 0.0)


def sensitivity(state, field, weights, term):
    def energy(i):
        s = i + 1
        total = jnp.zeros((ROWS, LANES), F32)
        sums = [0.0, 0.0]
        for c in range(3):
            a, b = state[c, s], field[c, s]
            x = (a - state[c, s - 1]) * (b - field[c, s - 1]) + (a - state[c, s + 1]) * (b - field[c, s + 1])
            total = total + (x + x if c == 0 else x)
            for axis in (0, 1):
                part = (a - roll(a, 1, axis)) * (b - roll(b, 1, axis))
                sums[axis] = sums[axis] + (part + part if c == axis + 1 else part)
        for axis in (0, 1):
            total = total + sums[axis] + roll(sums[axis], -1, axis)
        rho = weights[s]
        term[i] = rho * (-3.0 * rho * rho * (0.5 * total))

    loop(0, BX + 4, energy)


def weigh(field, x):
    classes = {}
    for a in range(-2, 3):
        t = field[x + 2 + a]
        for b, value in ((0, t), (1, roll(t, 1, 0) + roll(t, -1, 0)), (2, roll(t, 2, 0) + roll(t, -2, 0))):
            q = a * a + b * b
            classes[q] = value if q not in classes else classes[q] + value
    parts = []
    for z in (0, 1, 2):
        part = None
        for q, value in classes.items():
            w = distance_weight(q + z * z)
            if w > 0.0:
                part = w * value if part is None else part + w * value
        parts.append(part)
    result = parts[0] + roll(parts[1], 1, 1) + roll(parts[1], -1, 1) + roll(parts[2], 2, 1) + roll(parts[2], -2, 1)
    return result[:BY, :BZ]


def arrive(far, near, copied):
    moves = [pltpu.make_async_copy(source, target, copied.at[i]) for i, (source, target) in enumerate(zip(far, near))]
    for move in moves:
        move.start()
    for move in moves:
        move.wait()


def filter_iterate(pos, *rest):
    far, out, near, (term, inside, copied) = rest[:3], rest[3], rest[4:7], rest[7:]
    arrive(far, near, copied)
    iterate, state, weights = near
    sensitivity(state, iterate, weights, term)

    def mark(i):
        inside[i] = jnp.where(weights[i + 1] > 0.0, 1.0, 0.0)

    loop(0, BX + 4, mark)

    def smooth(x):
        factor = 1.0 / (weights[x + 3][:BY, :BZ] * weigh(inside, x))
        out[0, x] = factor * weigh(term, x)
        out[1, x] = factor

    loop(0, BX, smooth)


def filter_precond(pos, *rest):
    far, out, near, (term, copied) = rest[:6], rest[6], rest[7:13], rest[13:]
    moves = [pltpu.make_async_copy(source, target, copied.at[i]) for i, (source, target) in enumerate(zip(far, near))]
    for move in moves[3:] + moves[:3]:
        move.start()
    for move in moves[3:]:
        move.wait()
    precond, state, weights = near[3:]
    sensitivity(state, precond, weights, term)

    def smooth(x):
        out[x] = weigh(term, x)

    loop(0, BX, smooth)
    for move in moves[:3]:
        move.wait()


def finish(pos, totals, *rest):
    second, iterate, parts, smooth, solution, residual, filtered = rest
    total = jnp.sum(totals[...], axis=0, keepdims=True)
    lane = iota((1, BZ), 1)
    one = jnp.sum(jnp.where(lane == 0, total, 0.0), axis=1, keepdims=True)
    two = jnp.sum(jnp.where(lane == 1, total, 0.0), axis=1, keepdims=True)
    alpha = one / two

    def update(x):
        for c in range(3):
            solution[c, x] = iterate[c, x] + alpha * parts[c, x]
            residual[c, x] = parts[3 + c, x] - alpha * parts[6 + c, x]
        filtered[x] = smooth[0, x] + alpha * (second[x] * smooth[1, x])

    loop(0, BX, update)


def body(right_side, iterate, state, classes, load_mask, fixed_mask):
    nx, ny, nz = (lax.axis_size(axis) for axis in ("gx", "gy", "gz"))
    pos = jnp.stack([lax.axis_index("gx"), lax.axis_index("gy"), lax.axis_index("gz")]).astype(jnp.int32)
    pos = jnp.concatenate([pos, jnp.array([nx, ny, nz], jnp.int32)])
    cells = (BX, BY, BZ)
    field = (3,) + cells
    wide = (ROWS, LANES)

    def slabs(n):
        return (n,) + wide

    def fields(n):
        return (3, n) + wide

    main, last, first = launch(
        4, prepare, [(11,) + cells, cells, cells], [field], [pos],
        far=[right_side, iterate, state, classes, load_mask, fixed_mask], copies=6)
    from_lower, from_upper = shift_along(last, "gz", 1), shift_along(first, "gz", -1)
    edge = (9, BX, BY // 2, BZ)
    packed, to_upper, to_lower = launch(4, pack_rows, [cells, edge, edge], [], [pos, main, from_lower, from_upper])
    from_lower, from_upper = shift_along(to_upper, "gy", 1), shift_along(to_lower, "gy", -1)
    sides = (SENT, ROWS, BZ)
    own, to_upper, to_lower = launch(
        14, pack_slabs, [(12, BX, ROWS, BZ), sides, sides],
        [slabs(BX)] * 3 + [fields(BX)] * 2 + [slabs(BX)] * 3 + [fields(BX)], [pos, main, packed, from_lower, from_upper])
    from_lower, from_upper = shift_along(to_upper, "gx", 1), shift_along(to_lower, "gx", -1)

    one, three = slabs(SLABS), fields(SLABS)
    quarters = (22, 8, BZ)
    coarse, low, high, v1, start, kx, ky, kz, inverse, u, weights, forward = launch(
        24, descend, [(44, 16, BZ), quarters, quarters],
        [three, three, one, one, one, three, three, one, fields(14), one, one, three, three, (ROWS, BZ), (44 * 16, BZ)],
        [pos, own, from_lower, from_upper],
        far_outs=[fields(18), fields(16), slabs(17)] + [slabs(16)] * 2 + [fields(16), fields(14), slabs(14), fields(14)],
        copies=9)
    smooth = launch(
        10, filter_iterate, [(2,) + cells], [fields(14), fields(14), slabs(14), slabs(12), slabs(12)], [pos],
        far=[u, forward, weights], copies=3,
        cost=pl.CostEstimate(flops=12_000_000, bytes_accessed=4_000_000, transcendentals=0))[0]

    from_lower, from_upper = shift_along(high, "gz", 1), shift_along(low, "gz", -1)
    coarse, center = launch(4, join_lanes, [(44, 16, BZ), (44, 8, BZ)], [], [pos, coarse, from_lower, from_upper])
    from_lower, from_upper = shift_along(center, "gy", 1), shift_along(center, "gy", -1)
    wide1 = (16, BZ)
    one1, three1 = (10,) + wide1, (3, 10) + wide1
    chunk = launch(
        4, level_one, [(ny, 24, BZ)], [one1] * 3 + [three1] * 5 + [(24, BZ), (40, BZ), (40, BZ)], [pos, coarse])[0]
    side = (32, 24, BZ)
    column = lax.all_to_all(chunk, "gy", 0, 0, tiled=True)
    to_upper, to_lower, center = launch(
        4, join_rows, [side, side], [(44, 24, BZ)], [pos, center, from_lower, from_upper],
        far_outs=[(44, 24, BZ)], copies=1)
    column = launch(8, pack_column, [(nx, 20 * ny, BZ)], [], [pos, column])[0]
    gathered = lax.all_to_all(column, "gx", 0, 0, tiled=True)
    from_lower, from_upper = shift_along(to_upper, "gx", 1), shift_along(to_lower, "gx", -1)

    wide1 = (24, BZ)
    one1, three1 = (18,) + wide1, (3, 18) + wide1
    wide2, wide3 = (4 * ny, BZ), (2 * ny, BZ)
    one2, three2 = (nx + 2,) + wide2, (3, nx + 2) + wide2
    one3, three3 = (nx + 2,) + wide3, (3, nx + 2) + wide3
    work = [one2, one2, three2] + [one2] * 4 + [three2] * 4 + [wide2, (5 * nx * 2 * ny, BZ)]
    work += [one3, one3, three3] + [one3] * 3 + [three3] * 3 + [(nx * 2 * ny, BZ)]
    parts = (9,) + cells
    far = [center, v1, start, kx, ky, kz, inverse]
    scratch = [x.shape for x in far] + [
        (3, nx + 4) + wide2, (15 * 4 * ny, LANES), (40, BZ), three1, three1, (ROWS + 16, BZ), (240, LANES), fields(16), fields(14), parts
    ] + [three1] * 2 + [one1] * 3 + [three1, one1, one1, three1, three1] + work
    sums, parts, precond = launch(
        30, functools.partial(ascend, nx=nx, ny=ny), [(8, BZ)], scratch, [pos, from_lower, from_upper, gathered],
        far_outs=[parts, fields(14)], far=far + [smooth], copies=10)
    ready = launch(
        12, filter_precond, [cells, field, parts.shape, smooth.shape], [fields(14), fields(14), slabs(14), slabs(12)], [pos],
        far=[iterate, parts, smooth, precond, forward, weights], copies=6, pin=True,
        cost=pl.CostEstimate(flops=8_000_000, bytes_accessed=4_000_000, transcendentals=0))
    total = lax.all_to_all(jnp.broadcast_to(sums[:1], (nx * ny, BZ)), ("gx", "gy"), 0, 0, tiled=True)
    total = jnp.sum(total, axis=0, keepdims=True)
    total = lax.all_to_all(jnp.broadcast_to(total, (nz, BZ)), "gz", 0, 0, tiled=True)
    return tuple(launch(4, finish, [field, field, cells], [], [pos, total, *ready]))


def solution(mesh):
    field, cells = P(None, "gx", "gy", "gz"), P("gx", "gy", "gz")
    return jax.shard_map(
        body,
        mesh=mesh,
        in_specs=(field, field, field, cells, cells, cells),
        out_specs=(field, field, cells),
        check_vma=False,
    )
```
